32 devices in a mesh: dp: 2 (over core), expert: 16 (over z, y, x).
Axes of the slice: x: 2, y: 2, z: 4, core: 2. Of those that a mesh axis runs over, the one named last changes fastest.
Arguments:
- tokens: bfloat16 [4096, 2048], P(('dp', 'expert')), may hold values from -6 to 6
- expert_ids: int32 [4096, 2], P(('dp', 'expert')), may hold values from 0 to 15, all different within a row; in each aligned block of 128 rows (0 to 127, 128 to 255, ...) at most 32 rows name the same one
- gate_prob: float32 [4096, 2], P(('dp', 'expert')), may hold values from 0.1 to 1
- w_gate: bfloat16 [16, 2048, 704], P('expert'), may hold values from -0.125 to 0.125
- w_up: bfloat16 [16, 2048, 704], P('expert'), may hold values from -0.125 to 0.125
- w_down: bfloat16 [16, 704, 2048], P('expert'), may hold values from -0.21875 to 0.21875
- d_mixed: bfloat16 [4096, 2048], P(('dp', 'expert')), may hold values from -6 to 6
Outputs:
- mixed: bfloat16 [4096, 2048], P(('dp', 'expert'))
- d_tokens: bfloat16 [4096, 2048], P(('dp', 'expert'))
- d_gate: float32 [4096, 2], P(('dp', 'expert'))
- grad_gate: float32 [16, 2048, 704], P('expert', 'dp')
- grad_up: float32 [16, 2048, 704], P('expert', 'dp')
- grad_down: float32 [16, 704, 2048], P('expert', None, 'dp')
The draws below stay inside these ranges and needn't reach their ends.
Inputs may be any that keep to these rules, and one draw needn't show every extreme that they name: `expert_ids`: each token names 2 different experts; among the 128 tokens of one device (aligned blocks) no expert is named more than 32 times, a bound that some block reaches.
All inputs are finite; a program needn't handle non-finite values.
Results may differ from the reference program's by a relative error of at most 0.0065.
Values may be sent and summed in bfloat16 or wider, within the bound.
No kernel may reach another device: no remote copies, remote signals or barrier semaphores. Data moves between devices by JAX's collectives and lax.ppermute only.
A program may use at most 128 MiB of HBM per device.

```python
import math
import jax
import jax.numpy as jnp
import numpy as np
from jax import lax

D = 2048
FF = 704
TOP = 2
TOK_DEV = 128
EXPERTS = 16
CAP = 32
TOKENS = 4096
N_DP = 2
DEVICES = 32


def level_of(key, extent, pieces, smallest, largest):
    factor_of = 1.0
    for dim, blocks in pieces:
        heights = jax.random.uniform(jax.random.fold_in(jax.random.fold_in(key, 6), dim), (blocks,), jnp.float32, smallest / len(pieces), largest / len(pieces))
        factor_of = factor_of * jnp.repeat(jnp.exp(heights), extent[dim] // blocks).reshape((-1,) + (1,) * (len(extent) - 1 - dim))
    return factor_of


def assign_block(rng, own, number, rows, amount, top, reach, skew):
    sequence = jax.random.permutation(rng, amount)
    packed, usual = portions_of(amount, rows * top, reach, skew, True), portions_of(amount, rows * top, reach, skew, False)
    places = jnp.arange(amount)

    def named(sizes, offset_by):
        used = int((sizes > 0).sum())
        fixed = max(1, used // 4)
        moved = fixed + (places - fixed + offset_by * (used - fixed)) % max(1, amount - fixed)
        return jnp.zeros((amount,), jnp.int32).at[sequence[jnp.where(places < fixed, places, moved)]].set(jnp.asarray(sizes, jnp.int32))

    sizes = jnp.where(number % 4 == 0, named(packed, number // 4), named(usual, number - number // 4 - 1))
    mixed = jax.random.permutation(jax.random.fold_in(own, 3), amount)
    source_of, taker = mixed[0:amount // 2 * 2:2], mixed[1:amount // 2 * 2:2]
    slack = jnp.minimum(sizes[source_of] - 1, reach - sizes[taker]) // 2
    slack = jnp.where((source_of == sequence[0]) | (taker == sequence[0]) | (sizes[taker] == 0), 0, jnp.maximum(slack, 0))
    moved = jax.random.randint(jax.random.fold_in(own, 4), (amount // 2,), 0, 1 << 20) % (slack + 1)
    sizes = sizes.at[source_of].add(-moved).at[taker].add(moved)
    items = jnp.searchsorted(jnp.cumsum(sizes), jnp.arange(rows * top), side="right").astype(jnp.int32)
    listing = items.reshape(top, rows).T
    listing = listing[jax.random.permutation(jax.random.fold_in(own, 1), rows)]
    offset_by = jax.random.randint(jax.random.fold_in(own, 2), (rows, 1), 0, top)
    return jnp.take_along_axis(listing, (jnp.arange(top)[None, :] + offset_by) % top, axis=1)


def portions_of(count, total, reach, lean, full):
    weights = [(1 << 20) // math.isqrt(grade ** lean) + 1 for grade in range(1, count + 1)]
    largest = reach if full else min(reach, max(-(-total // count), total * weights[0] // sum(weights)))
    least = 1 if total - largest >= count - 1 else 0
    counts, rest = [largest] + [least] * (count - 1), total - largest - least * (count - 1)
    while rest > 0:
        free = [i for i in range(1, count) if counts[i] < largest] or [i for i in range(1, count) if counts[i] < reach]
        pool, budget = sum([weights[i] for i in free]), rest
        for i in free:
            extra = min(reach - counts[i], max(1, budget * weights[i] // pool), rest)
            counts[i] = counts[i] + extra
            rest = rest - extra
    return np.array(counts)


def centred(rng, extent, deviation, reach, split=(), held_as=jnp.bfloat16):
    array = jax.random.normal(rng, extent, jnp.float32) * deviation
    if len(split) > 0:
        array = level_of(rng, extent, split, -0.22, 0.18) * array
    return jnp.clip(array, min=-reach, max=reach).astype(held_as)


def setup_inputs(seed: int = 0) -> dict:
    splits = jax.random.split(jax.random.key(seed), 8)
    tokens = centred(splits[0], (TOKENS, D), 1.0, 6.0, ((0, 32),))
    expert_ids_keys = jax.random.split(jax.random.fold_in(splits[1], 1), TOKENS // TOK_DEV)
    expert_ids_turns = jax.random.permutation(jax.random.fold_in(splits[1], 3), TOKENS // TOK_DEV)
    expert_ids = jax.vmap(lambda own, number: assign_block(jax.random.fold_in(splits[1], 2), own, number, TOK_DEV, EXPERTS, TOP, CAP, 2))(expert_ids_keys, expert_ids_turns).reshape((TOKENS, TOP))
    gate_prob = jnp.clip(jnp.exp(math.log(1.0) - 2.3025851 * jax.random.uniform(splits[2], (TOKENS, TOP), jnp.float32) ** level_of(splits[2], (TOKENS, TOP), ((0, 32),), -0.2, 0.2)), 0.1, 1.0)
    w_gate = centred(splits[3], (EXPERTS, D, FF), D ** -0.5, 0.125, ((0, 16),))
    w_up = centred(splits[4], (EXPERTS, D, FF), D ** -0.5, 0.125, ((0, 16),))
    w_down = centred(splits[5], (EXPERTS, FF, D), FF ** -0.5, 0.21875, ((0, 16),))
    d_mixed = centred(splits[6], (TOKENS, D), 1.0, 6.0, ((0, 32),))
    return dict(tokens=tokens, expert_ids=expert_ids, gate_prob=gate_prob, w_gate=w_gate, w_up=w_up, w_down=w_down, d_mixed=d_mixed)


def expert_pass(x_rows, dy_rows, gate_matrix, up_matrix, down_matrix):
    x_wide = x_rows.astype(jnp.float32)
    gate_pre = jnp.dot(x_wide, gate_matrix.astype(jnp.float32))
    up_pre = jnp.dot(x_wide, up_matrix.astype(jnp.float32))
    sig_gate = jax.nn.sigmoid(gate_pre)
    silu_gate = gate_pre * sig_gate
    hidden = (silu_gate * up_pre).astype(jnp.bfloat16)
    expert_out = jnp.dot(hidden.astype(jnp.float32), down_matrix.astype(jnp.float32)).astype(jnp.bfloat16)
    back_hidden = jnp.dot(dy_rows.astype(jnp.float32), down_matrix.astype(jnp.float32).T)
    d_silu = sig_gate * (1.0 + gate_pre * (1.0 - sig_gate))
    grad_pre_gate = (back_hidden * up_pre * d_silu).astype(jnp.bfloat16)
    grad_pre_up = (back_hidden * silu_gate).astype(jnp.bfloat16)
    expert_dx = (jnp.dot(grad_pre_gate.astype(jnp.float32), gate_matrix.astype(jnp.float32).T)
                 + jnp.dot(grad_pre_up.astype(jnp.float32), up_matrix.astype(jnp.float32).T)).astype(jnp.bfloat16)
    return expert_out, expert_dx, hidden, grad_pre_gate, grad_pre_up


def grouped_sum(left, right):
    left_grouped = left.reshape(N_DP, -1, left.shape[1]).astype(jnp.float32)
    right_grouped = right.reshape(N_DP, -1, right.shape[1]).astype(jnp.float32)
    partial_terms = jnp.einsum("irs,irf->isf", left_grouped, right_grouped).astype(jnp.bfloat16)
    partial_terms = lax.optimization_barrier(partial_terms)
    return jnp.sum(partial_terms.astype(jnp.float32), 0)


def reference(tokens, expert_ids, gate_prob, w_gate, w_up, w_down, d_mixed):
    pair_count = TOK_DEV * TOP
    ids_dev = expert_ids.reshape(DEVICES, pair_count)
    onehot = (ids_dev[:, :, None] == jnp.arange(EXPERTS, dtype=jnp.int32)[None, None, :]).astype(jnp.int32)
    pair_rank = jnp.sum((jnp.cumsum(onehot, 1) - 1) * onehot, 2)
    device_index = jnp.arange(DEVICES, dtype=jnp.int32)[:, None]
    slot_global = ids_dev * (DEVICES * CAP) + device_index * CAP + pair_rank
    table = jnp.full((EXPERTS * DEVICES * CAP,), -1, jnp.int32)
    table = table.at[slot_global.reshape(-1)].set(jnp.arange(TOKENS * TOP, dtype=jnp.int32))
    table = table.reshape(EXPERTS, DEVICES * CAP)
    gate_flat = gate_prob.reshape(-1)

    def step(carry, inputs):
        mixed_acc, dx_acc, dgate_acc = carry
        pair_ids, gate_matrix, up_matrix, down_matrix = inputs
        valid = pair_ids >= 0
        safe_pair = jnp.where(valid, pair_ids, 0)
        token_index = safe_pair // TOP
        gate_rows = jnp.where(valid, gate_flat[safe_pair], jnp.zeros((), jnp.float32))
        x_rows = jnp.where(valid[:, None], tokens[token_index], jnp.zeros((), jnp.bfloat16))
        dy_token = d_mixed[token_index]
        dy_rows = (gate_rows[:, None] * dy_token.astype(jnp.float32)).astype(jnp.bfloat16)
        expert_out, expert_dx, hidden, grad_pre_gate, grad_pre_up = expert_pass(x_rows, dy_rows, gate_matrix, up_matrix, down_matrix)
        target = jnp.where(valid, token_index, TOKENS)
        mixed_acc = mixed_acc.at[target].add(gate_rows[:, None] * expert_out.astype(jnp.float32), mode="drop")
        dx_acc = dx_acc.at[target].add(expert_dx.astype(jnp.float32), mode="drop")
        gate_grads = jnp.sum(dy_token.astype(jnp.float32) * expert_out.astype(jnp.float32), 1)
        dgate_acc = dgate_acc.at[jnp.where(valid, safe_pair, TOKENS * TOP)].set(gate_grads, mode="drop")
        grad_g = grouped_sum(x_rows, grad_pre_gate)
        grad_u = grouped_sum(x_rows, grad_pre_up)
        grad_d = grouped_sum(dy_rows, hidden).T
        return (mixed_acc, dx_acc, dgate_acc), (grad_g, grad_u, grad_d)

    init = (jnp.zeros((TOKENS, D), jnp.float32), jnp.zeros((TOKENS, D), jnp.float32), jnp.zeros((TOKENS * TOP,), jnp.float32))
    (mixed_acc, dx_acc, dgate_acc), (grad_gate, grad_up, grad_down) = lax.scan(step, init, (table, w_gate, w_up, w_down))
    return (mixed_acc.astype(jnp.bfloat16), dx_acc.astype(jnp.bfloat16), dgate_acc.reshape(TOKENS, TOP), grad_gate, grad_up, grad_down)
```

```python
import jax
import jax.numpy as jnp
from jax import lax
from jax.sharding import PartitionSpec as P

BF16 = jnp.bfloat16
F32 = jnp.float32


def slot_table(ids, expert_of_row, capacity):
    tok = ids.shape[-1]
    member = jnp.any(ids[..., None, :, :] == expert_of_row[:, None, None], axis=-2)
    earlier = (jnp.arange(tok)[:, None] < jnp.arange(tok)[None, :]).astype(BF16)
    rank = jnp.dot(member.astype(BF16), earlier, preferred_element_type=F32).astype(jnp.int32)
    place = jnp.arange(capacity, dtype=jnp.int32)
    return member[:, None, :] & (rank[:, None, :] == place[None, :, None])


def on_device(tokens, expert_ids, gate_prob, w_gate, w_up, w_down, d_mixed):
    tok, feature = tokens.shape
    top = expert_ids.shape[1]
    experts = lax.axis_size("expert")
    capacity = max(2, 2 * tok * top // experts)
    planes = max(1, experts * capacity // tok)
    plane = experts // planes
    me = lax.axis_index("expert")
    my_plane, my_col = me // plane, me % plane
    bits = [1 << b for b in range(planes.bit_length() - 1)]

    def hop(value, flip):
        pairs = [(e, e ^ flip) for e in range(experts)]
        return lax.ppermute(value, "expert", pairs)

    def along_z(value):
        held = {0: value}
        for bit in reversed(bits):
            for j in sorted(held):
                held[j ^ bit] = hop(held[j], bit * plane)
        return held

    ids_own = expert_ids.T
    meta = jnp.concatenate([ids_own.astype(F32), gate_prob.T], 0)
    meta_all = lax.all_gather(meta, "expert")
    order = jnp.array(
        [[(j * plane) ^ i for i in range(plane)] for j in range(planes)], jnp.int32
    ).reshape(-1)
    meta_rel = meta_all[me ^ order]
    ids_rel = meta_rel[:, :top].astype(jnp.int32)
    gate_rel = meta_rel[:, top:]
    columns = my_plane * plane + (my_col ^ jnp.arange(plane, dtype=jnp.int32))
    pick = {0: slot_table(ids_own, columns, capacity).astype(BF16)}
    for j in range(1, planes):
        pick[j] = slot_table(ids_rel[j * plane], columns, capacity).astype(BF16)
    mine = jax.vmap(lambda ids: slot_table(ids, me[None], capacity)[0])(ids_rel)
    gate_tok = jnp.sum(jnp.where(ids_rel == me, gate_rel, 0.0), 1)
    gate_slot = jnp.sum(jnp.where(mine, gate_tok[:, None, :], 0.0), 2).reshape(-1, 1)

    def dispatch(held):
        parts = {}
        for j in held:
            rows = jnp.einsum("irt,tf->irf", pick[j], held[j], preferred_element_type=F32).astype(BF16)
            for i in range(plane):
                parts[j, i] = rows[i] if i == 0 else hop(rows[i], i)
        return jnp.concatenate([parts[j, i] for j in range(planes) for i in range(plane)], 0)

    def combine(rows):
        rows = rows.reshape(planes, plane, capacity, feature)
        total = {}
        for j in reversed(range(planes)):
            back = [rows[j, i] if i == 0 else hop(rows[j, i], i) for i in range(plane)]
            total[j] = jnp.einsum(
                "irt,irf->tf", pick[j], jnp.stack(back), preferred_element_type=F32
            )
        for bit in bits:
            for j in sorted(total, reverse=True):
                if j & bit:
                    came = hop(total.pop(j).astype(BF16), bit * plane)
                    total[j ^ bit] = total[j ^ bit] + came.astype(F32)
        return total[0].astype(BF16)

    gate_matrix, up_matrix, down_matrix = w_gate[0], w_up[0], w_down[0]
    hidden_units = gate_matrix.shape[1]
    contract_rows = (((0,), (0,)), ((), ()))
    contract_cols = (((1,), (1,)), ((), ()))

    held_x = along_z(tokens)
    held_d = along_z(d_mixed)
    x_rows = dispatch(held_x)
    gate_pre = jnp.dot(x_rows, gate_matrix, preferred_element_type=F32)
    up_pre = jnp.dot(x_rows, up_matrix, preferred_element_type=F32)
    sig_gate = jax.nn.sigmoid(gate_pre)
    silu_gate = gate_pre * sig_gate
    hidden = (silu_gate * up_pre).astype(BF16)
    expert_out = jnp.dot(hidden, down_matrix, preferred_element_type=F32).astype(BF16)
    y_scaled = (gate_slot * expert_out.astype(F32)).astype(BF16)
    mixed = combine(y_scaled)

    d_rows = dispatch(held_d)
    dy_rows = (gate_slot * d_rows.astype(F32)).astype(BF16)
    back_hidden = lax.dot_general(dy_rows, down_matrix, contract_cols, preferred_element_type=F32)
    d_silu = sig_gate * (1.0 + gate_pre * (1.0 - sig_gate))
    grad_pre_gate = (back_hidden * up_pre * d_silu).astype(BF16)
    grad_pre_up = (back_hidden * silu_gate).astype(BF16)
    expert_dx = (
        lax.dot_general(grad_pre_gate, gate_matrix, contract_cols, preferred_element_type=F32)
        + lax.dot_general(grad_pre_up, up_matrix, contract_cols, preferred_element_type=F32)
    ).astype(BF16)
    d_tokens = combine(expert_dx)

    slot_grad = jnp.sum(d_rows.astype(F32) * expert_out.astype(F32), 1).reshape(experts, capacity)
    slot_grad = slot_grad[me ^ order]
    grad_all = lax.all_gather(slot_grad, "expert")
    grad_own = lax.dynamic_index_in_dim(grad_all, me, 1, keepdims=False)
    table = slot_table(ids_own, jnp.arange(experts, dtype=jnp.int32), capacity)
    grad_tok = jnp.sum(jnp.where(table, grad_own[:, :, None], 0.0), 1)
    named = ids_own[:, None, :] == jnp.arange(experts, dtype=jnp.int32)[None, :, None]
    d_gate = jnp.sum(jnp.where(named, grad_tok[None], 0.0), 1).T

    term_gate = lax.dot_general(x_rows, grad_pre_gate, contract_rows, preferred_element_type=F32)
    term_up = lax.dot_general(x_rows, grad_pre_up, contract_rows, preferred_element_type=F32)
    term_down = lax.dot_general(dy_rows, hidden, contract_rows, preferred_element_type=F32)
    summed = lax.psum_scatter(
        jnp.concatenate([term_gate, term_up, term_down], 1).astype(BF16),
        "dp",
        scatter_dimension=0,
        tiled=True,
    ).astype(F32)
    grad_gate = summed[:, :hidden_units][None]
    grad_up = summed[:, hidden_units : 2 * hidden_units][None]
    grad_down = summed[:, 2 * hidden_units :].T[None]
    return (mixed, d_tokens, d_gate, grad_gate, grad_up, grad_down)


def solution(mesh):
    in_specs = (
        P(("dp", "expert"), None),
        P(("dp", "expert"), None),
        P(("dp", "expert"), None),
        P("expert", None, None),
        P("expert", None, None),
        P("expert", None, None),
        P(("dp", "expert"), None),
    )
    out_specs = (
        P(("dp", "expert"), None),
        P(("dp", "expert"), None),
        P(("dp", "expert"), None),
        P("expert", "dp", None),
        P("expert", "dp", None),
        P("expert", None, "dp"),
    )
    return jax.shard_map(
        on_device, mesh=mesh, in_specs=in_specs, out_specs=out_specs, check_vma=False
    )
```

```python
import functools

import jax
import jax.numpy as jnp
from jax import lax
from jax.experimental import pallas as pl
from jax.experimental.pallas import tpu as pltpu
from jax.sharding import PartitionSpec as P

BF16 = jnp.bfloat16
F32 = jnp.float32
LANES = 128
STRIP = 512
VMEM = pl.BlockSpec(memory_space=pltpu.VMEM)
PARAMS = pltpu.CompilerParams(vmem_limit_bytes=40 * 1024 * 1024)


def pieces(value):
    out = []
    for _ in range(3):
        part = lax.reduce_precision(value, 8, 7)
        out.append(part.astype(BF16))
        value = value - part
    return out


def local_call(kernel, outs, args, flops):
    size = sum(x.size * x.dtype.itemsize for x in (*outs, *args))
    return pl.pallas_call(
        kernel,
        out_shape=outs,
        in_specs=[VMEM] * len(args),
        out_specs=[VMEM] * len(outs),
        compiler_params=PARAMS,
        cost_estimate=pl.CostEstimate(flops=flops, bytes_accessed=size, transcendentals=0),
    )(*args)


def strips(width):
    return [(c, min(c + STRIP, width)) for c in range(0, width, STRIP)]


def table_kernel(plane, capacity, top, count, *refs):
    metas, (me_ref,), tables = refs[:count], refs[count : count + 1], refs[count + 1 :]
    me = me_ref[0]
    tok = metas[0].shape[0]
    span = 2 * capacity
    wide = plane * span
    slot = lax.broadcasted_iota(jnp.int32, (1, wide), 1)
    expert = (me - lax.rem(me, plane)) + slot // span + 1
    member_of = lax.rem(slot, span) // capacity
    place = lax.rem(slot, capacity)
    row = lax.broadcasted_iota(jnp.int32, (tok, tok), 0)
    column = lax.broadcasted_iota(jnp.int32, (tok, tok), 1)
    earlier = jnp.where(row > column, 1.0, 0.0).astype(BF16)
    for b in range(count):
        ids = metas[b][:, :top].astype(F32)
        member = jnp.zeros((tok, wide), F32)
        for k in range(top):
            member += jnp.where(ids[:, k : k + 1] == expert.astype(F32), 1.0, 0.0)
        rank = jnp.dot(earlier, member.astype(BF16), preferred_element_type=F32)
        mine = jnp.where(member_of == b % 2, 1.0, 0.0)
        held = jnp.where(rank == place.astype(F32), member * mine, 0.0)
        tables[b // 2][(b % 2) * tok : (b % 2 + 1) * tok, :] = held.astype(BF16)


def pick_kernel(n_out, with_meta, *refs):
    table_ref, first, second = refs[:3]
    parts = refs[len(refs) - n_out :]
    table = table_ref[...]
    rows = parts[0].shape[0]
    width = first.shape[1]
    sources = [(c, e, (first, second), c) for c, e in strips(width)]
    if with_meta:
        sources.append((0, LANES, (refs[3], refs[4]), width))
    for c, e, (one, two), at in sources:
        block = jnp.concatenate([one[:, c:e], two[:, c:e]], 0)
        got = lax.dot_general(
            table, block, (((0,), (0,)), ((), ())), preferred_element_type=F32
        ).astype(BF16)
        for i in range(n_out):
            parts[i][:, at : at + e - c] = got[i * rows : (i + 1) * rows]


def info_kernel(top, got_ref, me_ref, info_ref):
    number = (me_ref[0] + 1).astype(F32)
    tail = got_ref[...].astype(F32)
    lane = lax.broadcasted_iota(jnp.int32, tail.shape, 1)
    out = jnp.zeros_like(tail)
    total = jnp.zeros((tail.shape[0], 1), F32)
    for k in range(top):
        named = jnp.where(tail[:, k : k + 1] == number, 1.0, 0.0)
        weight = tail[:, top + k : top + k + 1]
        for term in (1, 2):
            weight = weight + tail[:, top + term * top + k : top + term * top + k + 1]
        total += named * weight
        out = jnp.where(lane == k + 1, named, out)
    info_ref[...] = jnp.where(lane == 0, total, out)


def combine_kernel(table_ref, back_ref, out_ref):
    table = table_ref[...]
    for c, e in strips(out_ref.shape[1]):
        got = jnp.dot(table, back_ref[:, c:e], preferred_element_type=F32)
        out_ref[:, c:e] = got.astype(out_ref.dtype)


def on_device(tokens, expert_ids, gate_prob, w_gate, w_up, w_down, d_mixed):
    tok, feature = tokens.shape
    top = expert_ids.shape[1]
    experts = lax.axis_size("expert")
    capacity = max(2, 2 * tok * top // experts)
    planes = experts * capacity // tok
    plane = experts // planes
    me = lax.axis_index("expert")
    me_arr = me[None]
    bits = [1 << b for b in range(planes.bit_length() - 1)]
    groups = [[j, j + planes // 2] for j in range(planes // 2)]
    plane_sets = [[z * plane + p for p in range(plane)] for z in range(planes)]
    rows = 2 * tok

    def hop(value, flip):
        pairs = [(e, e ^ flip) for e in range(experts)]
        return lax.ppermute(value, "expert", pairs)

    def in_plane(value):
        shaped = value.reshape(plane, 2 * capacity, value.shape[1])
        got = lax.all_to_all(
            shaped, "expert", 0, 0, axis_index_groups=plane_sets, tiled=True
        )
        return got.reshape(value.shape)

    def after(value, *earlier):
        return lax.optimization_barrier((value, *earlier))

    shape = jax.ShapeDtypeStruct

    def along_z(value):
        held = {0: value}
        for bit in reversed(bits):
            for j in sorted(held):
                held[j ^ bit] = hop(held[j], bit * plane)
        return held

    blank = jnp.zeros((tok, LANES - 4 * top), BF16)
    meta = jnp.concatenate([(expert_ids + 1).astype(BF16), *pieces(gate_prob), blank], 1)
    held_x, held_m = {0: tokens}, {0: meta}
    for bit in reversed(bits):
        for j in sorted(held_x):
            held_x[j ^ bit] = hop(held_x[j], bit * plane)
        for j in sorted(held_m):
            held_m[j ^ bit] = hop(held_m[j], bit * plane)
        if bit == bits[-1]:
            held_x[bit], held_m[bit] = after(held_x[bit], held_m[bit])
    top_bit = bits[-1]
    d_late, held_x[top_bit] = after(d_mixed, held_x[top_bit])
    held_d = along_z(d_late)

    tables = [
        local_call(
            functools.partial(table_kernel, plane, capacity, top, 2),
            [shape((rows, rows), BF16)],
            [held_m[group[0]], held_m[group[1]], me_arr],
            4 * rows * rows * tok,
        )[0]
        for group in groups
    ]

    def dispatch(g, held, extra):
        group = groups[g]
        args = [tables[g], held[group[0]], held[group[1]]]
        width = feature
        if extra is not None:
            args += [extra[group[0]], extra[group[1]]]
            width += LANES
        (picked,) = local_call(
            functools.partial(pick_kernel, 1, extra is not None),
            [shape((rows, width), BF16)],
            args,
            2 * rows * rows * width,
        )
        return in_plane(picked)

    def combine(g, value):
        back = in_plane(value)
        (both,) = local_call(
            combine_kernel,
            [shape(back.shape, F32 if g == 0 else BF16)],
            [tables[g], back],
            2 * rows * rows * back.shape[1],
        )
        return both

    def back_along_z(total):
        for bit in bits[:-1]:
            for g in sorted(total, reverse=True):
                if g & bit:
                    came = hop(total.pop(g).astype(BF16), bit * plane)
                    total[g ^ bit] = total[g ^ bit] + came.astype(F32)
        came = hop(total[0][tok:].astype(BF16), top_bit * plane)
        return total[0][:tok] + came.astype(F32)

    gate_matrix, up_matrix, down_matrix = w_gate[0], w_up[0], w_down[0]
    hidden_units = gate_matrix.shape[1]
    contract_rows = (((0,), (0,)), ((), ()))
    contract_cols = (((1,), (1,)), ((), ()))
    order = range(len(groups))

    x_rows, info, gate_pre, up_pre, sig_gate, silu_gate, hidden = {}, {}, {}, {}, {}, {}, {}
    for g in order:
        got = dispatch(g, held_x, held_m)
        x_rows[g] = got[:, :feature]
        info[g] = pl.pallas_call(
            functools.partial(info_kernel, top),
            out_shape=shape((rows, LANES), F32),
            grid=(1,),
            in_specs=[
                pl.BlockSpec((rows, LANES), lambda n: (0, feature // LANES)),
                pl.BlockSpec(memory_space=pltpu.SMEM),
            ],
            out_specs=pl.BlockSpec((rows, LANES), lambda n: (0, 0)),
            compiler_params=PARAMS,
        )(got, me_arr)
        gate_pre[g] = jnp.dot(x_rows[g], gate_matrix, preferred_element_type=F32)
        up_pre[g] = jnp.dot(x_rows[g], up_matrix, preferred_element_type=F32)
        sig_gate[g] = jax.nn.sigmoid(gate_pre[g])
        silu_gate[g] = gate_pre[g] * sig_gate[g]
        hidden[g] = (silu_gate[g] * up_pre[g]).astype(BF16)
    expert_out, y_scaled, total = {}, {}, {}
    for g in reversed(order):
        expert_out[g] = jnp.dot(hidden[g], down_matrix, preferred_element_type=F32).astype(BF16)
        y_scaled[g] = (info[g][:, :1] * expert_out[g].astype(F32)).astype(BF16)
    info[0], *held_y = after(info[0], *[y_scaled[g] for g in order])
    for g in reversed(order):
        total[g] = combine(g, held_y[g])
    last = groups[-1][0]
    held_d[last], total[order[-1]] = after(held_d[last], total[order[-1]])
    mixed = back_along_z(total).astype(BF16)

    dy_rows, grad_pre_gate, grad_pre_up, back_rows = {}, {}, {}, {}
    for g in order:
        d_rows = dispatch(g, held_d, None)
        dy_rows[g] = (info[g][:, :1] * d_rows.astype(F32)).astype(BF16)
        back_hidden = lax.dot_general(
            dy_rows[g], down_matrix, contract_cols, preferred_element_type=F32
        )
        d_silu = sig_gate[g] * (1.0 + gate_pre[g] * (1.0 - sig_gate[g]))
        grad_pre_gate[g] = (back_hidden * up_pre[g] * d_silu).astype(BF16)
        grad_pre_up[g] = (back_hidden * silu_gate[g]).astype(BF16)
        expert_dx = (
            lax.dot_general(
                grad_pre_gate[g], gate_matrix, contract_cols, preferred_element_type=F32
            )
            + lax.dot_general(
                grad_pre_up[g], up_matrix, contract_cols, preferred_element_type=F32
            )
        ).astype(BF16)
        slot_grad = jnp.sum(d_rows.astype(F32) * expert_out[g].astype(F32), 1, keepdims=True)
        grad_cols = jnp.concatenate(pieces(info[g][:, 1 : 1 + top] * slot_grad), 1)
        blank = jnp.zeros((rows, LANES - 3 * top), BF16)
        back_rows[g] = jnp.concatenate([expert_dx, grad_cols, blank], 1)
    joined = after(
        back_rows[0],
        back_rows[1],
        *[jnp.concatenate([part[g] for g in order], 0) for part in (grad_pre_gate, grad_pre_up)],
    )
    back_rows[0], back_rows[1], all_gate, all_up = joined
    total = {}
    for g in reversed(order):
        total[g] = combine(g, back_rows[g])
    result = back_along_z(total)
    d_tokens = result[:, :feature].astype(BF16)
    d_gate = functools.reduce(
        lambda a, b: a + b,
        [result[:, feature + n * top : feature + (n + 1) * top] for n in range(3)],
    )

    all_x, all_dy, all_hidden = (
        jnp.concatenate([part[g] for g in order], 0) for part in (x_rows, dy_rows, hidden)
    )
    term_gate = lax.dot_general(all_gate, all_x, contract_rows, preferred_element_type=F32)
    term_up = lax.dot_general(all_up, all_x, contract_rows, preferred_element_type=F32)
    term_down = lax.dot_general(all_hidden, all_dy, contract_rows, preferred_element_type=F32)
    summed = lax.psum_scatter(
        jnp.concatenate([term_gate, term_up, term_down], 0).astype(BF16),
        "dp",
        scatter_dimension=1,
        tiled=True,
    )
    grad_gate = summed[:hidden_units].astype(F32).T[None]
    grad_up = summed[hidden_units : 2 * hidden_units].astype(F32).T[None]
    grad_down = summed[2 * hidden_units :].astype(F32)[None]
    return (mixed, d_tokens, d_gate, grad_gate, grad_up, grad_down)


def solution(mesh):
    in_specs = (
        P(("dp", "expert"), None),
        P(("dp", "expert"), None),
        P(("dp", "expert"), None),
        P("expert", None, None),
        P("expert", None, None),
        P("expert", None, None),
        P(("dp", "expert"), None),
    )
    out_specs = (
        P(("dp", "expert"), None),
        P(("dp", "expert"), None),
        P(("dp", "expert"), None),
        P("expert", "dp", None),
        P("expert", "dp", None),
        P("expert", None, "dp"),
    )
    return jax.shard_map(
        on_device, mesh=mesh, in_specs=in_specs, out_specs=out_specs, check_vma=False
    )
```

```python
import functools

import jax
import jax.numpy as jnp
from jax import lax
from jax.experimental import pallas as pl
from jax.experimental.pallas import tpu as pltpu
from jax.sharding import PartitionSpec as P

BF16 = jnp.bfloat16
F32 = jnp.float32
LANES = 128
STRIP = 512
VMEM = pl.BlockSpec(memory_space=pltpu.VMEM)
SMEM = pl.BlockSpec(memory_space=pltpu.SMEM)


def local_call(kernel, outs, me, args, flops):
    size = sum(x.size * x.dtype.itemsize for x in (*outs, *args))
    return pl.pallas_call(
        kernel,
        out_shape=outs,
        in_specs=[SMEM] + [VMEM] * len(args),
        out_specs=[VMEM] * len(outs),
        compiler_params=pltpu.CompilerParams(vmem_limit_bytes=16 * 1024 * 1024),
        cost_estimate=pl.CostEstimate(flops=flops, bytes_accessed=size, transcendentals=0),
    )(me, *args)


def strips(width):
    return [(c, min(c + STRIP, width)) for c in range(0, width, STRIP)]


def slot_tables(me, metas, top, side, capacity):
    count = len(metas)
    span = count * capacity
    tok = metas[0].shape[1]
    slot = lax.broadcasted_iota(jnp.int32, (side * span, tok), 0)
    expert = ((me - lax.rem(me, side)) + slot // span).astype(F32)
    block_of = lax.rem(slot, span) // capacity
    place = lax.rem(slot, capacity).astype(F32)
    row = lax.broadcasted_iota(jnp.int32, (tok, tok), 0)
    column = lax.broadcasted_iota(jnp.int32, (tok, tok), 1)
    earlier = jnp.where(row < column, 1.0, 0.0).astype(BF16)
    tables = []
    for b in range(count):
        named = [jnp.where(metas[b][k : k + 1, :] == expert, 1.0, 0.0) for k in range(top)]
        member = functools.reduce(lambda p, q: p + q, named)
        rank = jnp.dot(member.astype(BF16), earlier, preferred_element_type=F32)
        here = rank == place
        if count > 1:
            here = here & (block_of == b)
        tables.append([jnp.where(here, part, 0.0) for part in named])
    return tables


def pick_kernel(top, side, capacity, count, scaled, me_ref, *refs):
    metas, blocks, out = refs[:count], refs[count : 2 * count], refs[2 * count]
    tables = slot_tables(me_ref[0], metas, top, side, capacity)
    held = jnp.concatenate([functools.reduce(lambda p, q: p + q, ks) for ks in tables], 1)
    held = held.astype(BF16)
    if scaled:
        gate = 0.0
        for meta, ks in zip(metas, tables):
            for k, part in enumerate(ks):
                gate += jnp.sum(part * meta[top + k : top + k + 1, :], 1, keepdims=True)
    for c, e in strips(out.shape[1]):
        block = jnp.concatenate([ref[:, c:e] for ref in blocks], 0)
        got = jnp.dot(held, block, preferred_element_type=F32)
        out[:, c:e] = ((gate * got) if scaled else got).astype(BF16)


TRANSPOSED = (((0,), (0,)), ((), ()))


def sum_kernel(top, side, capacity, count, me_ref, *refs):
    metas, back, outs = refs[:count], refs[count], refs[count + 1 :]
    tables = slot_tables(me_ref[0], metas, top, side, capacity)
    for ks, out in zip(tables, outs):
        held = functools.reduce(lambda p, q: p + q, ks).astype(BF16)
        for c, e in strips(out.shape[1]):
            out[:, c:e] = lax.dot_general(
                held, back[:, c:e], TRANSPOSED, preferred_element_type=F32
            ).astype(out.dtype)


def mix_kernel(top, side, capacity, count, me_ref, *refs):
    metas, blocks, back = refs[:count], refs[count : 2 * count], refs[2 * count]
    outs, grads = refs[2 * count + 1 : 3 * count + 1], refs[3 * count + 1 :]
    tables = slot_tables(me_ref[0], metas, top, side, capacity)
    tok = metas[0].shape[1]
    lane = lax.broadcasted_iota(jnp.int32, (tok, LANES), 1)
    for b in range(count):
        held = [part.astype(BF16) for part in tables[b]]
        gates = [metas[b][top + k : top + k + 1, :] for k in range(top)]
        gates = [jnp.transpose(jnp.broadcast_to(g, (8, tok)))[:, :1] for g in gates]
        sums = [jnp.zeros((tok, 1), F32) for _ in range(top)]
        for c, e in strips(outs[b].shape[1]):
            cotangent = blocks[b][:, c:e].astype(F32)
            mixed = 0.0
            for k in range(top):
                got = lax.dot_general(held[k], back[:, c:e], TRANSPOSED, preferred_element_type=F32)
                mixed += gates[k] * got
                sums[k] += jnp.sum(cotangent * got, 1, keepdims=True)
            outs[b][:, c:e] = mixed.astype(outs[b].dtype)
        grad = jnp.zeros((tok, LANES), F32)
        for k in range(top):
            grad = jnp.where(lane == k, sums[k], grad)
        grads[b][...] = grad


def on_device(tokens, expert_ids, gate_prob, w_gate, w_up, w_down, d_mixed):
    tok, feature = tokens.shape
    top = expert_ids.shape[1]
    experts = lax.axis_size("expert")
    capacity = max(2, 2 * tok * top // experts)
    side = experts // 2
    half = side * capacity
    me = lax.axis_index("expert")
    me_arr = me[None]
    sets = [[h * side + p for p in range(side)] for h in range(2)]
    shape = jax.ShapeDtypeStruct

    def across(value):
        return lax.ppermute(value, "expert", [(e, (e + side) % experts) for e in range(experts)])

    def exchange(value):
        shaped = value.reshape(side, value.shape[0] // side, value.shape[1])
        got = lax.all_to_all(shaped, "expert", 0, 0, axis_index_groups=sets, tiled=True)
        return got.reshape(value.shape)

    def after(value, *earlier):
        return lax.optimization_barrier((value, *earlier))

    def pick(metas, blocks, scaled):
        count = len(metas)
        return local_call(
            functools.partial(pick_kernel, top, side, capacity, count, scaled),
            [shape((count * half, feature), BF16)],
            me_arr,
            [*metas, *blocks],
            2 * count * count * half * tok * feature,
        )[0]

    def split(rows):
        parts = rows.reshape(side, 2, capacity, feature)
        return [parts[:, b].reshape(half, feature) for b in range(2)]

    meta = jnp.concatenate([expert_ids.T.astype(F32), gate_prob.T], 0)
    x_far = across(tokens)
    meta_far = across(meta)
    x_own = exchange(pick([meta], [tokens], False))
    x_far, meta_far = after(x_far, meta_far)
    d_mixed, x_far = after(d_mixed, x_far)
    d_far = across(d_mixed)
    x_other = exchange(pick([meta_far], [x_far], False))
    x_rows = jnp.stack(
        [part.reshape(side, capacity, feature) for part in (x_own, x_other)], 1
    ).reshape(2 * half, feature)

    metas = [meta, meta_far]
    dy_rows = exchange(pick(metas, [d_mixed, d_far], True))

    gate_matrix, up_matrix, down_matrix = w_gate[0], w_up[0], w_down[0]
    hidden_units = gate_matrix.shape[1]
    contract_rows = (((0,), (0,)), ((), ()))
    contract_cols = (((1,), (1,)), ((), ()))

    gate_pre = jnp.dot(x_rows, gate_matrix, preferred_element_type=F32)
    up_pre = jnp.dot(x_rows, up_matrix, preferred_element_type=F32)
    sig_gate = jax.nn.sigmoid(gate_pre)
    silu_gate = gate_pre * sig_gate
    hidden = (silu_gate * up_pre).astype(BF16)
    expert_out = jnp.dot(hidden, down_matrix, preferred_element_type=F32).astype(BF16)
    expert_out, dy_rows = after(expert_out, dy_rows)
    y_back = exchange(expert_out)

    back_hidden = lax.dot_general(dy_rows, down_matrix, contract_cols, preferred_element_type=F32)
    d_silu = sig_gate * (1.0 + gate_pre * (1.0 - sig_gate))
    grad_pre_gate = (back_hidden * up_pre * d_silu).astype(BF16)
    grad_pre_up = (back_hidden * silu_gate).astype(BF16)
    expert_dx = (
        lax.dot_general(grad_pre_gate, gate_matrix, contract_cols, preferred_element_type=F32)
        + lax.dot_general(grad_pre_up, up_matrix, contract_cols, preferred_element_type=F32)
    ).astype(BF16)
    expert_dx, grad_pre_gate, grad_pre_up = after(expert_dx, grad_pre_gate, grad_pre_up)

    def reduced(left, right):
        term = lax.dot_general(left, right, contract_rows, preferred_element_type=F32)
        return lax.psum_scatter(term.astype(BF16), "dp", scatter_dimension=1, tiled=True)

    grad_down = reduced(hidden, dy_rows)
    grad_gate = reduced(grad_pre_gate, x_rows)
    grad_up = reduced(grad_pre_up, x_rows)

    mixed_own, mixed_far, grads_own, grads_far = local_call(
        functools.partial(mix_kernel, top, side, capacity, 2),
        [
            shape((tok, feature), F32),
            shape((tok, feature), BF16),
            shape((tok, LANES), F32),
            shape((tok, LANES), F32),
        ],
        me_arr,
        [*metas, d_mixed, d_far, y_back],
        4 * top * half * 2 * tok * feature,
    )
    dx_own, dx_far = split(expert_dx)
    dx_far, y_back = after(dx_far, y_back)
    far_back = exchange(dx_far)
    far_back, dx_own = after(far_back, dx_own)
    own_back = exchange(dx_own)

    def total(metas, back, kind):
        return local_call(
            functools.partial(sum_kernel, top, side, capacity, 1),
            [shape((tok, feature), kind)],
            me_arr,
            [*metas, back],
            2 * half * tok * feature,
        )[0]

    tokens_far = across(total([meta_far], far_back, BF16))
    mixed = (mixed_own + across(mixed_far).astype(F32)).astype(BF16)
    d_gate = (grads_own + across(grads_far))[:, :top]
    tokens_own = total([meta], own_back, F32)
    d_tokens = (tokens_own + tokens_far.astype(F32)).astype(BF16)
    return (
        mixed,
        d_tokens,
        d_gate,
        grad_gate.astype(F32).T[None],
        grad_up.astype(F32).T[None],
        grad_down.astype(F32)[None],
    )


def solution(mesh):
    in_specs = (
        P(("dp", "expert"), None),
        P(("dp", "expert"), None),
        P(("dp", "expert"), None),
        P("expert", None, None),
        P("expert", None, None),
        P("expert", None, None),
        P(("dp", "expert"), None),
    )
    out_specs = (
        P(("dp", "expert"), None),
        P(("dp", "expert"), None),
        P(("dp", "expert"), None),
        P("expert", "dp", None),
        P("expert", "dp", None),
        P("expert", None, "dp"),
    )
    return jax.shard_map(
        on_device, mesh=mesh, in_specs=in_specs, out_specs=out_specs, check_vma=False
    )
```

```python
import functools

import jax
import jax.numpy as jnp
from jax import lax
from jax.experimental import pallas as pl
from jax.experimental.pallas import tpu as pltpu
from jax.sharding import PartitionSpec as P

BF16 = jnp.bfloat16
F32 = jnp.float32
LANES = 128
STRIP = 512
VMEM = pl.BlockSpec(memory_space=pltpu.VMEM)
SMEM = pl.BlockSpec(memory_space=pltpu.SMEM)


def local_call(kernel, outs, me, args, flops):
    size = sum(x.size * x.dtype.itemsize for x in (*outs, *args))
    return pl.pallas_call(
        kernel,
        out_shape=outs,
        in_specs=[SMEM] + [VMEM] * len(args),
        out_specs=[VMEM] * len(outs),
        compiler_params=pltpu.CompilerParams(vmem_limit_bytes=16 * 1024 * 1024),
        cost_estimate=pl.CostEstimate(flops=flops, bytes_accessed=size, transcendentals=0),
    )(me, *args)


def strips(width):
    return [(c, min(c + STRIP, width)) for c in range(0, width, STRIP)]


def slot_tables(me, metas, top, side, capacity):
    count = len(metas)
    span = count * capacity
    tok = metas[0].shape[1]
    slot = lax.broadcasted_iota(jnp.int32, (side * span, tok), 0)
    expert = ((me - lax.rem(me, side)) + slot // span).astype(F32)
    block_of = lax.rem(slot, span) // capacity
    place = lax.rem(slot, capacity).astype(F32)
    row = lax.broadcasted_iota(jnp.int32, (tok, tok), 0)
    column = lax.broadcasted_iota(jnp.int32, (tok, tok), 1)
    earlier = jnp.where(row < column, 1.0, 0.0).astype(BF16)
    tables = []
    for b in range(count):
        named = [jnp.where(metas[b][k : k + 1, :] == expert, 1.0, 0.0) for k in range(top)]
        member = functools.reduce(lambda p, q: p + q, named)
        rank = jnp.dot(member.astype(BF16), earlier, preferred_element_type=F32)
        here = rank == place
        if count > 1:
            here = here & (block_of == b)
        tables.append([jnp.where(here, part, 0.0) for part in named])
    return tables


def pick_kernel(top, side, capacity, count, scaled, me_ref, *refs):
    metas, blocks, out = refs[:count], refs[count : 2 * count], refs[2 * count]
    tables = slot_tables(me_ref[0], metas, top, side, capacity)
    held = jnp.concatenate([functools.reduce(lambda p, q: p + q, ks) for ks in tables], 1)
    held = held.astype(BF16)
    if scaled:
        gate = 0.0
        for meta, ks in zip(metas, tables):
            for k, part in enumerate(ks):
                gate += jnp.sum(part * meta[top + k : top + k + 1, :], 1, keepdims=True)
    for c, e in strips(out.shape[1]):
        block = jnp.concatenate([ref[:, c:e] for ref in blocks], 0)
        got = jnp.dot(held, block, preferred_element_type=F32)
        out[:, c:e] = ((gate * got) if scaled else got).astype(BF16)


TRANSPOSED = (((0,), (0,)), ((), ()))


def sum_kernel(top, side, capacity, count, me_ref, *refs):
    metas, back, outs = refs[:count], refs[count], refs[count + 1 :]
    tables = slot_tables(me_ref[0], metas, top, side, capacity)
    for ks, out in zip(tables, outs):
        held = functools.reduce(lambda p, q: p + q, ks).astype(BF16)
        for c, e in strips(out.shape[1]):
            out[:, c:e] = lax.dot_general(
                held, back[:, c:e], TRANSPOSED, preferred_element_type=F32
            ).astype(out.dtype)


def mix_kernel(top, side, capacity, count, me_ref, *refs):
    metas, blocks, back = refs[:count], refs[count : 2 * count], refs[2 * count]
    outs, grads = refs[2 * count + 1 : 3 * count + 1], refs[3 * count + 1 :]
    tables = slot_tables(me_ref[0], metas, top, side, capacity)
    tok = metas[0].shape[1]
    lane = lax.broadcasted_iota(jnp.int32, (tok, LANES), 1)
    for b in range(count):
        held = [part.astype(BF16) for part in tables[b]]
        gates = [metas[b][top + k : top + k + 1, :] for k in range(top)]
        gates = [jnp.transpose(jnp.broadcast_to(g, (8, tok)))[:, :1] for g in gates]
        sums = [jnp.zeros((tok, 1), F32) for _ in range(top)]
        for c, e in strips(outs[b].shape[1]):
            cotangent = blocks[b][:, c:e].astype(F32)
            mixed = 0.0
            for k in range(top):
                got = lax.dot_general(held[k], back[:, c:e], TRANSPOSED, preferred_element_type=F32)
                mixed += gates[k] * got
                sums[k] += jnp.sum(cotangent * got, 1, keepdims=True)
            outs[b][:, c:e] = mixed.astype(outs[b].dtype)
        grad = jnp.zeros((tok, LANES), F32)
        for k in range(top):
            grad = jnp.where(lane == k, sums[k], grad)
        grads[b][...] = grad


def on_device(tokens, expert_ids, gate_prob, w_gate, w_up, w_down, d_mixed):
    tok, feature = tokens.shape
    top = expert_ids.shape[1]
    experts = lax.axis_size("expert")
    capacity = max(2, 2 * tok * top // experts)
    side = experts // 2
    half = side * capacity
    me = lax.axis_index("expert")
    me_arr = me[None]
    sets = [[h * side + p for p in range(side)] for h in range(2)]
    shape = jax.ShapeDtypeStruct

    def across(value):
        return lax.ppermute(value, "expert", [(e, (e + side) % experts) for e in range(experts)])

    def exchange(value):
        shaped = value.reshape(side, value.shape[0] // side, value.shape[1])
        got = lax.all_to_all(shaped, "expert", 0, 0, axis_index_groups=sets, tiled=True)
        return got.reshape(value.shape)

    def after(value, *earlier):
        return lax.optimization_barrier((value, *earlier))

    def pick(metas, blocks, scaled):
        count = len(metas)
        return local_call(
            functools.partial(pick_kernel, top, side, capacity, count, scaled),
            [shape((count * half, feature), BF16)],
            me_arr,
            [*metas, *blocks],
            2 * count * count * half * tok * feature,
        )[0]

    meta = jnp.concatenate([expert_ids.T.astype(F32), gate_prob.T], 0)
    x_far = across(tokens)
    meta_far = across(meta)
    x_far, meta_far = after(x_far, meta_far)
    d_mixed, x_far = after(d_mixed, x_far)
    d_far = across(d_mixed)
    metas = [meta, meta_far]
    x_rows = exchange(pick(metas, [tokens, x_far], False))
    dy_rows = exchange(pick(metas, [d_mixed, d_far], True))

    gate_matrix, up_matrix, down_matrix = w_gate[0], w_up[0], w_down[0]
    hidden_units = gate_matrix.shape[1]
    contract_rows = (((0,), (0,)), ((), ()))
    contract_cols = (((1,), (1,)), ((), ()))

    gate_pre = jnp.dot(x_rows, gate_matrix, preferred_element_type=F32)
    up_pre = jnp.dot(x_rows, up_matrix, preferred_element_type=F32)
    sig_gate = jax.nn.sigmoid(gate_pre)
    silu_gate = gate_pre * sig_gate
    hidden = (silu_gate * up_pre).astype(BF16)
    expert_out = jnp.dot(hidden, down_matrix, preferred_element_type=F32).astype(BF16)
    expert_out, dy_rows = after(expert_out, dy_rows)
    y_back = exchange(expert_out)

    back_hidden = lax.dot_general(dy_rows, down_matrix, contract_cols, preferred_element_type=F32)
    d_silu = sig_gate * (1.0 + gate_pre * (1.0 - sig_gate))
    grad_pre_gate = (back_hidden * up_pre * d_silu).astype(BF16)
    grad_pre_up = (back_hidden * silu_gate).astype(BF16)
    expert_dx = (
        lax.dot_general(grad_pre_gate, gate_matrix, contract_cols, preferred_element_type=F32)
        + lax.dot_general(grad_pre_up, up_matrix, contract_cols, preferred_element_type=F32)
    ).astype(BF16)
    expert_dx, y_back, grad_pre_gate, grad_pre_up, hidden = after(
        expert_dx, y_back, grad_pre_gate, grad_pre_up, hidden
    )

    def reduced(left, right):
        term = lax.dot_general(left, right, contract_rows, preferred_element_type=F32)
        return lax.psum_scatter(term.astype(BF16), "dp", scatter_dimension=1, tiled=True)

    grad_down = reduced(hidden, dy_rows)
    grad_gate = reduced(grad_pre_gate, x_rows)
    grad_up = reduced(grad_pre_up, x_rows)

    mixed_own, mixed_far, grads_own, grads_far = local_call(
        functools.partial(mix_kernel, top, side, capacity, 2),
        [
            shape((tok, feature), F32),
            shape((tok, feature), BF16),
            shape((tok, LANES), F32),
            shape((tok, LANES), F32),
        ],
        me_arr,
        [*metas, d_mixed, d_far, y_back],
        4 * top * half * 2 * tok * feature,
    )
    dx_back = exchange(expert_dx)
    tokens_own, tokens_far = local_call(
        functools.partial(sum_kernel, top, side, capacity, 2),
        [shape((tok, feature), F32), shape((tok, feature), BF16)],
        me_arr,
        [*metas, dx_back],
        4 * half * tok * feature,
    )
    mixed = (mixed_own + across(mixed_far).astype(F32)).astype(BF16)
    d_gate = (grads_own + across(grads_far))[:, :top]
    d_tokens = (tokens_own + across(tokens_far).astype(F32)).astype(BF16)
    return (
        mixed,
        d_tokens,
        d_gate,
        grad_gate.astype(F32).T[None],
        grad_up.astype(F32).T[None],
        grad_down.astype(F32)[None],
    )


def solution(mesh):
    in_specs = (
        P(("dp", "expert"), None),
        P(("dp", "expert"), None),
        P(("dp", "expert"), None),
        P("expert", None, None),
        P("expert", None, None),
        P("expert", None, None),
        P(("dp", "expert"), None),
    )
    out_specs = (
        P(("dp", "expert"), None),
        P(("dp", "expert"), None),
        P(("dp", "expert"), None),
        P("expert", "dp", None),
        P("expert", "dp", None),
        P("expert", None, "dp"),
    )
    return jax.shard_map(
        on_device, mesh=mesh, in_specs=in_specs, out_specs=out_specs, check_vma=False
    )
```

```python
import functools

import jax
import jax.numpy as jnp
from jax import lax
from jax.experimental import pallas as pl
from jax.experimental.pallas import tpu as pltpu
from jax.sharding import PartitionSpec as P

BF16 = jnp.bfloat16
F32 = jnp.float32
LANES = 128
STRIP = 512
VMEM = pl.BlockSpec(memory_space=pltpu.VMEM)
SMEM = pl.BlockSpec(memory_space=pltpu.SMEM)


def local_call(kernel, outs, me, args, flops):
    size = sum(x.size * x.dtype.itemsize for x in (*outs, *args))
    return pl.pallas_call(
        kernel,
        out_shape=outs,
        in_specs=[SMEM] + [VMEM] * len(args),
        out_specs=[VMEM] * len(outs),
        compiler_params=pltpu.CompilerParams(vmem_limit_bytes=16 * 1024 * 1024),
        cost_estimate=pl.CostEstimate(flops=flops, bytes_accessed=size, transcendentals=0),
    )(me, *args)


def strips(width, step=STRIP):
    return [(c, min(c + step, width)) for c in range(0, width, step)]


def slot_tables(me, metas, top, side, capacity):
    count = len(metas)
    span = count * capacity
    tok = metas[0].shape[1]
    slot = lax.broadcasted_iota(jnp.int32, (side * span, tok), 0)
    expert = ((me - lax.rem(me, side)) + slot // span).astype(F32)
    block_of = lax.rem(slot, span) // capacity
    place = lax.rem(slot, capacity).astype(F32)
    row = lax.broadcasted_iota(jnp.int32, (tok, tok), 0)
    column = lax.broadcasted_iota(jnp.int32, (tok, tok), 1)
    earlier = jnp.where(row < column, 1.0, 0.0).astype(BF16)
    tables = []
    for b in range(count):
        named = [jnp.where(metas[b][k : k + 1, :] == expert, 1.0, 0.0) for k in range(top)]
        member = functools.reduce(lambda p, q: p + q, named)
        rank = jnp.dot(member.astype(BF16), earlier, preferred_element_type=F32)
        here = rank == place
        if count > 1:
            here = here & (block_of == b)
        tables.append([jnp.where(here, part, 0.0) for part in named])
    return tables


def pick_kernel(top, side, capacity, count, scaled, me_ref, *refs):
    metas, blocks, out = refs[:count], refs[count : 2 * count], refs[2 * count]
    tables = slot_tables(me_ref[0], metas, top, side, capacity)
    held = jnp.concatenate([functools.reduce(lambda p, q: p + q, ks) for ks in tables], 1)
    held = held.astype(BF16)
    if scaled:
        gate = 0.0
        for meta, ks in zip(metas, tables):
            for k, part in enumerate(ks):
                gate += jnp.sum(part * meta[top + k : top + k + 1, :], 1, keepdims=True)
    for c, e in strips(out.shape[1]):
        block = jnp.concatenate([ref[:, c:e] for ref in blocks], 0)
        got = jnp.dot(held, block, preferred_element_type=F32)
        out[:, c:e] = ((gate * got) if scaled else got).astype(BF16)


TRANSPOSED = (((0,), (0,)), ((), ()))


def sum_kernel(top, side, capacity, count, me_ref, *refs):
    metas, back, outs = refs[:count], refs[count], refs[count + 1 :]
    tables = slot_tables(me_ref[0], metas, top, side, capacity)
    for ks, out in zip(tables, outs):
        held = functools.reduce(lambda p, q: p + q, ks).astype(BF16)
        for c, e in strips(out.shape[1]):
            out[:, c:e] = lax.dot_general(
                held, back[:, c:e], TRANSPOSED, preferred_element_type=F32
            ).astype(out.dtype)


def mix_kernel(top, side, capacity, count, me_ref, *refs):
    metas, blocks, back = refs[:count], refs[count : 2 * count], refs[2 * count]
    outs, grads = refs[2 * count + 1 : 3 * count + 1], refs[3 * count + 1 :]
    tables = slot_tables(me_ref[0], metas, top, side, capacity)
    tok = metas[0].shape[1]
    lane = lax.broadcasted_iota(jnp.int32, (tok, LANES), 1)
    for b in range(count):
        held = [part.astype(BF16) for part in tables[b]]
        gates = [metas[b][top + k : top + k + 1, :] for k in range(top)]
        gates = [jnp.transpose(jnp.broadcast_to(g, (8, tok)))[:, :1] for g in gates]
        sums = [jnp.zeros((tok, 1), F32) for _ in range(top)]
        for c, e in strips(outs[b].shape[1]):
            cotangent = blocks[b][:, c:e].astype(F32)
            mixed = 0.0
            for k in range(top):
                got = lax.dot_general(held[k], back[:, c:e], TRANSPOSED, preferred_element_type=F32)
                mixed += gates[k] * got
                sums[k] += jnp.sum(cotangent * got, 1, keepdims=True)
            outs[b][:, c:e] = mixed.astype(outs[b].dtype)
        grad = jnp.zeros((tok, LANES), F32)
        for k in range(top):
            grad = jnp.where(lane == k, sums[k], grad)
        grads[b][...] = grad


def backward_kernel(
    dy_ref, x_ref, gate_ref, up_ref, hidden_ref, wg_ref, wu_ref, wd_ref, dx_ref, terms_ref, gg_ref, gu_ref
):
    rows, units = gate_ref.shape
    across_last = (((1,), (1,)), ((), ()))
    for c, e in strips(units, 256):
        back = lax.dot_general(
            dy_ref[...], wd_ref[c:e, :], across_last, preferred_element_type=F32
        )
        gate = gate_ref[:, c:e]
        sig = 1.0 / (1.0 + jnp.exp(-gate))
        gg_ref[:, c:e] = (back * up_ref[:, c:e] * (sig * (1.0 + gate * (1.0 - sig)))).astype(BF16)
        gu_ref[:, c:e] = (back * (gate * sig)).astype(BF16)
    for c, e in strips(dx_ref.shape[1]):
        got = jnp.dot(gg_ref[...], wg_ref[:, c:e], preferred_element_type=F32)
        got += jnp.dot(gu_ref[...], wu_ref[:, c:e], preferred_element_type=F32)
        dx_ref[:, c:e] = got.astype(BF16)
    pairs = ((gg_ref, x_ref), (gu_ref, x_ref), (hidden_ref, dy_ref))
    for n, (left, right) in enumerate(pairs):
        for r, t in strips(units, 256):
            for c, e in strips(dx_ref.shape[1], 1024):
                terms_ref[n * units + r : n * units + t, c:e] = lax.dot_general(
                    left[:, r:t], right[:, c:e], TRANSPOSED, preferred_element_type=F32
                ).astype(BF16)


def on_device(tokens, expert_ids, gate_prob, w_gate, w_up, w_down, d_mixed):
    tok, feature = tokens.shape
    top = expert_ids.shape[1]
    experts = lax.axis_size("expert")
    capacity = max(2, 2 * tok * top // experts)
    side = experts // 2
    half = side * capacity
    me = lax.axis_index("expert")
    me_arr = me[None]
    sets = [[h * side + p for p in range(side)] for h in range(2)]
    shape = jax.ShapeDtypeStruct

    def across(value):
        return lax.ppermute(value, "expert", [(e, (e + side) % experts) for e in range(experts)])

    def exchange(value):
        shaped = value.reshape(side, value.shape[0] // side, value.shape[1])
        got = lax.all_to_all(shaped, "expert", 0, 0, axis_index_groups=sets, tiled=True)
        return got.reshape(value.shape)

    def after(value, *earlier):
        return lax.optimization_barrier((value, *earlier))

    def pick(metas, blocks, scaled):
        count = len(metas)
        return local_call(
            functools.partial(pick_kernel, top, side, capacity, count, scaled),
            [shape((count * half, feature), BF16)],
            me_arr,
            [*metas, *blocks],
            2 * count * count * half * tok * feature,
        )[0]

    def split(rows):
        parts = rows.reshape(side, 2, capacity, feature)
        return [parts[:, b].reshape(half, feature) for b in range(2)]

    meta = jnp.concatenate([expert_ids.T.astype(F32), gate_prob.T], 0)
    x_far = across(tokens)
    meta_far = across(meta)
    x_own = exchange(pick([meta], [tokens], False))
    x_far, meta_far = after(x_far, meta_far)
    d_mixed, x_far = after(d_mixed, x_far)
    d_far = across(d_mixed)
    x_other = exchange(pick([meta_far], [x_far], False))
    x_rows = jnp.stack(
        [part.reshape(side, capacity, feature) for part in (x_own, x_other)], 1
    ).reshape(2 * half, feature)

    metas = [meta, meta_far]
    dy_rows = exchange(pick(metas, [d_mixed, d_far], True))

    gate_matrix, up_matrix, down_matrix = w_gate[0], w_up[0], w_down[0]
    hidden_units = gate_matrix.shape[1]

    gate_pre = jnp.dot(x_rows, gate_matrix, preferred_element_type=F32)
    up_pre = jnp.dot(x_rows, up_matrix, preferred_element_type=F32)
    sig_gate = jax.nn.sigmoid(gate_pre)
    silu_gate = gate_pre * sig_gate
    hidden = (silu_gate * up_pre).astype(BF16)
    expert_out = jnp.dot(hidden, down_matrix, preferred_element_type=F32).astype(BF16)
    expert_out, dy_rows = after(expert_out, dy_rows)
    y_back = exchange(expert_out)

    n_rows = 2 * half
    expert_dx, terms = pl.pallas_call(
        backward_kernel,
        out_shape=[shape((n_rows, feature), BF16), shape((3 * hidden_units, feature), BF16)],
        in_specs=[VMEM] * 8,
        out_specs=[VMEM] * 2,
        scratch_shapes=[pltpu.VMEM((n_rows, hidden_units), BF16)] * 2,
        compiler_params=pltpu.CompilerParams(vmem_limit_bytes=48 * 1024 * 1024),
        cost_estimate=pl.CostEstimate(flops=1, bytes_accessed=1, transcendentals=0),
    )(dy_rows, x_rows, gate_pre, up_pre, hidden, gate_matrix.T, up_matrix.T, down_matrix)
    summed = lax.psum_scatter(terms, "dp", scatter_dimension=1, tiled=True)

    mixed_own, mixed_far, grads_own, grads_far = local_call(
        functools.partial(mix_kernel, top, side, capacity, 2),
        [
            shape((tok, feature), F32),
            shape((tok, feature), BF16),
            shape((tok, LANES), F32),
            shape((tok, LANES), F32),
        ],
        me_arr,
        [*metas, d_mixed, d_far, y_back],
        4 * top * half * 2 * tok * feature,
    )
    dx_own, dx_far = split(expert_dx)
    dx_far, y_back = after(dx_far, y_back)
    far_back = exchange(dx_far)
    far_back, dx_own = after(far_back, dx_own)
    own_back = exchange(dx_own)

    def total(metas, back, kind):
        return local_call(
            functools.partial(sum_kernel, top, side, capacity, 1),
            [shape((tok, feature), kind)],
            me_arr,
            [*metas, back],
            2 * half * tok * feature,
        )[0]

    tokens_far = across(total([meta_far], far_back, BF16))
    mixed_far, grads_far, own_back = after(across(mixed_far), across(grads_far), own_back)
    mixed = (mixed_own + mixed_far.astype(F32)).astype(BF16)
    d_gate = (grads_own + grads_far)[:, :top]
    tokens_own = total([meta], own_back, F32)
    d_tokens = (tokens_own + tokens_far.astype(F32)).astype(BF16)
    return (
        mixed,
        d_tokens,
        d_gate,
        summed[:hidden_units].astype(F32).T[None],
        summed[hidden_units : 2 * hidden_units].astype(F32).T[None],
        summed[2 * hidden_units :].astype(F32)[None],
    )


def solution(mesh):
    in_specs = (
        P(("dp", "expert"), None),
        P(("dp", "expert"), None),
        P(("dp", "expert"), None),
        P("expert", None, None),
        P("expert", None, None),
        P("expert", None, None),
        P(("dp", "expert"), None),
    )
    out_specs = (
        P(("dp", "expert"), None),
        P(("dp", "expert"), None),
        P(("dp", "expert"), None),
        P("expert", "dp", None),
        P("expert", "dp", None),
        P("expert", None, "dp"),
    )
    return jax.shard_map(
        on_device, mesh=mesh, in_specs=in_specs, out_specs=out_specs, check_vma=False
    )
```

```python
import functools

import jax
import jax.numpy as jnp
from jax import lax
from jax.experimental import pallas as pl
from jax.experimental.pallas import tpu as pltpu
from jax.sharding import PartitionSpec as P

BF16 = jnp.bfloat16
F32 = jnp.float32
LANES = 128
STRIP = 512
VMEM = pl.BlockSpec(memory_space=pltpu.VMEM)
SMEM = pl.BlockSpec(memory_space=pltpu.SMEM)


def local_call(kernel, outs, me, args, flops):
    size = sum(x.size * x.dtype.itemsize for x in (*outs, *args))
    return pl.pallas_call(
        kernel,
        out_shape=outs,
        in_specs=[SMEM] + [VMEM] * len(args),
        out_specs=[VMEM] * len(outs),
        compiler_params=pltpu.CompilerParams(vmem_limit_bytes=16 * 1024 * 1024),
        cost_estimate=pl.CostEstimate(flops=flops, bytes_accessed=size, transcendentals=0),
    )(me, *args)


def strips(width, step=STRIP):
    return [(c, min(c + step, width)) for c in range(0, width, step)]


def slot_tables(me, metas, top, side, capacity):
    count = len(metas)
    span = count * capacity
    tok = metas[0].shape[1]
    slot = lax.broadcasted_iota(jnp.int32, (side * span, tok), 0)
    expert = ((me - lax.rem(me, side)) + slot // span).astype(F32)
    block_of = lax.rem(slot, span) // capacity
    place = lax.rem(slot, capacity).astype(F32)
    row = lax.broadcasted_iota(jnp.int32, (tok, tok), 0)
    column = lax.broadcasted_iota(jnp.int32, (tok, tok), 1)
    earlier = jnp.where(row < column, 1.0, 0.0).astype(BF16)
    tables = []
    for b in range(count):
        named = [jnp.where(metas[b][k : k + 1, :] == expert, 1.0, 0.0) for k in range(top)]
        member = functools.reduce(lambda p, q: p + q, named)
        rank = jnp.dot(member.astype(BF16), earlier, preferred_element_type=F32)
        here = rank == place
        if count > 1:
            here = here & (block_of == b)
        tables.append([jnp.where(here, part, 0.0) for part in named])
    return tables


def pick_kernel(top, side, capacity, count, scaled, me_ref, *refs):
    metas, blocks, out = refs[:count], refs[count : 2 * count], refs[2 * count]
    tables = slot_tables(me_ref[0], metas, top, side, capacity)
    held = jnp.concatenate([functools.reduce(lambda p, q: p + q, ks) for ks in tables], 1)
    held = held.astype(BF16)
    if scaled:
        gate = 0.0
        for meta, ks in zip(metas, tables):
            for k, part in enumerate(ks):
                gate += jnp.sum(part * meta[top + k : top + k + 1, :], 1, keepdims=True)
    for c, e in strips(out.shape[1]):
        block = jnp.concatenate([ref[:, c:e] for ref in blocks], 0)
        got = jnp.dot(held, block, preferred_element_type=F32)
        out[:, c:e] = ((gate * got) if scaled else got).astype(BF16)


TRANSPOSED = (((0,), (0,)), ((), ()))


def sum_kernel(top, side, capacity, me_ref, meta, back, *refs):
    (table,) = slot_tables(me_ref[0], [meta], top, side, capacity)
    held = functools.reduce(lambda p, q: p + q, table).astype(BF16)
    out = refs[-1]
    for c, e in strips(out.shape[1]):
        got = lax.dot_general(held, back[:, c:e], TRANSPOSED, preferred_element_type=F32)
        for other in refs[:-1]:
            got += other[:, c:e].astype(F32)
        out[:, c:e] = got.astype(BF16)


def mix_kernel(top, side, capacity, count, me_ref, *refs):
    metas, blocks, back = refs[:count], refs[count : 2 * count], refs[2 * count]
    outs, grads = refs[2 * count + 1 : 3 * count + 1], refs[3 * count + 1 :]
    tables = slot_tables(me_ref[0], metas, top, side, capacity)
    tok = metas[0].shape[1]
    lane = lax.broadcasted_iota(jnp.int32, (tok, LANES), 1)
    for b in range(count):
        held = [part.astype(BF16) for part in tables[b]]
        gates = [metas[b][top + k : top + k + 1, :] for k in range(top)]
        gates = [jnp.transpose(jnp.broadcast_to(g, (8, tok)))[:, :1] for g in gates]
        sums = [jnp.zeros((tok, 1), F32) for _ in range(top)]
        for c, e in strips(outs[b].shape[1]):
            cotangent = blocks[b][:, c:e].astype(F32)
            mixed = 0.0
            for k in range(top):
                got = lax.dot_general(held[k], back[:, c:e], TRANSPOSED, preferred_element_type=F32)
                mixed += gates[k] * got
                sums[k] += jnp.sum(cotangent * got, 1, keepdims=True)
            outs[b][:, c:e] = mixed.astype(outs[b].dtype)
        grad = jnp.zeros((tok, LANES), F32)
        for k in range(top):
            grad = jnp.where(lane == k, sums[k], grad)
        grads[b][...] = grad


def backward_kernel(
    side, dy_ref, x_ref, gate_ref, up_ref, hidden_ref, wg_ref, wu_ref, wd_ref, own_ref, far_ref, terms_ref, gg_ref, gu_ref
):
    units, feature = gate_ref.shape[1], x_ref.shape[1]
    across_last = (((1,), (1,)), ((), ()))
    for c, e in strips(units, 256):
        back = lax.dot_general(
            dy_ref[...], wd_ref[c:e, :], across_last, preferred_element_type=F32
        )
        gate = gate_ref[:, c:e]
        sig = 1.0 / (1.0 + jnp.exp(-gate))
        gg_ref[:, c:e] = (back * up_ref[:, c:e] * (sig * (1.0 + gate * (1.0 - sig)))).astype(BF16)
        gu_ref[:, c:e] = (back * (gate * sig)).astype(BF16)
    for c, e in strips(feature):
        got = jnp.dot(gg_ref[...], wg_ref[:, c:e], preferred_element_type=F32)
        got += jnp.dot(gu_ref[...], wu_ref[:, c:e], preferred_element_type=F32)
        blocks = got.reshape(side, 2, own_ref.shape[0] // side, e - c)
        for b, out in enumerate((own_ref, far_ref)):
            out[:, c:e] = blocks[:, b].reshape(out.shape[0], e - c).astype(BF16)
    pairs = ((gg_ref, x_ref), (gu_ref, x_ref), (hidden_ref, dy_ref))
    for n, (left, right) in enumerate(pairs):
        for r, t in strips(units, 256):
            for c, e in strips(feature, 1024):
                terms_ref[n * units + r : n * units + t, c:e] = lax.dot_general(
                    left[:, r:t], right[:, c:e], TRANSPOSED, preferred_element_type=F32
                ).astype(BF16)


def on_device(tokens, expert_ids, gate_prob, w_gate, w_up, w_down, d_mixed):
    tok, feature = tokens.shape
    top = expert_ids.shape[1]
    experts = lax.axis_size("expert")
    capacity = max(2, 2 * tok * top // experts)
    side = experts // 2
    half = side * capacity
    me = lax.axis_index("expert")
    me_arr = me[None]
    sets = [[h * side + p for p in range(side)] for h in range(2)]
    shape = jax.ShapeDtypeStruct

    def across(value):
        return lax.ppermute(value, "expert", [(e, (e + side) % experts) for e in range(experts)])

    def exchange(value):
        shaped = value.reshape(side, value.shape[0] // side, value.shape[1])
        got = lax.all_to_all(shaped, "expert", 0, 0, axis_index_groups=sets, tiled=True)
        return got.reshape(value.shape)

    def after(value, *earlier):
        return lax.optimization_barrier((value, *earlier))

    def pick(metas, blocks, scaled):
        count = len(metas)
        return local_call(
            functools.partial(pick_kernel, top, side, capacity, count, scaled),
            [shape((count * half, feature), BF16)],
            me_arr,
            [*metas, *blocks],
            2 * count * count * half * tok * feature,
        )[0]

    meta = jnp.concatenate([expert_ids.T.astype(F32), gate_prob.T], 0)
    x_far = across(tokens)
    meta_far = across(meta)
    x_own = exchange(pick([meta], [tokens], False))
    x_far, meta_far = after(x_far, meta_far)
    d_mixed, x_far = after(d_mixed, x_far)
    d_far = across(d_mixed)
    x_other = exchange(pick([meta_far], [x_far], False))
    x_rows = jnp.stack(
        [part.reshape(side, capacity, feature) for part in (x_own, x_other)], 1
    ).reshape(2 * half, feature)

    metas = [meta, meta_far]
    dy_rows = exchange(pick(metas, [d_mixed, d_far], True))

    gate_matrix, up_matrix, down_matrix = w_gate[0], w_up[0], w_down[0]
    hidden_units = gate_matrix.shape[1]

    gate_pre = jnp.dot(x_rows, gate_matrix, preferred_element_type=F32)
    up_pre = jnp.dot(x_rows, up_matrix, preferred_element_type=F32)
    sig_gate = jax.nn.sigmoid(gate_pre)
    silu_gate = gate_pre * sig_gate
    hidden = (silu_gate * up_pre).astype(BF16)
    expert_out = jnp.dot(hidden, down_matrix, preferred_element_type=F32).astype(BF16)
    expert_out, dy_rows = after(expert_out, dy_rows)
    y_back = exchange(expert_out)

    n_rows = 2 * half
    dx_own, dx_far, terms = pl.pallas_call(
        functools.partial(backward_kernel, side),
        out_shape=[
            shape((half, feature), BF16),
            shape((half, feature), BF16),
            shape((3 * hidden_units, feature), BF16),
        ],
        in_specs=[VMEM] * 8,
        out_specs=[VMEM] * 3,
        scratch_shapes=[pltpu.VMEM((n_rows, hidden_units), BF16)] * 2,
        compiler_params=pltpu.CompilerParams(vmem_limit_bytes=48 * 1024 * 1024),
        cost_estimate=pl.CostEstimate(flops=1, bytes_accessed=1, transcendentals=0),
    )(dy_rows, x_rows, gate_pre, up_pre, hidden, gate_matrix.T, up_matrix.T, down_matrix)
    dx_far, dx_own, terms, y_back = after(dx_far, dx_own, terms, y_back)
    summed = lax.psum_scatter(terms, "dp", scatter_dimension=1, tiled=True)

    mixed_own, mixed_far, grads_own, grads_far = local_call(
        functools.partial(mix_kernel, top, side, capacity, 2),
        [
            shape((tok, feature), F32),
            shape((tok, feature), BF16),
            shape((tok, LANES), F32),
            shape((tok, LANES), F32),
        ],
        me_arr,
        [*metas, d_mixed, d_far, y_back],
        4 * top * half * 2 * tok * feature,
    )
    far_back = exchange(dx_far)
    far_back, dx_own = after(far_back, dx_own)
    own_back = exchange(dx_own)

    def total(meta, back, *other):
        return local_call(
            functools.partial(sum_kernel, top, side, capacity),
            [shape((tok, feature), BF16)],
            me_arr,
            [meta, back, *other],
            2 * half * tok * feature,
        )[0]

    tokens_far, mixed_far, grads_far = after(
        total(meta_far, far_back), across(mixed_far), across(grads_far)
    )
    tokens_far = across(tokens_far)
    mixed = (mixed_own + mixed_far.astype(F32)).astype(BF16)
    d_gate = (grads_own + grads_far)[:, :top]
    d_tokens = total(meta, own_back, tokens_far)
    return (
        mixed,
        d_tokens,
        d_gate,
        summed[:hidden_units].astype(F32).T[None],
        summed[hidden_units : 2 * hidden_units].astype(F32).T[None],
        summed[2 * hidden_units :].astype(F32)[None],
    )


def solution(mesh):
    in_specs = (
        P(("dp", "expert"), None),
        P(("dp", "expert"), None),
        P(("dp", "expert"), None),
        P("expert", None, None),
        P("expert", None, None),
        P("expert", None, None),
        P(("dp", "expert"), None),
    )
    out_specs = (
        P(("dp", "expert"), None),
        P(("dp", "expert"), None),
        P(("dp", "expert"), None),
        P("expert", "dp", None),
        P("expert", "dp", None),
        P("expert", None, "dp"),
    )
    return jax.shard_map(
        on_device, mesh=mesh, in_specs=in_specs, out_specs=out_specs, check_vma=False
    )
```

```python
import functools

import jax
import jax.numpy as jnp
from jax import lax
from jax.experimental import pallas as pl
from jax.experimental.pallas import tpu as pltpu
from jax.sharding import PartitionSpec as P

BF16 = jnp.bfloat16
F32 = jnp.float32
LANES = 128
STRIP = 512
VMEM = pl.BlockSpec(memory_space=pltpu.VMEM)
SMEM = pl.BlockSpec(memory_space=pltpu.SMEM)


def local_call(kernel, outs, me, args, flops):
    size = sum(x.size * x.dtype.itemsize for x in (*outs, *args))
    return pl.pallas_call(
        kernel,
        out_shape=outs,
        in_specs=[SMEM] + [VMEM] * len(args),
        out_specs=[VMEM] * len(outs),
        compiler_params=pltpu.CompilerParams(vmem_limit_bytes=16 * 1024 * 1024),
        cost_estimate=pl.CostEstimate(flops=flops, bytes_accessed=size, transcendentals=0),
    )(me, *args)


def strips(width, step=STRIP):
    return [(c, min(c + step, width)) for c in range(0, width, step)]


def slot_tables(me, metas, top, side, capacity):
    count = len(metas)
    span = count * capacity
    tok = metas[0].shape[1]
    slot = lax.broadcasted_iota(jnp.int32, (side * span, tok), 0)
    expert = ((me - lax.rem(me, side)) + slot // span).astype(F32)
    block_of = lax.rem(slot, span) // capacity
    place = lax.rem(slot, capacity).astype(F32)
    row = lax.broadcasted_iota(jnp.int32, (tok, tok), 0)
    column = lax.broadcasted_iota(jnp.int32, (tok, tok), 1)
    earlier = jnp.where(row < column, 1.0, 0.0).astype(BF16)
    tables = []
    for b in range(count):
        named = [jnp.where(metas[b][k : k + 1, :] == expert, 1.0, 0.0) for k in range(top)]
        member = functools.reduce(lambda p, q: p + q, named)
        rank = jnp.dot(member.astype(BF16), earlier, preferred_element_type=F32)
        here = rank == place
        if count > 1:
            here = here & (block_of == b)
        tables.append([jnp.where(here, part, 0.0) for part in named])
    return tables


def pick_kernel(top, side, capacity, scaled, me_ref, *refs):
    count = len(scaled)
    metas, blocks, out = refs[:count], refs[count : 2 * count], refs[2 * count]
    tables = slot_tables(me_ref[0], metas, top, side, capacity)
    held = jnp.concatenate([functools.reduce(lambda p, q: p + q, ks) for ks in tables], 1)
    held = held.astype(BF16)
    gate = 0.0
    for meta, ks, has in zip(metas, tables, scaled):
        for k, part in enumerate(ks):
            if has:
                part = part * meta[top + k : top + k + 1, :]
            gate += jnp.sum(part, 1, keepdims=True)
    for c, e in strips(out.shape[1]):
        block = jnp.concatenate([ref[:, c:e] for ref in blocks], 0)
        got = jnp.dot(held, block, preferred_element_type=F32)
        out[:, c:e] = ((gate * got) if any(scaled) else got).astype(BF16)


TRANSPOSED = (((0,), (0,)), ((), ()))


def picked_sum(table, back, c, e):
    return lax.dot_general(
        table.astype(BF16), back[:, c:e], TRANSPOSED, preferred_element_type=F32
    )


def sum_kernel(top, side, capacity, me_ref, meta, back, out):
    (table,) = slot_tables(me_ref[0], [meta], top, side, capacity)
    held = functools.reduce(lambda p, q: p + q, table)
    for c, e in strips(out.shape[1]):
        out[:, c:e] = picked_sum(held, back, c, e).astype(BF16)


def mix(top, table, meta, block, back, out, grads, far=None, far_grads=None):
    tok = meta.shape[1]
    gates = [meta[top + k : top + k + 1, :] for k in range(top)]
    gates = [jnp.transpose(jnp.broadcast_to(g, (8, tok)))[:, :1] for g in gates]
    sums = [jnp.zeros((tok, 1), F32) for _ in range(top)]
    for c, e in strips(out.shape[1]):
        cotangent = block[:, c:e].astype(F32)
        mixed = 0.0 if far is None else far[:, c:e].astype(F32)
        for k in range(top):
            got = picked_sum(table[k], back, c, e)
            mixed += gates[k] * got
            sums[k] += jnp.sum(cotangent * got, 1, keepdims=True)
        out[:, c:e] = mixed.astype(BF16)
    lane = lax.broadcasted_iota(jnp.int32, (tok, LANES), 1)
    grad = jnp.zeros((tok, LANES), F32) if far_grads is None else far_grads[...]
    for k in range(top):
        grad += jnp.where(lane == k, sums[k], 0.0)
    grads[...] = grad


def mix_kernel(top, side, capacity, me_ref, meta, block, back, out, grads):
    (table,) = slot_tables(me_ref[0], [meta], top, side, capacity)
    mix(top, table, meta, block, back, out, grads)


def last_kernel(
    top, side, capacity, me_ref, meta, block, back, far, far_grads, far_dx, out, grads, dx
):
    tables = slot_tables(me_ref[0], [meta, meta], top, side, capacity)
    mix(top, tables[0], meta, block, back, out, grads, far, far_grads)
    held = functools.reduce(lambda p, q: p + q, tables[1])
    for c, e in strips(dx.shape[1]):
        dx[:, c:e] = (picked_sum(held, back, c, e) + far_dx[:, c:e].astype(F32)).astype(BF16)


def backward_kernel(
    dy_ref, x_ref, gate_ref, up_ref, hidden_ref, wg_ref, wu_ref, wd_ref, own_ref, far_ref, terms_ref, gg_ref, gu_ref
):
    units, feature = gate_ref.shape[1], x_ref.shape[1]
    across_last = (((1,), (1,)), ((), ()))
    for c, e in strips(units, 256):
        back = lax.dot_general(
            dy_ref[...], wd_ref[c:e, :], across_last, preferred_element_type=F32
        )
        gate = gate_ref[:, c:e]
        sig = 1.0 / (1.0 + jnp.exp(-gate))
        gg_ref[:, c:e] = (back * up_ref[:, c:e] * (sig * (1.0 + gate * (1.0 - sig)))).astype(BF16)
        gu_ref[:, c:e] = (back * (gate * sig)).astype(BF16)
    for c, e in strips(feature):
        got = jnp.dot(gg_ref[...], wg_ref[:, c:e], preferred_element_type=F32)
        got += jnp.dot(gu_ref[...], wu_ref[:, c:e], preferred_element_type=F32)
        own_ref[:, c:e] = got[: own_ref.shape[0]].astype(BF16)
        far_ref[:, c:e] = got[own_ref.shape[0] :].astype(BF16)
    pairs = ((gg_ref, x_ref), (gu_ref, x_ref), (hidden_ref, dy_ref))
    for n, (left, right) in enumerate(pairs):
        for r, t in strips(units, 256):
            for c, e in strips(feature, 1024):
                terms_ref[n * units + r : n * units + t, c:e] = lax.dot_general(
                    left[:, r:t], right[:, c:e], TRANSPOSED, preferred_element_type=F32
                ).astype(BF16)


def on_device(tokens, expert_ids, gate_prob, w_gate, w_up, w_down, d_mixed):
    tok, feature = tokens.shape
    top = expert_ids.shape[1]
    experts = lax.axis_size("expert")
    capacity = max(2, 2 * tok * top // experts)
    side = experts // 2
    half = side * capacity
    me = lax.axis_index("expert")
    me_arr = me[None]
    sets = [[h * side + p for p in range(side)] for h in range(2)]
    shape = jax.ShapeDtypeStruct

    def across(value):
        return lax.ppermute(value, "expert", [(e, (e + side) % experts) for e in range(experts)])

    def exchange(value):
        shaped = value.reshape(side, value.shape[0] // side, value.shape[1])
        got = lax.all_to_all(shaped, "expert", 0, 0, axis_index_groups=sets, tiled=True)
        return got.reshape(value.shape)

    def after(value, *earlier):
        return lax.optimization_barrier((value, *earlier))

    def call(kernel, outs, args, flops):
        return local_call(
            functools.partial(kernel, top, side, capacity),
            [shape(*out) for out in outs],
            me_arr,
            args,
            flops,
        )

    def pick(metas, blocks, scaled):
        count = len(metas)
        return local_call(
            functools.partial(pick_kernel, top, side, capacity, scaled),
            [shape((count * half, feature), BF16)],
            me_arr,
            [*metas, *blocks],
            2 * count * count * half * tok * feature,
        )[0]

    meta = jnp.concatenate([expert_ids.T.astype(F32), gate_prob.T], 0)
    own = exchange(pick([meta, meta], [tokens, d_mixed], (False, True)))
    own = own.reshape(side, 2, capacity, feature)
    x_far, meta_far = after(across(tokens), across(meta))
    d_late, x_far = after(d_mixed, x_far)
    d_far = across(d_late)
    far_rows = exchange(pick([meta_far], [x_far], (False,)))
    x_rows = jnp.concatenate([own[:, 0].reshape(half, feature), far_rows], 0)
    far_rows, d_far = after(far_rows, d_far)
    d_far_rows = exchange(pick([meta_far], [d_far], (True,)))

    gate_matrix, up_matrix, down_matrix = w_gate[0], w_up[0], w_down[0]
    hidden_units = gate_matrix.shape[1]
    gate_pre = jnp.dot(x_rows, gate_matrix, preferred_element_type=F32)
    up_pre = jnp.dot(x_rows, up_matrix, preferred_element_type=F32)
    hidden = (gate_pre * jax.nn.sigmoid(gate_pre) * up_pre).astype(BF16)
    y_far, y_own = (
        jnp.dot(part, down_matrix, preferred_element_type=F32).astype(BF16)
        for part in (hidden[half:], hidden[:half])
    )
    y_far, y_own, d_far_rows = after(y_far, y_own, d_far_rows)
    y_far_back = exchange(y_far)
    dy_rows = jnp.concatenate([own[:, 1].reshape(half, feature), d_far_rows], 0)

    dx_own, dx_far, terms = pl.pallas_call(
        backward_kernel,
        out_shape=[
            shape((half, feature), BF16),
            shape((half, feature), BF16),
            shape((3 * hidden_units, feature), BF16),
        ],
        in_specs=[VMEM] * 8,
        out_specs=[VMEM] * 3,
        scratch_shapes=[pltpu.VMEM((2 * half, hidden_units), BF16)] * 2,
        compiler_params=pltpu.CompilerParams(vmem_limit_bytes=48 * 1024 * 1024),
        cost_estimate=pl.CostEstimate(flops=1, bytes_accessed=1, transcendentals=0),
    )(dy_rows, x_rows, gate_pre, up_pre, hidden, gate_matrix.T, up_matrix.T, down_matrix)
    dx_far, dx_own, terms, y_far_back = after(dx_far, dx_own, terms, y_far_back)
    summed = lax.psum_scatter(terms, "dp", scatter_dimension=1, tiled=True)

    token_rows, grad_rows = ((tok, feature), BF16), ((tok, LANES), F32)
    work = 2 * half * tok * feature
    mixed_far, grads_far = call(
        mix_kernel, [token_rows, grad_rows], [meta_far, d_far, y_far_back], top * work
    )
    dx_far, mixed_far, grads_far = after(dx_far, mixed_far, grads_far)
    far_back = exchange(dx_far)
    both = jnp.stack([part.reshape(side, capacity, feature) for part in (y_own, dx_own)], 1)
    far_back, both = after(far_back, both)
    own_back = exchange(both.reshape(2 * half, feature))

    (tokens_far,) = call(sum_kernel, [token_rows], [meta_far, far_back], work)
    tokens_far, mixed_far, grads_far = after(tokens_far, across(mixed_far), across(grads_far))
    weight_grads = (
        summed[:hidden_units].astype(F32).T[None],
        summed[hidden_units : 2 * hidden_units].astype(F32).T[None],
        summed[2 * hidden_units :].astype(F32)[None],
    )
    own_back, *weight_grads = after(own_back, *weight_grads)
    mixed, grads, d_tokens = call(
        last_kernel,
        [token_rows, grad_rows, token_rows],
        [meta, d_mixed, own_back, mixed_far, grads_far, across(tokens_far)],
        (top + 1) * 2 * work,
    )
    return (mixed, d_tokens, grads[:, :top], *weight_grads)


def solution(mesh):
    in_specs = (
        P(("dp", "expert"), None),
        P(("dp", "expert"), None),
        P(("dp", "expert"), None),
        P("expert", None, None),
        P("expert", None, None),
        P("expert", None, None),
        P(("dp", "expert"), None),
    )
    out_specs = (
        P(("dp", "expert"), None),
        P(("dp", "expert"), None),
        P(("dp", "expert"), None),
        P("expert", "dp", None),
        P("expert", "dp", None),
        P("expert", None, "dp"),
    )
    return jax.shard_map(
        on_device, mesh=mesh, in_specs=in_specs, out_specs=out_specs, check_vma=False
    )
```

```python
import functools

import jax
import jax.numpy as jnp
from jax import lax
from jax.experimental import pallas as pl
from jax.experimental.pallas import tpu as pltpu
from jax.sharding import PartitionSpec as P

BF16 = jnp.bfloat16
F32 = jnp.float32
LANES = 128
STRIP = 512
VMEM = pl.BlockSpec(memory_space=pltpu.VMEM)
SMEM = pl.BlockSpec(memory_space=pltpu.SMEM)


def local_call(kernel, outs, me, args, flops):
    size = sum(x.size * x.dtype.itemsize for x in (*outs, *args))
    return pl.pallas_call(
        kernel,
        out_shape=outs,
        in_specs=[SMEM] + [VMEM] * len(args),
        out_specs=[VMEM] * len(outs),
        compiler_params=pltpu.CompilerParams(vmem_limit_bytes=16 * 1024 * 1024),
        cost_estimate=pl.CostEstimate(flops=flops, bytes_accessed=size, transcendentals=0),
    )(me, *args)


def strips(width, step=STRIP):
    return [(c, min(c + step, width)) for c in range(0, width, step)]


def slot_tables(me, metas, top, side, capacity):
    count = len(metas)
    span = count * capacity
    tok = metas[0].shape[1]
    slot = lax.broadcasted_iota(jnp.int32, (side * span, tok), 0)
    expert = ((me - lax.rem(me, side)) + slot // span).astype(F32)
    block_of = lax.rem(slot, span) // capacity
    place = lax.rem(slot, capacity).astype(F32)
    row = lax.broadcasted_iota(jnp.int32, (tok, tok), 0)
    column = lax.broadcasted_iota(jnp.int32, (tok, tok), 1)
    earlier = jnp.where(row < column, 1.0, 0.0).astype(BF16)
    tables = []
    for b in range(count):
        named = [jnp.where(metas[b][k : k + 1, :] == expert, 1.0, 0.0) for k in range(top)]
        member = functools.reduce(lambda p, q: p + q, named)
        rank = jnp.dot(member.astype(BF16), earlier, preferred_element_type=F32)
        here = rank == place
        if count > 1:
            here = here & (block_of == b)
        tables.append([jnp.where(here, part, 0.0) for part in named])
    return tables


def pick_kernel(top, side, capacity, scaled, me_ref, *refs):
    count = len(scaled)
    metas, blocks, out = refs[:count], refs[count : 2 * count], refs[2 * count]
    tables = slot_tables(me_ref[0], metas, top, side, capacity)
    held = jnp.concatenate([functools.reduce(lambda p, q: p + q, ks) for ks in tables], 1)
    held = held.astype(BF16)
    gate = 0.0
    for meta, ks, has in zip(metas, tables, scaled):
        for k, part in enumerate(ks):
            if has:
                part = part * meta[top + k : top + k + 1, :]
            gate += jnp.sum(part, 1, keepdims=True)
    for c, e in strips(out.shape[1]):
        block = jnp.concatenate([ref[:, c:e] for ref in blocks], 0)
        got = jnp.dot(held, block, preferred_element_type=F32)
        out[:, c:e] = ((gate * got) if any(scaled) else got).astype(BF16)


TRANSPOSED = (((0,), (0,)), ((), ()))


def picked_sum(table, back, c, e):
    return lax.dot_general(
        table.astype(BF16), back[:, c:e], TRANSPOSED, preferred_element_type=F32
    )


def sum_kernel(top, side, capacity, me_ref, meta, back, out):
    (table,) = slot_tables(me_ref[0], [meta], top, side, capacity)
    held = functools.reduce(lambda p, q: p + q, table)
    for c, e in strips(out.shape[1]):
        out[:, c:e] = picked_sum(held, back, c, e).astype(BF16)


def mix(top, table, meta, block, back, out, grads, far=None, far_grads=None):
    tok = meta.shape[1]
    gates = [meta[top + k : top + k + 1, :] for k in range(top)]
    gates = [jnp.transpose(jnp.broadcast_to(g, (8, tok)))[:, :1] for g in gates]
    sums = [jnp.zeros((tok, 1), F32) for _ in range(top)]
    for c, e in strips(out.shape[1]):
        cotangent = block[:, c:e].astype(F32)
        mixed = 0.0 if far is None else far[:, c:e].astype(F32)
        for k in range(top):
            got = picked_sum(table[k], back, c, e)
            mixed += gates[k] * got
            sums[k] += jnp.sum(cotangent * got, 1, keepdims=True)
        out[:, c:e] = mixed.astype(BF16)
    lane = lax.broadcasted_iota(jnp.int32, (tok, LANES), 1)
    grad = jnp.zeros((tok, LANES), F32) if far_grads is None else far_grads[...]
    for k in range(top):
        grad += jnp.where(lane == k, sums[k], 0.0)
    grads[...] = grad


def mix_kernel(top, side, capacity, me_ref, meta, block, back, out, grads):
    (table,) = slot_tables(me_ref[0], [meta], top, side, capacity)
    mix(top, table, meta, block, back, out, grads)


def last_kernel(
    top, side, capacity, me_ref, meta, block, back, far, far_grads, far_dx, out, grads, dx
):
    tables = slot_tables(me_ref[0], [meta, meta], top, side, capacity)
    mix(top, tables[0], meta, block, back, out, grads, far, far_grads)
    held = functools.reduce(lambda p, q: p + q, tables[1])
    for c, e in strips(dx.shape[1]):
        dx[:, c:e] = (picked_sum(held, back, c, e) + far_dx[:, c:e].astype(F32)).astype(BF16)


def dx_kernel(
    side, d_own, d_far, gate_ref, up_ref, y_own, wg_ref, wu_ref, wd_ref, both, far, gg_ref, gu_ref
):
    half, feature = far.shape
    units = gate_ref.shape[1]
    across_last = (((1,), (1,)), ((), ()))
    for r, d_rows in ((0, d_own), (half, d_far)):
        at = slice(r, r + half)
        for c, e in strips(units, 256):
            back = lax.dot_general(
                d_rows[...], wd_ref[c:e, :], across_last, preferred_element_type=F32
            )
            gate = gate_ref[at, c:e]
            sig = 1.0 / (1.0 + jnp.exp(-gate))
            gg_ref[at, c:e] = (
                back * up_ref[at, c:e] * (sig * (1.0 + gate * (1.0 - sig)))
            ).astype(BF16)
            gu_ref[at, c:e] = (back * (gate * sig)).astype(BF16)
    for c, e in strips(feature):
        got = jnp.dot(gg_ref[...], wg_ref[:, c:e], preferred_element_type=F32)
        got += jnp.dot(gu_ref[...], wu_ref[:, c:e], preferred_element_type=F32)
        far[:, c:e] = got[half:].astype(BF16)
        pair = [
            part.reshape(side, 1, half // side, e - c)
            for part in (y_own[:, c:e].astype(F32), got[:half])
        ]
        both[:, c:e] = jnp.concatenate(pair, 1).reshape(2 * half, e - c).astype(BF16)


def terms_kernel(gg, gu, hidden, x_own, x_far, d_own, d_far, out):
    half, feature = x_own.shape
    units = gg.shape[1]
    pairs = ((gg, x_own, x_far), (gu, x_own, x_far), (hidden, d_own, d_far))
    for n, (left, own, far) in enumerate(pairs):
        for r, t in strips(units, 256):
            for c, e in strips(feature, 1024):
                got = lax.dot_general(
                    left[:half, r:t], own[:, c:e], TRANSPOSED, preferred_element_type=F32
                )
                got += lax.dot_general(
                    left[half:, r:t], far[:, c:e], TRANSPOSED, preferred_element_type=F32
                )
                out[n * units + r : n * units + t, c:e] = got.astype(BF16)


def on_device(tokens, expert_ids, gate_prob, w_gate, w_up, w_down, d_mixed):
    tok, feature = tokens.shape
    top = expert_ids.shape[1]
    experts = lax.axis_size("expert")
    capacity = max(2, 2 * tok * top // experts)
    side = experts // 2
    half = side * capacity
    me = lax.axis_index("expert")
    me_arr = me[None]
    sets = [[h * side + p for p in range(side)] for h in range(2)]
    shape = jax.ShapeDtypeStruct

    def across(value):
        return lax.ppermute(value, "expert", [(e, (e + side) % experts) for e in range(experts)])

    def exchange(value):
        shaped = value.reshape(side, value.shape[0] // side, value.shape[1])
        got = lax.all_to_all(shaped, "expert", 0, 0, axis_index_groups=sets, tiled=True)
        return got.reshape(value.shape)

    def after(value, *earlier):
        return lax.optimization_barrier((value, *earlier))

    def call(kernel, outs, args, flops):
        return local_call(
            functools.partial(kernel, top, side, capacity),
            [shape(*out) for out in outs],
            me_arr,
            args,
            flops,
        )

    def pick(metas, blocks, scaled):
        count = len(metas)
        return local_call(
            functools.partial(pick_kernel, top, side, capacity, scaled),
            [shape((count * half, feature), BF16)],
            me_arr,
            [*metas, *blocks],
            2 * count * count * half * tok * feature,
        )[0]

    meta = jnp.concatenate([expert_ids.T.astype(F32), gate_prob.T], 0)
    own = exchange(pick([meta, meta], [tokens, d_mixed], (False, True)))
    own = own.reshape(side, 2, capacity, feature)
    x_far, meta_far = after(across(tokens), across(meta))
    d_late, x_far = after(d_mixed, x_far)
    d_far = across(d_late)
    x_far, own = after(x_far, own)
    x_own, d_own = (own[:, n].reshape(half, feature) for n in range(2))
    x_far_rows = exchange(pick([meta_far], [x_far], (False,)))
    x_rows = jnp.concatenate([x_own, x_far_rows], 0)
    x_far_rows, d_far = after(x_far_rows, d_far)
    d_far_rows = exchange(pick([meta_far], [d_far], (True,)))

    gate_matrix, up_matrix, down_matrix = w_gate[0], w_up[0], w_down[0]
    hidden_units = gate_matrix.shape[1]
    gate_pre = jnp.dot(x_rows, gate_matrix, preferred_element_type=F32)
    up_pre = jnp.dot(x_rows, up_matrix, preferred_element_type=F32)
    hidden = (gate_pre * jax.nn.sigmoid(gate_pre) * up_pre).astype(BF16)
    y_far, y_own = (
        jnp.dot(part, down_matrix, preferred_element_type=F32).astype(BF16)
        for part in (hidden[half:], hidden[:half])
    )
    y_far, y_own, d_far_rows = after(y_far, y_own, d_far_rows)
    y_far_back = exchange(y_far)

    n_rows = 2 * half
    rows, units = shape((half, feature), BF16), shape((n_rows, hidden_units), BF16)
    both, dx_far, gg, gu = pl.pallas_call(
        functools.partial(dx_kernel, side),
        out_shape=[shape((n_rows, feature), BF16), rows, units, units],
        in_specs=[VMEM] * 8,
        out_specs=[VMEM] * 4,
        compiler_params=pltpu.CompilerParams(vmem_limit_bytes=32 * 1024 * 1024),
        cost_estimate=pl.CostEstimate(flops=1, bytes_accessed=1, transcendentals=0),
    )(d_own, d_far_rows, gate_pre, up_pre, y_own, gate_matrix.T, up_matrix.T, down_matrix)
    (terms,) = pl.pallas_call(
        terms_kernel,
        out_shape=[shape((3 * hidden_units, feature), BF16)],
        in_specs=[VMEM] * 7,
        out_specs=[VMEM],
        compiler_params=pltpu.CompilerParams(vmem_limit_bytes=32 * 1024 * 1024),
        cost_estimate=pl.CostEstimate(flops=1, bytes_accessed=1, transcendentals=0),
    )(gg, gu, hidden, x_own, x_far_rows, d_own, d_far_rows)
    dx_far, both, terms, y_far_back = after(dx_far, both, terms, y_far_back)

    token_rows, grad_rows = ((tok, feature), BF16), ((tok, LANES), F32)
    work = 2 * half * tok * feature
    mixed_far, grads_far = call(
        mix_kernel, [token_rows, grad_rows], [meta_far, d_far, y_far_back], top * work
    )
    dx_far, mixed_far, grads_far = after(dx_far, mixed_far, grads_far)
    far_back = exchange(dx_far)
    (tokens_far,) = call(sum_kernel, [token_rows], [meta_far, far_back], work)
    summed = lax.psum_scatter(terms, "dp", scatter_dimension=1, tiled=True)
    tokens_far, both, mixed_far, grads_far = after(
        tokens_far, both, across(mixed_far), across(grads_far)
    )
    own_back = exchange(both)
    weight_grads = (
        summed[:hidden_units].astype(F32).T[None],
        summed[hidden_units : 2 * hidden_units].astype(F32).T[None],
        summed[2 * hidden_units :].astype(F32)[None],
    )
    own_back, *weight_grads = after(own_back, *weight_grads)
    mixed, grads, d_tokens = call(
        last_kernel,
        [token_rows, grad_rows, token_rows],
        [meta, d_mixed, own_back, mixed_far, grads_far, across(tokens_far)],
        (top + 1) * 2 * work,
    )
    return (mixed, d_tokens, grads[:, :top], *weight_grads)


def solution(mesh):
    in_specs = (
        P(("dp", "expert"), None),
        P(("dp", "expert"), None),
        P(("dp", "expert"), None),
        P("expert", None, None),
        P("expert", None, None),
        P("expert", None, None),
        P(("dp", "expert"), None),
    )
    out_specs = (
        P(("dp", "expert"), None),
        P(("dp", "expert"), None),
        P(("dp", "expert"), None),
        P("expert", "dp", None),
        P("expert", "dp", None),
        P("expert", None, "dp"),
    )
    return jax.shard_map(
        on_device, mesh=mesh, in_specs=in_specs, out_specs=out_specs, check_vma=False
    )
```

```python
import functools

import jax
import jax.numpy as jnp
from jax import lax
from jax.experimental import pallas as pl
from jax.experimental.pallas import tpu as pltpu
from jax.sharding import PartitionSpec as P

BF16 = jnp.bfloat16
F32 = jnp.float32
LANES = 128
STRIP = 512
VMEM = pl.BlockSpec(memory_space=pltpu.VMEM)
SMEM = pl.BlockSpec(memory_space=pltpu.SMEM)


def local_call(kernel, outs, me, args, flops):
    size = sum(x.size * x.dtype.itemsize for x in (*outs, *args))
    return pl.pallas_call(
        kernel,
        out_shape=outs,
        in_specs=[SMEM] + [VMEM] * len(args),
        out_specs=[VMEM] * len(outs),
        compiler_params=pltpu.CompilerParams(vmem_limit_bytes=6 * 1024 * 1024),
        cost_estimate=pl.CostEstimate(flops=flops, bytes_accessed=size, transcendentals=0),
    )(me, *args)


def strips(width, step=STRIP):
    return [(c, min(c + step, width)) for c in range(0, width, step)]


def slot_tables(me, metas, top, side, capacity):
    count = len(metas)
    span = count * capacity
    tok = metas[0].shape[1]
    slot = lax.broadcasted_iota(jnp.int32, (side * span, tok), 0)
    expert = ((me - lax.rem(me, side)) + slot // span).astype(F32)
    block_of = lax.rem(slot, span) // capacity
    place = lax.rem(slot, capacity).astype(F32)
    row = lax.broadcasted_iota(jnp.int32, (tok, tok), 0)
    column = lax.broadcasted_iota(jnp.int32, (tok, tok), 1)
    earlier = jnp.where(row < column, 1.0, 0.0).astype(BF16)
    tables = []
    for b in range(count):
        named = [jnp.where(metas[b][k : k + 1, :] == expert, 1.0, 0.0) for k in range(top)]
        member = functools.reduce(lambda p, q: p + q, named)
        rank = jnp.dot(member.astype(BF16), earlier, preferred_element_type=F32)
        here = rank == place
        if count > 1:
            here = here & (block_of == b)
        tables.append([jnp.where(here, part, 0.0) for part in named])
    return tables


def pick_kernel(top, side, capacity, scaled, me_ref, *refs):
    count = len(scaled)
    metas, blocks, out = refs[:count], refs[count : 2 * count], refs[2 * count]
    tables = slot_tables(me_ref[0], metas, top, side, capacity)
    held = jnp.concatenate([functools.reduce(lambda p, q: p + q, ks) for ks in tables], 1)
    held = held.astype(BF16)
    gate = 0.0
    for meta, ks, has in zip(metas, tables, scaled):
        for k, part in enumerate(ks):
            if has:
                part = part * meta[top + k : top + k + 1, :]
            gate += jnp.sum(part, 1, keepdims=True)
    for c, e in strips(out.shape[1]):
        block = jnp.concatenate([ref[:, c:e] for ref in blocks], 0)
        got = jnp.dot(held, block, preferred_element_type=F32)
        out[:, c:e] = ((gate * got) if any(scaled) else got).astype(BF16)


TRANSPOSED = (((0,), (0,)), ((), ()))


def picked_sum(table, back, c, e):
    return lax.dot_general(
        table.astype(BF16), back[:, c:e], TRANSPOSED, preferred_element_type=F32
    )


def sum_kernel(top, side, capacity, me_ref, meta, back, out):
    (table,) = slot_tables(me_ref[0], [meta], top, side, capacity)
    held = functools.reduce(lambda p, q: p + q, table)
    for c, e in strips(out.shape[1]):
        out[:, c:e] = picked_sum(held, back, c, e).astype(BF16)


def mix(top, table, meta, block, back, out, grads, far=None, far_grads=None):
    tok = meta.shape[1]
    gates = [meta[top + k : top + k + 1, :] for k in range(top)]
    gates = [jnp.transpose(jnp.broadcast_to(g, (8, tok)))[:, :1] for g in gates]
    sums = [jnp.zeros((tok, 1), F32) for _ in range(top)]
    for c, e in strips(out.shape[1]):
        cotangent = block[:, c:e].astype(F32)
        mixed = 0.0 if far is None else far[:, c:e].astype(F32)
        for k in range(top):
            got = picked_sum(table[k], back, c, e)
            mixed += gates[k] * got
            sums[k] += jnp.sum(cotangent * got, 1, keepdims=True)
        out[:, c:e] = mixed.astype(BF16)
    lane = lax.broadcasted_iota(jnp.int32, (tok, LANES), 1)
    grad = jnp.zeros((tok, LANES), F32) if far_grads is None else far_grads[...]
    for k in range(top):
        grad += jnp.where(lane == k, sums[k], 0.0)
    grads[...] = grad


def mix_kernel(top, side, capacity, me_ref, meta, block, back, out, grads):
    (table,) = slot_tables(me_ref[0], [meta], top, side, capacity)
    mix(top, table, meta, block, back, out, grads)


def last_kernel(
    top, side, capacity, me_ref, meta, block, back, far, far_grads, far_dx, out, grads, dx
):
    tables = slot_tables(me_ref[0], [meta, meta], top, side, capacity)
    mix(top, tables[0], meta, block, back, out, grads, far, far_grads)
    held = functools.reduce(lambda p, q: p + q, tables[1])
    for c, e in strips(dx.shape[1]):
        dx[:, c:e] = (picked_sum(held, back, c, e) + far_dx[:, c:e].astype(F32)).astype(BF16)


def dx_kernel(
    side, d_own, d_far, gate_ref, up_ref, y_own, wg_ref, wu_ref, wd_ref, both, far, gg_ref, gu_ref
):
    half, feature = far.shape
    units = gate_ref.shape[1]
    across_last = (((1,), (1,)), ((), ()))
    for r, d_rows in ((0, d_own), (half, d_far)):
        at = slice(r, r + half)
        for c, e in strips(units, 256):
            back = lax.dot_general(
                d_rows[...], wd_ref[c:e, :], across_last, preferred_element_type=F32
            )
            gate = gate_ref[at, c:e]
            sig = 1.0 / (1.0 + jnp.exp(-gate))
            gg_ref[at, c:e] = (
                back * up_ref[at, c:e] * (sig * (1.0 + gate * (1.0 - sig)))
            ).astype(BF16)
            gu_ref[at, c:e] = (back * (gate * sig)).astype(BF16)
    for c, e in strips(feature):
        got = jnp.dot(gg_ref[...], wg_ref[:, c:e], preferred_element_type=F32)
        got += jnp.dot(gu_ref[...], wu_ref[:, c:e], preferred_element_type=F32)
        far[:, c:e] = got[half:].astype(BF16)
        pair = [
            part.reshape(side, 1, half // side, e - c)
            for part in (y_own[:, c:e].astype(F32), got[:half])
        ]
        both[:, c:e] = jnp.concatenate(pair, 1).reshape(2 * half, e - c).astype(BF16)


def terms_kernel(gg, gu, hidden, x_own, x_far, d_own, d_far, out, tiles, sems):
    half, feature = x_own.shape
    units = gg.shape[1]
    pairs = ((gg, x_own, x_far), (gu, x_own, x_far), (hidden, d_own, d_far))
    steps = [(n, r, t) for n in range(3) for r, t in strips(units, tiles.shape[1])]
    copies = []
    for step, (n, r, t) in enumerate(steps):
        left, own, far = pairs[n]
        slot = step % 2
        if step > 1:
            copies[step - 2].wait()
        for c, e in strips(feature, 1024):
            got = lax.dot_general(
                left[:half, r:t], own[:, c:e], TRANSPOSED, preferred_element_type=F32
            )
            got += lax.dot_general(
                left[half:, r:t], far[:, c:e], TRANSPOSED, preferred_element_type=F32
            )
            tiles[slot, : t - r, c:e] = got.astype(BF16)
        copy = pltpu.make_async_copy(
            tiles.at[slot, pl.ds(0, t - r)],
            out.at[pl.ds(n * units + r, t - r)],
            sems.at[slot],
        )
        copy.start()
        copies.append(copy)
    for copy in copies[-2:]:
        copy.wait()


def on_device(tokens, expert_ids, gate_prob, w_gate, w_up, w_down, d_mixed):
    tok, feature = tokens.shape
    top = expert_ids.shape[1]
    experts = lax.axis_size("expert")
    capacity = max(2, 2 * tok * top // experts)
    side = experts // 2
    half = side * capacity
    me = lax.axis_index("expert")
    me_arr = me[None]
    sets = [[h * side + p for p in range(side)] for h in range(2)]
    shape = jax.ShapeDtypeStruct

    def across(value):
        return lax.ppermute(value, "expert", [(e, (e + side) % experts) for e in range(experts)])

    def exchange(value):
        shaped = value.reshape(side, value.shape[0] // side, value.shape[1])
        got = lax.all_to_all(shaped, "expert", 0, 0, axis_index_groups=sets, tiled=True)
        return got.reshape(value.shape)

    def after(value, *earlier):
        return lax.optimization_barrier((value, *earlier))

    def call(kernel, outs, args, flops):
        return local_call(
            functools.partial(kernel, top, side, capacity),
            [shape(*out) for out in outs],
            me_arr,
            args,
            flops,
        )

    def pick(metas, blocks, scaled):
        count = len(metas)
        return local_call(
            functools.partial(pick_kernel, top, side, capacity, scaled),
            [shape((count * half, feature), BF16)],
            me_arr,
            [*metas, *blocks],
            2 * count * count * half * tok * feature,
        )[0]

    meta = jnp.concatenate([expert_ids.T.astype(F32), gate_prob.T], 0)
    own = exchange(pick([meta, meta], [tokens, d_mixed], (False, True)))
    own = own.reshape(side, 2, capacity, feature)
    x_far, meta_far = after(across(tokens), across(meta))
    x_far, d_far, own = after(x_far, across(d_mixed), own)
    x_own, d_own = (own[:, n].reshape(half, feature) for n in range(2))
    x_far_rows = exchange(pick([meta_far], [x_far], (False,)))
    x_rows = jnp.concatenate([x_own, x_far_rows], 0)
    x_far_rows, d_far = after(x_far_rows, d_far)
    d_far_rows = exchange(pick([meta_far], [d_far], (True,)))

    gate_matrix, up_matrix, down_matrix = w_gate[0], w_up[0], w_down[0]
    hidden_units = gate_matrix.shape[1]
    gate_pre = jnp.dot(x_rows, gate_matrix, preferred_element_type=F32)
    up_pre = jnp.dot(x_rows, up_matrix, preferred_element_type=F32)
    hidden = (gate_pre * jax.nn.sigmoid(gate_pre) * up_pre).astype(BF16)
    y_far, y_own = (
        jnp.dot(part, down_matrix, preferred_element_type=F32).astype(BF16)
        for part in (hidden[half:], hidden[:half])
    )
    y_far, y_own, d_far_rows = after(y_far, y_own, d_far_rows)
    y_far_back = exchange(y_far)

    n_rows = 2 * half
    rows, units = shape((half, feature), BF16), shape((n_rows, hidden_units), BF16)
    both, dx_far, gg, gu = pl.pallas_call(
        functools.partial(dx_kernel, side),
        out_shape=[shape((n_rows, feature), BF16), rows, units, units],
        in_specs=[VMEM] * 8,
        out_specs=[VMEM] * 4,
        compiler_params=pltpu.CompilerParams(vmem_limit_bytes=10 * 1024 * 1024),
        cost_estimate=pl.CostEstimate(flops=1, bytes_accessed=1, transcendentals=0),
    )(d_own, d_far_rows, gate_pre, up_pre, y_own, gate_matrix.T, up_matrix.T, down_matrix)
    (terms,) = pl.pallas_call(
        terms_kernel,
        out_shape=[shape((3 * hidden_units, feature), BF16)],
        in_specs=[VMEM] * 7,
        out_specs=[pl.BlockSpec(memory_space=pltpu.HBM)],
        scratch_shapes=[pltpu.VMEM((2, 256, feature), BF16), pltpu.SemaphoreType.DMA((2,))],
        compiler_params=pltpu.CompilerParams(vmem_limit_bytes=10 * 1024 * 1024),
        cost_estimate=pl.CostEstimate(flops=1, bytes_accessed=1, transcendentals=0),
    )(gg, gu, hidden, x_own, x_far_rows, d_own, d_far_rows)
    dx_far, both, terms, y_far_back = after(dx_far, both, terms, y_far_back)

    token_rows, grad_rows = ((tok, feature), BF16), ((tok, LANES), F32)
    work = 2 * half * tok * feature
    mixed_far, grads_far = call(
        mix_kernel, [token_rows, grad_rows], [meta_far, d_far, y_far_back], top * work
    )
    dx_far, mixed_far, grads_far = after(dx_far, mixed_far, grads_far)
    far_back = exchange(dx_far)
    (tokens_far,) = call(sum_kernel, [token_rows], [meta_far, far_back], work)
    summed = lax.psum_scatter(terms, "dp", scatter_dimension=1, tiled=True)
    tokens_far, both, mixed_far, grads_far = after(
        tokens_far, both, across(mixed_far), across(grads_far)
    )
    own_back = exchange(both)
    weight_grads = (
        summed[:hidden_units].astype(F32).T[None],
        summed[hidden_units : 2 * hidden_units].astype(F32).T[None],
        summed[2 * hidden_units :].astype(F32)[None],
    )
    own_back, *weight_grads = after(own_back, *weight_grads)
    mixed, grads, d_tokens = call(
        last_kernel,
        [token_rows, grad_rows, token_rows],
        [meta, d_mixed, own_back, mixed_far, grads_far, across(tokens_far)],
        (top + 1) * 2 * work,
    )
    return (mixed, d_tokens, grads[:, :top], *weight_grads)


def solution(mesh):
    in_specs = (
        P(("dp", "expert"), None),
        P(("dp", "expert"), None),
        P(("dp", "expert"), None),
        P("expert", None, None),
        P("expert", None, None),
        P("expert", None, None),
        P(("dp", "expert"), None),
    )
    out_specs = (
        P(("dp", "expert"), None),
        P(("dp", "expert"), None),
        P(("dp", "expert"), None),
        P("expert", "dp", None),
        P("expert", "dp", None),
        P("expert", None, "dp"),
    )
    return jax.shard_map(
        on_device, mesh=mesh, in_specs=in_specs, out_specs=out_specs, check_vma=False
    )
```

```python
import functools

import jax
import jax.numpy as jnp
from jax import lax
from jax.experimental import pallas as pl
from jax.experimental.pallas import tpu as pltpu
from jax.sharding import PartitionSpec as P

BF16 = jnp.bfloat16
F32 = jnp.float32
LANES = 128
STRIP = 512
VMEM = pl.BlockSpec(memory_space=pltpu.VMEM)
SMEM = pl.BlockSpec(memory_space=pltpu.SMEM)


def local_call(kernel, outs, me, args, flops):
    size = sum(x.size * x.dtype.itemsize for x in (*outs, *args))
    return pl.pallas_call(
        kernel,
        out_shape=outs,
        in_specs=[SMEM] + [VMEM] * len(args),
        out_specs=[VMEM] * len(outs),
        compiler_params=pltpu.CompilerParams(vmem_limit_bytes=6 * 1024 * 1024),
        cost_estimate=pl.CostEstimate(flops=flops, bytes_accessed=size, transcendentals=0),
    )(me, *args)


def strips(width, step=STRIP):
    return [(c, min(c + step, width)) for c in range(0, width, step)]


def slot_tables(me, metas, top, side, capacity):
    count = len(metas)
    span = count * capacity
    tok = metas[0].shape[1]
    slot = lax.broadcasted_iota(jnp.int32, (side * span, tok), 0)
    expert = ((me - lax.rem(me, side)) + slot // span).astype(F32)
    block_of = lax.rem(slot, span) // capacity
    place = lax.rem(slot, capacity).astype(F32)
    row = lax.broadcasted_iota(jnp.int32, (tok, tok), 0)
    column = lax.broadcasted_iota(jnp.int32, (tok, tok), 1)
    earlier = jnp.where(row < column, 1.0, 0.0).astype(BF16)
    tables = []
    for b in range(count):
        named = [jnp.where(metas[b][k : k + 1, :] == expert, 1.0, 0.0) for k in range(top)]
        member = functools.reduce(lambda p, q: p + q, named)
        rank = jnp.dot(member.astype(BF16), earlier, preferred_element_type=F32)
        here = rank == place
        if count > 1:
            here = here & (block_of == b)
        tables.append([jnp.where(here, part, 0.0) for part in named])
    return tables


def pick_kernel(top, side, capacity, scaled, me_ref, *refs):
    count = len(scaled)
    metas, blocks, out = refs[:count], refs[count : 2 * count], refs[2 * count]
    tables = slot_tables(me_ref[0], metas, top, side, capacity)
    held = jnp.concatenate([functools.reduce(lambda p, q: p + q, ks) for ks in tables], 1)
    held = held.astype(BF16)
    gate = 0.0
    for meta, ks, has in zip(metas, tables, scaled):
        for k, part in enumerate(ks):
            if has:
                part = part * meta[top + k : top + k + 1, :]
            gate += jnp.sum(part, 1, keepdims=True)
    for c, e in strips(out.shape[1]):
        block = jnp.concatenate([ref[:, c:e] for ref in blocks], 0)
        got = jnp.dot(held, block, preferred_element_type=F32)
        out[:, c:e] = ((gate * got) if any(scaled) else got).astype(BF16)


TRANSPOSED = (((0,), (0,)), ((), ()))


def picked_sum(table, back, c, e):
    return lax.dot_general(
        table.astype(BF16), back[:, c:e], TRANSPOSED, preferred_element_type=F32
    )


def sum_kernel(top, side, capacity, me_ref, meta, back, out):
    (table,) = slot_tables(me_ref[0], [meta], top, side, capacity)
    held = functools.reduce(lambda p, q: p + q, table)
    for c, e in strips(out.shape[1]):
        out[:, c:e] = picked_sum(held, back, c, e).astype(BF16)


def mix(top, table, meta, block, back, out, grads, far=None, far_grads=None):
    tok = meta.shape[1]
    gates = [meta[top + k : top + k + 1, :] for k in range(top)]
    gates = [jnp.transpose(jnp.broadcast_to(g, (8, tok)))[:, :1] for g in gates]
    sums = [jnp.zeros((tok, 1), F32) for _ in range(top)]
    for c, e in strips(out.shape[1]):
        cotangent = block[:, c:e].astype(F32)
        mixed = 0.0 if far is None else far[:, c:e].astype(F32)
        for k in range(top):
            got = picked_sum(table[k], back, c, e)
            mixed += gates[k] * got
            sums[k] += jnp.sum(cotangent * got, 1, keepdims=True)
        out[:, c:e] = mixed.astype(BF16)
    lane = lax.broadcasted_iota(jnp.int32, (tok, LANES), 1)
    grad = jnp.zeros((tok, LANES), F32) if far_grads is None else far_grads[...]
    for k in range(top):
        grad += jnp.where(lane == k, sums[k], 0.0)
    grads[...] = grad


def mix_kernel(top, side, capacity, me_ref, meta, block, back, out, grads):
    (table,) = slot_tables(me_ref[0], [meta], top, side, capacity)
    mix(top, table, meta, block, back, out, grads)


def sum_last_kernel(top, side, capacity, me_ref, meta, back, far, out):
    (table,) = slot_tables(me_ref[0], [meta], top, side, capacity)
    held = functools.reduce(lambda p, q: p + q, table)
    for c, e in strips(out.shape[1]):
        out[:, c:e] = (picked_sum(held, back, c, e) + far[:, c:e].astype(F32)).astype(BF16)


def mix_last_kernel(
    top, side, capacity, me_ref, meta, block, back, far, far_grads, out, grads
):
    (table,) = slot_tables(me_ref[0], [meta], top, side, capacity)
    mix(top, table, meta, block, back, out, grads, far, far_grads)


def fetch(sources, targets, sems):
    copies = []
    for n, (source, target) in enumerate(zip(sources, targets)):
        copies.append(pltpu.make_async_copy(source, target, sems.at[n]))
        copies[n].start()
    return copies


def dx_kernel(*refs):
    sources, (own_out, far_out, gg_ref, gu_ref) = refs[:7], refs[7:11]
    local, sems = refs[11:18], refs[18]
    wd, d_own, gate, up, d_far, wg, wu = local
    copies = fetch(sources, local, sems)
    half, feature = d_own.shape
    units = gate.shape[1]
    across_last = (((1,), (1,)), ((), ()))
    copies[0].wait()
    for r, d_rows, needed in ((0, d_own, (1, 2, 3)), (half, d_far, (4,))):
        at = slice(r, r + half)
        for n in needed:
            copies[n].wait()
        for c, e in strips(units, 256):
            back = lax.dot_general(
                d_rows[...], wd[c:e, :], across_last, preferred_element_type=F32
            )
            pre = gate[at, c:e]
            sig = 1.0 / (1.0 + jnp.exp(-pre))
            gg_ref[at, c:e] = (
                back * up[at, c:e] * (sig * (1.0 + pre * (1.0 - sig)))
            ).astype(BF16)
            gu_ref[at, c:e] = (back * (pre * sig)).astype(BF16)
    copies[5].wait()
    copies[6].wait()
    for c, e in strips(feature):
        got = jnp.dot(gg_ref[...], wg[:, c:e], preferred_element_type=F32)
        got += jnp.dot(gu_ref[...], wu[:, c:e], preferred_element_type=F32)
        own_out[:, c:e] = got[:half].astype(BF16)
        far_out[:, c:e] = got[half:].astype(BF16)


def terms_kernel(*refs):
    sources, out, local = refs[:7], refs[7], refs[8:15]
    sems, tiles, tile_sems = refs[15:]
    x_own, x_far, gg, gu, d_own, d_far, hidden = local
    loads = fetch(sources, local, sems)
    half, feature = x_own.shape
    units = gg.shape[1]
    pairs = (
        (gg, x_own, x_far, (0, 1, 2)),
        (gu, x_own, x_far, (3,)),
        (hidden, d_own, d_far, (4, 5, 6)),
    )
    copies = []
    for n, (left, own, far, needed) in enumerate(pairs):
        for m in needed:
            loads[m].wait()
        for r, t in strips(units, tiles.shape[1]):
            slot = len(copies) % 2
            if len(copies) > 1:
                copies[-2].wait()
            for c, e in strips(feature, 1024):
                got = lax.dot_general(
                    left[:half, r:t], own[:, c:e], TRANSPOSED, preferred_element_type=F32
                )
                got += lax.dot_general(
                    left[half:, r:t], far[:, c:e], TRANSPOSED, preferred_element_type=F32
                )
                tiles[slot, : t - r, c:e] = got.astype(BF16)
            copy = pltpu.make_async_copy(
                tiles.at[slot, pl.ds(0, t - r)],
                out.at[pl.ds(n * units + r, t - r)],
                tile_sems.at[slot],
            )
            copy.start()
            copies.append(copy)
    for copy in copies[-2:]:
        copy.wait()


def streamed_call(kernel, outs, args, out_space, scratch, limit):
    return pl.pallas_call(
        kernel,
        out_shape=outs,
        in_specs=[pl.BlockSpec(memory_space=pl.ANY)] * len(args),
        out_specs=[pl.BlockSpec(memory_space=out_space)] * len(outs),
        scratch_shapes=[
            *[pltpu.VMEM(x.shape, x.dtype) for x in args],
            pltpu.SemaphoreType.DMA((len(args),)),
            *scratch,
        ],
        compiler_params=pltpu.CompilerParams(vmem_limit_bytes=limit * 1024 * 1024),
        cost_estimate=pl.CostEstimate(flops=1, bytes_accessed=1, transcendentals=0),
    )(*args)


def on_device(tokens, expert_ids, gate_prob, w_gate, w_up, w_down, d_mixed):
    tok, feature = tokens.shape
    top = expert_ids.shape[1]
    experts = lax.axis_size("expert")
    capacity = max(2, 2 * tok * top // experts)
    side = experts // 2
    half = side * capacity
    me = lax.axis_index("expert")
    me_arr = me[None]
    sets = [[h * side + p for p in range(side)] for h in range(2)]
    shape = jax.ShapeDtypeStruct

    def across(value):
        return lax.ppermute(value, "expert", [(e, (e + side) % experts) for e in range(experts)])

    def exchange(value):
        shaped = value.reshape(side, value.shape[0] // side, value.shape[1])
        got = lax.all_to_all(shaped, "expert", 0, 0, axis_index_groups=sets, tiled=True)
        return got.reshape(value.shape)

    def after(value, *earlier):
        return lax.optimization_barrier((value, *earlier))

    def call(kernel, outs, args, flops):
        return local_call(
            functools.partial(kernel, top, side, capacity),
            [shape(*out) for out in outs],
            me_arr,
            args,
            flops,
        )

    def pick(metas, blocks, scaled):
        count = len(metas)
        return local_call(
            functools.partial(pick_kernel, top, side, capacity, scaled),
            [shape((count * half, feature), BF16)],
            me_arr,
            [*metas, *blocks],
            2 * count * count * half * tok * feature,
        )[0]

    meta = jnp.concatenate([expert_ids.T.astype(F32), gate_prob.T], 0)
    own = exchange(pick([meta, meta], [tokens, d_mixed], (False, True)))
    own = own.reshape(side, 2, capacity, feature)
    x_far, meta_far = after(across(tokens), across(meta))
    x_far, d_far, own = after(x_far, across(d_mixed), own)
    x_own, d_own = (own[:, n].reshape(half, feature) for n in range(2))
    x_far_rows = exchange(pick([meta_far], [x_far], (False,)))
    x_rows = jnp.concatenate([x_own, x_far_rows], 0)
    d_picked, x_own, d_own, _ = after(
        pick([meta_far], [d_far], (True,)), x_own, d_own, x_far_rows
    )
    d_far_rows = exchange(d_picked)

    gate_matrix, up_matrix, down_matrix = w_gate[0], w_up[0], w_down[0]
    hidden_units = gate_matrix.shape[1]
    gate_pre = jnp.dot(x_rows, gate_matrix, preferred_element_type=F32)
    up_pre = jnp.dot(x_rows, up_matrix, preferred_element_type=F32)
    hidden = (gate_pre * jax.nn.sigmoid(gate_pre) * up_pre).astype(BF16)
    y_far, y_own = (
        jnp.dot(part, down_matrix, preferred_element_type=F32).astype(BF16)
        for part in (hidden[half:], hidden[:half])
    )
    y_far, y_own, d_far_rows = after(y_far, y_own, d_far_rows)
    y_far_back = exchange(y_far)

    rows, units = shape((half, feature), BF16), shape((2 * half, hidden_units), BF16)
    dx_own, dx_far, gg, gu = streamed_call(
        dx_kernel,
        [rows, rows, units, units],
        [down_matrix, d_own, gate_pre, up_pre, d_far_rows, gate_matrix.T, up_matrix.T],
        pltpu.VMEM,
        [],
        24,
    )
    dx_own, dx_far, gg, gu, y_far_back = after(dx_own, dx_far, gg, gu, y_far_back)

    token_rows, grad_rows = ((tok, feature), BF16), ((tok, LANES), F32)
    work = 2 * half * tok * feature
    mixed_far, grads_far = call(
        mix_kernel, [token_rows, grad_rows], [meta_far, d_far, y_far_back], top * work
    )
    y_own, gg, gu, mixed_far, grads_far = after(y_own, gg, gu, mixed_far, grads_far)
    y_own_back = exchange(y_own)
    (terms,) = streamed_call(
        terms_kernel,
        [shape((3 * hidden_units, feature), BF16)],
        [x_own, x_far_rows, gg, gu, d_own, d_far_rows, hidden],
        pltpu.HBM,
        [pltpu.VMEM((2, 256, feature), BF16), pltpu.SemaphoreType.DMA((2,))],
        16,
    )
    dx_far, dx_own, terms, y_own_back, mixed_far, grads_far = after(
        dx_far, dx_own, terms, y_own_back, across(mixed_far), across(grads_far)
    )
    summed = lax.psum_scatter(terms, "dp", scatter_dimension=1, tiled=True)
    dx_far_back = exchange(dx_far)
    (tokens_far,) = call(sum_kernel, [token_rows], [meta_far, dx_far_back], work)
    tokens_far, dx_own = after(tokens_far, dx_own)
    dx_own_back = exchange(dx_own)
    mixed, grads = call(
        mix_last_kernel,
        [token_rows, grad_rows],
        [meta, d_mixed, y_own_back, mixed_far, grads_far],
        top * work,
    )
    weight_grads = (
        summed[:hidden_units].astype(F32).T[None],
        summed[hidden_units : 2 * hidden_units].astype(F32).T[None],
        summed[2 * hidden_units :].astype(F32)[None],
    )
    dx_own_back, mixed, grads, *weight_grads = after(dx_own_back, mixed, grads, *weight_grads)
    (d_tokens,) = call(
        sum_last_kernel, [token_rows], [meta, dx_own_back, across(tokens_far)], work
    )
    return (mixed, d_tokens, grads[:, :top], *weight_grads)


def solution(mesh):
    in_specs = (
        P(("dp", "expert"), None),
        P(("dp", "expert"), None),
        P(("dp", "expert"), None),
        P("expert", None, None),
        P("expert", None, None),
        P("expert", None, None),
        P(("dp", "expert"), None),
    )
    out_specs = (
        P(("dp", "expert"), None),
        P(("dp", "expert"), None),
        P(("dp", "expert"), None),
        P("expert", "dp", None),
        P("expert", "dp", None),
        P("expert", None, "dp"),
    )
    return jax.shard_map(
        on_device, mesh=mesh, in_specs=in_specs, out_specs=out_specs, check_vma=False
    )
```

```python
import functools

import jax
import jax.numpy as jnp
from jax import lax
from jax.experimental import pallas as pl
from jax.experimental.pallas import tpu as pltpu
from jax.sharding import PartitionSpec as P

BF16 = jnp.bfloat16
F32 = jnp.float32
LANES = 128
STRIP = 512
VMEM = pl.BlockSpec(memory_space=pltpu.VMEM)
SMEM = pl.BlockSpec(memory_space=pltpu.SMEM)


def local_call(kernel, outs, me, args, flops):
    size = sum(x.size * x.dtype.itemsize for x in (*outs, *args))
    return pl.pallas_call(
        kernel,
        out_shape=outs,
        in_specs=[SMEM] + [VMEM] * len(args),
        out_specs=[VMEM] * len(outs),
        compiler_params=pltpu.CompilerParams(vmem_limit_bytes=6 * 1024 * 1024),
        cost_estimate=pl.CostEstimate(flops=flops, bytes_accessed=size, transcendentals=0),
    )(me, *args)


def strips(width, step=STRIP):
    return [(c, min(c + step, width)) for c in range(0, width, step)]


def slot_tables(me, metas, top, side, capacity):
    count = len(metas)
    span = count * capacity
    tok = metas[0].shape[1]
    slot = lax.broadcasted_iota(jnp.int32, (side * span, tok), 0)
    expert = ((me - lax.rem(me, side)) + slot // span).astype(F32)
    block_of = lax.rem(slot, span) // capacity
    place = lax.rem(slot, capacity).astype(F32)
    row = lax.broadcasted_iota(jnp.int32, (tok, tok), 0)
    column = lax.broadcasted_iota(jnp.int32, (tok, tok), 1)
    earlier = jnp.where(row < column, 1.0, 0.0).astype(BF16)
    tables = []
    for b in range(count):
        named = [jnp.where(metas[b][k : k + 1, :] == expert, 1.0, 0.0) for k in range(top)]
        member = functools.reduce(lambda p, q: p + q, named)
        rank = jnp.dot(member.astype(BF16), earlier, preferred_element_type=F32)
        here = rank == place
        if count > 1:
            here = here & (block_of == b)
        tables.append([jnp.where(here, part, 0.0) for part in named])
    return tables


def pick_kernel(top, side, capacity, scaled, me_ref, *refs):
    count = len(scaled)
    metas, blocks, out = refs[:count], refs[count : 2 * count], refs[2 * count]
    tables = slot_tables(me_ref[0], metas, top, side, capacity)
    held = jnp.concatenate([functools.reduce(lambda p, q: p + q, ks) for ks in tables], 1)
    held = held.astype(BF16)
    gate = 0.0
    for meta, ks, has in zip(metas, tables, scaled):
        for k, part in enumerate(ks):
            if has:
                part = part * meta[top + k : top + k + 1, :]
            gate += jnp.sum(part, 1, keepdims=True)
    for c, e in strips(out.shape[1]):
        block = jnp.concatenate([ref[:, c:e] for ref in blocks], 0)
        got = jnp.dot(held, block, preferred_element_type=F32)
        out[:, c:e] = ((gate * got) if any(scaled) else got).astype(BF16)


TRANSPOSED = (((0,), (0,)), ((), ()))


def picked_sum(table, back, c, e):
    return lax.dot_general(
        table.astype(BF16), back[:, c:e], TRANSPOSED, preferred_element_type=F32
    )


def sum_kernel(top, side, capacity, me_ref, meta, back, out):
    (table,) = slot_tables(me_ref[0], [meta], top, side, capacity)
    held = functools.reduce(lambda p, q: p + q, table)
    for c, e in strips(out.shape[1]):
        out[:, c:e] = picked_sum(held, back, c, e).astype(BF16)


def mix(top, table, meta, block, back, out, grads, far=None, far_grads=None):
    tok = meta.shape[1]
    gates = [meta[top + k : top + k + 1, :] for k in range(top)]
    gates = [jnp.transpose(jnp.broadcast_to(g, (8, tok)))[:, :1] for g in gates]
    sums = [jnp.zeros((tok, 1), F32) for _ in range(top)]
    for c, e in strips(out.shape[1]):
        cotangent = block[:, c:e].astype(F32)
        mixed = 0.0 if far is None else far[:, c:e].astype(F32)
        for k in range(top):
            got = picked_sum(table[k], back, c, e)
            mixed += gates[k] * got
            sums[k] += jnp.sum(cotangent * got, 1, keepdims=True)
        out[:, c:e] = mixed.astype(BF16)
    lane = lax.broadcasted_iota(jnp.int32, (tok, LANES), 1)
    grad = jnp.zeros((tok, LANES), F32) if far_grads is None else far_grads[...]
    for k in range(top):
        grad += jnp.where(lane == k, sums[k], 0.0)
    grads[...] = grad


def mix_kernel(top, side, capacity, me_ref, meta, block, back, out, grads):
    (table,) = slot_tables(me_ref[0], [meta], top, side, capacity)
    mix(top, table, meta, block, back, out, grads)


def sum_last_kernel(top, side, capacity, me_ref, meta, back, far, out):
    (table,) = slot_tables(me_ref[0], [meta], top, side, capacity)
    held = functools.reduce(lambda p, q: p + q, table)
    for c, e in strips(out.shape[1]):
        out[:, c:e] = (picked_sum(held, back, c, e) + far[:, c:e].astype(F32)).astype(BF16)


def mix_last_kernel(
    top, side, capacity, me_ref, meta, block, back, far, far_grads, out, grads
):
    (table,) = slot_tables(me_ref[0], [meta], top, side, capacity)
    mix(top, table, meta, block, back, out, grads, far, far_grads)


def fetch(sources, targets, sems):
    copies = []
    for n, (source, target) in enumerate(zip(sources, targets)):
        copies.append(pltpu.make_async_copy(source, target, sems.at[n]))
        copies[n].start()
    return copies


def backward_kernel(*refs):
    sources, (own_out, far_out, terms_out), local = refs[:10], refs[10:13], refs[13:23]
    sems, gg, gu, dx, tiles, out_sems = refs[23:]
    wd, d_own, gate, up, d_far, wg, wu, x_own, x_far, hidden = local
    loads = fetch(sources, local, sems)
    half, feature = d_own.shape
    units = gate.shape[1]
    across_last = (((1,), (1,)), ((), ()))
    loads[0].wait()
    for r, d_rows, needed in ((0, d_own, (1, 2, 3)), (half, d_far, (4,))):
        at = slice(r, r + half)
        for n in needed:
            loads[n].wait()
        for c, e in strips(units, 256):
            back = lax.dot_general(
                d_rows[...], wd[c:e, :], across_last, preferred_element_type=F32
            )
            pre = gate[at, c:e]
            sig = 1.0 / (1.0 + jnp.exp(-pre))
            gg[at, c:e] = (back * up[at, c:e] * (sig * (1.0 + pre * (1.0 - sig)))).astype(BF16)
            gu[at, c:e] = (back * (pre * sig)).astype(BF16)
    loads[5].wait()
    loads[6].wait()
    for c, e in strips(feature):
        got = jnp.dot(gg[...], wg[:, c:e], preferred_element_type=F32)
        got += jnp.dot(gu[...], wu[:, c:e], preferred_element_type=F32)
        dx[:, c:e] = got.astype(BF16)
    dx_copies = [
        pltpu.make_async_copy(dx.at[pl.ds(half, half)], far_out, out_sems.at[2]),
        pltpu.make_async_copy(dx.at[pl.ds(0, half)], own_out, out_sems.at[3]),
    ]
    for copy in dx_copies:
        copy.start()
    pairs = ((gg, x_own, x_far, (7, 8)), (gu, x_own, x_far, ()), (hidden, d_own, d_far, (9,)))
    copies = []
    for n, (left, own, far, needed) in enumerate(pairs):
        for m in needed:
            loads[m].wait()
        for r, t in strips(units, tiles.shape[1]):
            slot = len(copies) % 2
            if len(copies) > 1:
                copies[-2].wait()
            for c, e in strips(feature, 1024):
                got = lax.dot_general(
                    left[:half, r:t], own[:, c:e], TRANSPOSED, preferred_element_type=F32
                )
                got += lax.dot_general(
                    left[half:, r:t], far[:, c:e], TRANSPOSED, preferred_element_type=F32
                )
                tiles[slot, : t - r, c:e] = got.astype(BF16)
            copy = pltpu.make_async_copy(
                tiles.at[slot, pl.ds(0, t - r)],
                terms_out.at[pl.ds(n * units + r, t - r)],
                out_sems.at[slot],
            )
            copy.start()
            copies.append(copy)
    for copy in (*copies[-2:], *dx_copies):
        copy.wait()


def backward(side_rows, args):
    half, feature = side_rows.shape
    units = args[0].shape[0]
    anywhere = pl.BlockSpec(memory_space=pltpu.HBM)
    return pl.pallas_call(
        backward_kernel,
        out_shape=[side_rows, side_rows, jax.ShapeDtypeStruct((3 * units, feature), BF16)],
        in_specs=[anywhere] * len(args),
        out_specs=[anywhere] * 3,
        scratch_shapes=[
            *[pltpu.VMEM(x.shape, x.dtype) for x in args],
            pltpu.SemaphoreType.DMA((len(args),)),
            pltpu.VMEM((2 * half, units), BF16),
            pltpu.VMEM((2 * half, units), BF16),
            pltpu.VMEM((2 * half, feature), BF16),
            pltpu.VMEM((2, 256, feature), BF16),
            pltpu.SemaphoreType.DMA((4,)),
        ],
        compiler_params=pltpu.CompilerParams(vmem_limit_bytes=60 * 1024 * 1024),
        cost_estimate=pl.CostEstimate(flops=1, bytes_accessed=1, transcendentals=0),
    )(*args)


def on_device(tokens, expert_ids, gate_prob, w_gate, w_up, w_down, d_mixed):
    tok, feature = tokens.shape
    top = expert_ids.shape[1]
    experts = lax.axis_size("expert")
    capacity = max(2, 2 * tok * top // experts)
    side = experts // 2
    half = side * capacity
    me = lax.axis_index("expert")
    me_arr = me[None]
    sets = [[h * side + p for p in range(side)] for h in range(2)]
    shape = jax.ShapeDtypeStruct

    def across(value):
        return lax.ppermute(value, "expert", [(e, (e + side) % experts) for e in range(experts)])

    def exchange(value):
        shaped = value.reshape(side, value.shape[0] // side, value.shape[1])
        got = lax.all_to_all(shaped, "expert", 0, 0, axis_index_groups=sets, tiled=True)
        return got.reshape(value.shape)

    def after(value, *earlier):
        return lax.optimization_barrier((value, *earlier))

    def call(kernel, outs, args, flops):
        return local_call(
            functools.partial(kernel, top, side, capacity),
            [shape(*out) for out in outs],
            me_arr,
            args,
            flops,
        )

    def pick(metas, blocks, scaled):
        count = len(metas)
        return local_call(
            functools.partial(pick_kernel, top, side, capacity, scaled),
            [shape((count * half, feature), BF16)],
            me_arr,
            [*metas, *blocks],
            2 * count * count * half * tok * feature,
        )[0]

    meta = jnp.concatenate([expert_ids.T.astype(F32), gate_prob.T], 0)
    own = exchange(pick([meta, meta], [tokens, d_mixed], (False, True)))
    own = own.reshape(side, 2, capacity, feature)
    x_far, meta_far = after(across(tokens), across(meta))
    x_far, d_far, own = after(x_far, across(d_mixed), own)
    x_own, d_own = (own[:, n].reshape(half, feature) for n in range(2))
    x_far_rows = exchange(pick([meta_far], [x_far], (False,)))
    x_rows = jnp.concatenate([x_own, x_far_rows], 0)
    d_picked, x_own, d_own, _ = after(
        pick([meta_far], [d_far], (True,)), x_own, d_own, x_far_rows
    )
    d_far_rows = exchange(d_picked)

    gate_matrix, up_matrix, down_matrix = w_gate[0], w_up[0], w_down[0]
    hidden_units = gate_matrix.shape[1]
    gate_pre = jnp.dot(x_rows, gate_matrix, preferred_element_type=F32)
    up_pre = jnp.dot(x_rows, up_matrix, preferred_element_type=F32)
    hidden = (gate_pre * jax.nn.sigmoid(gate_pre) * up_pre).astype(BF16)
    y_far, y_own = (
        jnp.dot(part, down_matrix, preferred_element_type=F32).astype(BF16)
        for part in (hidden[half:], hidden[:half])
    )
    y_far, y_own, d_far_rows = after(y_far, y_own, d_far_rows)
    y_far_back = exchange(y_far)

    dx_own, dx_far, terms = backward(
        shape((half, feature), BF16),
        [
            down_matrix,
            d_own,
            gate_pre,
            up_pre,
            d_far_rows,
            gate_matrix.T,
            up_matrix.T,
            x_own,
            x_far_rows,
            hidden,
        ],
    )
    dx_own, dx_far, terms, y_far_back = after(dx_own, dx_far, terms, y_far_back)
    summed = lax.psum_scatter(terms, "dp", scatter_dimension=1, tiled=True)

    token_rows, grad_rows = ((tok, feature), BF16), ((tok, LANES), F32)
    work = 2 * half * tok * feature
    mixed_far, grads_far = call(
        mix_kernel, [token_rows, grad_rows], [meta_far, d_far, y_far_back], top * work
    )
    dx_far, mixed_far, grads_far = after(dx_far, mixed_far, grads_far)
    dx_far_back = exchange(dx_far)
    (tokens_far,) = call(sum_kernel, [token_rows], [meta_far, dx_far_back], work)
    tokens_far, y_own, mixed_far, grads_far = after(
        tokens_far, y_own, across(mixed_far), across(grads_far)
    )
    y_own_back = exchange(y_own)
    y_own_back, dx_own = after(y_own_back, dx_own)
    dx_own_back = exchange(dx_own)
    mixed, grads = call(
        mix_last_kernel,
        [token_rows, grad_rows],
        [meta, d_mixed, y_own_back, mixed_far, grads_far],
        top * work,
    )
    weight_grads = (
        summed[:hidden_units].astype(F32).T[None],
        summed[hidden_units : 2 * hidden_units].astype(F32).T[None],
        summed[2 * hidden_units :].astype(F32)[None],
    )
    dx_own_back, mixed, grads, *weight_grads = after(dx_own_back, mixed, grads, *weight_grads)
    (d_tokens,) = call(
        sum_last_kernel, [token_rows], [meta, dx_own_back, across(tokens_far)], work
    )
    return (mixed, d_tokens, grads[:, :top], *weight_grads)


def solution(mesh):
    in_specs = (
        P(("dp", "expert"), None),
        P(("dp", "expert"), None),
        P(("dp", "expert"), None),
        P("expert", None, None),
        P("expert", None, None),
        P("expert", None, None),
        P(("dp", "expert"), None),
    )
    out_specs = (
        P(("dp", "expert"), None),
        P(("dp", "expert"), None),
        P(("dp", "expert"), None),
        P("expert", "dp", None),
        P("expert", "dp", None),
        P("expert", None, "dp"),
    )
    return jax.shard_map(
        on_device, mesh=mesh, in_specs=in_specs, out_specs=out_specs, check_vma=False
    )
```

```python
import functools

import jax
import jax.numpy as jnp
from jax import lax
from jax.experimental import pallas as pl
from jax.experimental.pallas import tpu as pltpu
from jax.sharding import PartitionSpec as P

BF16 = jnp.bfloat16
F32 = jnp.float32
LANES = 128
STRIP = 512
VMEM = pl.BlockSpec(memory_space=pltpu.VMEM)
SMEM = pl.BlockSpec(memory_space=pltpu.SMEM)


def local_call(kernel, outs, me, args, flops):
    size = sum(x.size * x.dtype.itemsize for x in (*outs, *args))
    return pl.pallas_call(
        kernel,
        out_shape=outs,
        in_specs=[SMEM] + [VMEM] * len(args),
        out_specs=[VMEM] * len(outs),
        compiler_params=pltpu.CompilerParams(vmem_limit_bytes=6 * 1024 * 1024),
        cost_estimate=pl.CostEstimate(flops=flops, bytes_accessed=size, transcendentals=0),
    )(me, *args)


def strips(width, step=STRIP):
    return [(c, min(c + step, width)) for c in range(0, width, step)]


def slot_tables(me, metas, top, side, capacity):
    count = len(metas)
    span = count * capacity
    tok = metas[0].shape[1]
    slot = lax.broadcasted_iota(jnp.int32, (side * span, tok), 0)
    expert = ((me - lax.rem(me, side)) + slot // span).astype(F32)
    block_of = lax.rem(slot, span) // capacity
    place = lax.rem(slot, capacity).astype(F32)
    row = lax.broadcasted_iota(jnp.int32, (tok, tok), 0)
    column = lax.broadcasted_iota(jnp.int32, (tok, tok), 1)
    earlier = jnp.where(row < column, 1.0, 0.0).astype(BF16)
    tables = []
    for b in range(count):
        named = [jnp.where(metas[b][k : k + 1, :] == expert, 1.0, 0.0) for k in range(top)]
        member = functools.reduce(lambda p, q: p + q, named)
        rank = jnp.dot(member.astype(BF16), earlier, preferred_element_type=F32)
        here = rank == place
        if count > 1:
            here = here & (block_of == b)
        tables.append([jnp.where(here, part, 0.0) for part in named])
    return tables


def pick_kernel(top, side, capacity, scaled, me_ref, *refs):
    count = len(scaled)
    metas, blocks, out = refs[:count], refs[count:-1], refs[-1]
    tables = slot_tables(me_ref[0], metas, top, side, capacity)
    held = jnp.concatenate([functools.reduce(lambda p, q: p + q, ks) for ks in tables], 1)
    held = held.astype(BF16)
    gate = 0.0
    for meta, ks, has in zip(metas, tables, scaled):
        for k, part in enumerate(ks):
            if has:
                part = part * meta[top + k : top + k + 1, :]
            gate += jnp.sum(part, 1, keepdims=True)
    for c, e in strips(out.shape[1]):
        block = jnp.concatenate([ref[:, c:e] for ref in blocks], 0)
        got = jnp.dot(held, block, preferred_element_type=F32)
        out[:, c:e] = ((gate * got) if any(scaled) else got).astype(BF16)


TRANSPOSED = (((0,), (0,)), ((), ()))


def picked_sum(table, back, c, e):
    return lax.dot_general(
        table.astype(BF16), back[:, c:e], TRANSPOSED, preferred_element_type=F32
    )


def sum_kernel(top, side, capacity, me_ref, meta, back, out):
    (table,) = slot_tables(me_ref[0], [meta], top, side, capacity)
    held = functools.reduce(lambda p, q: p + q, table)
    for c, e in strips(out.shape[1]):
        out[:, c:e] = picked_sum(held, back, c, e).astype(BF16)


def mix(top, table, meta, blocks, back, outs, grads, fars=(), far_grads=None):
    tok = meta.shape[1]
    gates = [meta[top + k : top + k + 1, :] for k in range(top)]
    gates = [jnp.transpose(jnp.broadcast_to(g, (8, tok)))[:, :1] for g in gates]
    sums = [jnp.zeros((tok, 1), F32) for _ in range(top)]
    for c, e in strips(back.shape[1]):
        cotangent = jnp.concatenate([ref[:, c:e] for ref in blocks], 0).astype(F32)
        mixed = 0.0
        if fars:
            mixed = jnp.concatenate([ref[:, c:e] for ref in fars], 0).astype(F32)
        for k in range(top):
            got = picked_sum(table[k], back, c, e)
            mixed += gates[k] * got
            sums[k] += jnp.sum(cotangent * got, 1, keepdims=True)
        for n, out in enumerate(outs):
            rows = out.shape[0]
            out[:, c:e] = mixed[n * rows : (n + 1) * rows].astype(BF16)
    lane = lax.broadcasted_iota(jnp.int32, (tok, LANES), 1)
    grad = jnp.zeros((tok, LANES), F32) if far_grads is None else far_grads[...]
    for k in range(top):
        grad += jnp.where(lane == k, sums[k], 0.0)
    grads[...] = grad


def mix_kernel(top, side, capacity, me_ref, meta, one, two, back, out_one, out_two, grads):
    (table,) = slot_tables(me_ref[0], [meta], top, side, capacity)
    mix(top, table, meta, (one, two), back, (out_one, out_two), grads)


def mix_last_kernel(
    top, side, capacity, me_ref, meta, block, back, one, two, far_grads, out, grads
):
    (table,) = slot_tables(me_ref[0], [meta], top, side, capacity)
    mix(top, table, meta, (block,), back, (out,), grads, (one, two), far_grads)


def sum_last_kernel(top, side, capacity, me_ref, meta, back, far, out):
    (table,) = slot_tables(me_ref[0], [meta], top, side, capacity)
    held = functools.reduce(lambda p, q: p + q, table)
    for c, e in strips(out.shape[1]):
        out[:, c:e] = (picked_sum(held, back, c, e) + far[:, c:e].astype(F32)).astype(BF16)


def fetch(sources, targets, sems):
    copies = []
    for n, (source, target) in enumerate(zip(sources, targets)):
        copies.append(pltpu.make_async_copy(source, target, sems.at[n]))
        copies[n].start()
    return copies


def dx_kernel(*refs):
    sources, outs, local = refs[:7], refs[7:11], refs[11:18]
    sems, gg, gu, dx, out_sems = refs[18:]
    wd, d_own, gate, up, d_far, wg, wu = local
    loads = fetch(sources, local, sems)
    half, feature = d_own.shape
    units = gate.shape[1]
    across_last = (((1,), (1,)), ((), ()))
    loads[0].wait()
    for r, d_rows, needed in ((0, d_own, (1, 2, 3)), (half, d_far, (4,))):
        at = slice(r, r + half)
        for n in needed:
            loads[n].wait()
        for c, e in strips(units, 256):
            back = lax.dot_general(
                d_rows[...], wd[c:e, :], across_last, preferred_element_type=F32
            )
            pre = gate[at, c:e]
            sig = 1.0 / (1.0 + jnp.exp(-pre))
            gg[at, c:e] = (back * up[at, c:e] * (sig * (1.0 + pre * (1.0 - sig)))).astype(BF16)
            gu[at, c:e] = (back * (pre * sig)).astype(BF16)
    copies = [
        pltpu.make_async_copy(gg, outs[2], out_sems.at[0]),
        pltpu.make_async_copy(gu, outs[3], out_sems.at[1]),
        pltpu.make_async_copy(dx.at[pl.ds(half, half)], outs[1], out_sems.at[2]),
        pltpu.make_async_copy(dx.at[pl.ds(0, half)], outs[0], out_sems.at[3]),
    ]
    copies[0].start()
    copies[1].start()
    loads[5].wait()
    loads[6].wait()
    for c, e in strips(feature):
        got = jnp.dot(gg[...], wg[:, c:e], preferred_element_type=F32)
        got += jnp.dot(gu[...], wu[:, c:e], preferred_element_type=F32)
        dx[:, c:e] = got.astype(BF16)
    copies[2].start()
    copies[3].start()
    for copy in copies:
        copy.wait()


def terms_kernel(*refs):
    sources, out, local = refs[:7], refs[7], refs[8:15]
    sems, tiles, tile_sems = refs[15:]
    x_own, x_far, gg, gu, d_own, d_far, hidden = local
    loads = fetch(sources, local, sems)
    half, feature = x_own.shape
    units = gg.shape[1]
    pairs = (
        (gg, x_own, x_far, (0, 1, 2)),
        (gu, x_own, x_far, (3,)),
        (hidden, d_own, d_far, (4, 5, 6)),
    )
    copies = []
    for n, (left, own, far, needed) in enumerate(pairs):
        for m in needed:
            loads[m].wait()
        for r, t in strips(units, tiles.shape[1]):
            slot = len(copies) % 2
            if len(copies) > 1:
                copies[-2].wait()
            for c, e in strips(feature, 1024):
                got = lax.dot_general(
                    left[:half, r:t], own[:, c:e], TRANSPOSED, preferred_element_type=F32
                )
                got += lax.dot_general(
                    left[half:, r:t], far[:, c:e], TRANSPOSED, preferred_element_type=F32
                )
                tiles[slot, : t - r, c:e] = got.astype(BF16)
            copy = pltpu.make_async_copy(
                tiles.at[slot, pl.ds(0, t - r)],
                out.at[pl.ds(n * units + r, t - r)],
                tile_sems.at[slot],
            )
            copy.start()
            copies.append(copy)
    for copy in copies[-2:]:
        copy.wait()


def streamed_call(kernel, outs, args, scratch):
    anywhere = pl.BlockSpec(memory_space=pltpu.HBM)
    return pl.pallas_call(
        kernel,
        out_shape=outs,
        in_specs=[anywhere] * len(args),
        out_specs=[anywhere] * len(outs),
        scratch_shapes=[
            *[pltpu.VMEM(x.shape, x.dtype) for x in args],
            pltpu.SemaphoreType.DMA((len(args),)),
            *scratch,
        ],
        compiler_params=pltpu.CompilerParams(vmem_limit_bytes=60 * 1024 * 1024),
        cost_estimate=pl.CostEstimate(flops=1, bytes_accessed=1, transcendentals=0),
    )(*args)


def on_device(tokens, expert_ids, gate_prob, w_gate, w_up, w_down, d_mixed):
    tok, feature = tokens.shape
    top = expert_ids.shape[1]
    experts = lax.axis_size("expert")
    capacity = max(2, 2 * tok * top // experts)
    side = experts // 2
    half = side * capacity
    me = lax.axis_index("expert")
    me_arr = me[None]
    sets = [[h * side + p for p in range(side)] for h in range(2)]
    shape = jax.ShapeDtypeStruct

    def across(value):
        return lax.ppermute(value, "expert", [(e, (e + side) % experts) for e in range(experts)])

    def exchange(value):
        shaped = value.reshape(side, value.shape[0] // side, value.shape[1])
        got = lax.all_to_all(shaped, "expert", 0, 0, axis_index_groups=sets, tiled=True)
        return got.reshape(value.shape)

    def after(value, *earlier):
        return lax.optimization_barrier((value, *earlier))

    def call(kernel, outs, args, flops):
        return local_call(
            functools.partial(kernel, top, side, capacity),
            [shape(*out) for out in outs],
            me_arr,
            args,
            flops,
        )

    def pick(metas, blocks, scaled):
        count = len(metas)
        return local_call(
            functools.partial(pick_kernel, top, side, capacity, scaled),
            [shape((count * half, feature), BF16)],
            me_arr,
            [*metas, *blocks],
            2 * count * count * half * tok * feature,
        )[0]

    meta = jnp.concatenate([expert_ids.T.astype(F32), gate_prob.T], 0)
    own = exchange(pick([meta, meta], [tokens, d_mixed], (False, True)))
    own = own.reshape(side, 2, capacity, feature)
    x_far, meta_far = after(across(tokens), across(meta))
    d_far = [across(d_mixed[n * (tok // 2) : (n + 1) * (tok // 2)]) for n in range(2)]
    x_far, d_far[0], own = after(x_far, d_far[0], own)
    x_own, d_own = (own[:, n].reshape(half, feature) for n in range(2))
    x_far_rows = exchange(pick([meta_far], [x_far], (False,)))
    x_rows = jnp.concatenate([x_own, x_far_rows], 0)
    d_picked, x_own, d_own, _ = after(
        pick([meta_far], d_far, (True,)), x_own, d_own, x_far_rows
    )
    d_far_rows = exchange(d_picked)

    gate_matrix, up_matrix, down_matrix = w_gate[0], w_up[0], w_down[0]
    hidden_units = gate_matrix.shape[1]
    gate_pre = jnp.dot(x_rows, gate_matrix, preferred_element_type=F32)
    up_pre = jnp.dot(x_rows, up_matrix, preferred_element_type=F32)
    hidden = (gate_pre * jax.nn.sigmoid(gate_pre) * up_pre).astype(BF16)
    y_far, y_own = (
        jnp.dot(part, down_matrix, preferred_element_type=F32).astype(BF16)
        for part in (hidden[half:], hidden[:half])
    )
    y_far, y_own, d_far_rows = after(y_far, y_own, d_far_rows)
    y_far_back = exchange(y_far)

    rows, units = shape((half, feature), BF16), shape((2 * half, hidden_units), BF16)
    dx_own, dx_far, gg, gu = streamed_call(
        dx_kernel,
        [rows, rows, units, units],
        [down_matrix, d_own, gate_pre, up_pre, d_far_rows, gate_matrix.T, up_matrix.T],
        [
            pltpu.VMEM(units.shape, BF16),
            pltpu.VMEM(units.shape, BF16),
            pltpu.VMEM((2 * half, feature), BF16),
            pltpu.SemaphoreType.DMA((4,)),
        ],
    )
    dx_own, dx_far, gg, gu, y_far_back = after(dx_own, dx_far, gg, gu, y_far_back)

    token_rows, grad_rows = ((tok, feature), BF16), ((tok, LANES), F32)
    some_rows = ((tok // 2, feature), BF16)
    work = 2 * half * tok * feature
    mixed_one, mixed_two, grads_far = call(
        mix_kernel,
        [some_rows, some_rows, grad_rows],
        [meta_far, *d_far, y_far_back],
        top * work,
    )
    y_own, gg, gu, mixed_one, mixed_two, grads_far = after(
        y_own, gg, gu, mixed_one, mixed_two, grads_far
    )
    y_own_back = exchange(y_own)
    (terms,) = streamed_call(
        terms_kernel,
        [shape((3 * hidden_units, feature), BF16)],
        [x_own, x_far_rows, gg, gu, d_own, d_far_rows, hidden],
        [pltpu.VMEM((2, 256, feature), BF16), pltpu.SemaphoreType.DMA((2,))],
    )
    dx_far, dx_own, terms, y_own_back, mixed_one = after(
        dx_far, dx_own, terms, y_own_back, across(mixed_one)
    )
    summed = lax.psum_scatter(terms, "dp", scatter_dimension=1, tiled=True)
    dx_far_back = exchange(dx_far)
    (tokens_far,) = call(sum_kernel, [token_rows], [meta_far, dx_far_back], work)
    tokens_far, dx_own, mixed_two, grads_far = after(
        tokens_far, dx_own, across(mixed_two), across(grads_far)
    )
    dx_own_back = exchange(dx_own)
    mixed, grads = call(
        mix_last_kernel,
        [token_rows, grad_rows],
        [meta, d_mixed, y_own_back, mixed_one, mixed_two, grads_far],
        top * work,
    )
    weight_grads = (
        summed[:hidden_units].astype(F32).T[None],
        summed[hidden_units : 2 * hidden_units].astype(F32).T[None],
        summed[2 * hidden_units :].astype(F32)[None],
    )
    dx_own_back, mixed, grads, *weight_grads = after(dx_own_back, mixed, grads, *weight_grads)
    (d_tokens,) = call(
        sum_last_kernel, [token_rows], [meta, dx_own_back, across(tokens_far)], work
    )
    return (mixed, d_tokens, grads[:, :top], *weight_grads)


def solution(mesh):
    in_specs = (
        P(("dp", "expert"), None),
        P(("dp", "expert"), None),
        P(("dp", "expert"), None),
        P("expert", None, None),
        P("expert", None, None),
        P("expert", None, None),
        P(("dp", "expert"), None),
    )
    out_specs = (
        P(("dp", "expert"), None),
        P(("dp", "expert"), None),
        P(("dp", "expert"), None),
        P("expert", "dp", None),
        P("expert", "dp", None),
        P("expert", None, "dp"),
    )
    return jax.shard_map(
        on_device, mesh=mesh, in_specs=in_specs, out_specs=out_specs, check_vma=False
    )
```

```python
import functools

import jax
import jax.numpy as jnp
from jax import lax
from jax.experimental import pallas as pl
from jax.experimental.pallas import tpu as pltpu
from jax.sharding import PartitionSpec as P

BF16 = jnp.bfloat16
F32 = jnp.float32
LANES = 128
STRIP = 512
VMEM = pl.BlockSpec(memory_space=pltpu.VMEM)
SMEM = pl.BlockSpec(memory_space=pltpu.SMEM)


def local_call(kernel, outs, me, args, flops):
    size = sum(x.size * x.dtype.itemsize for x in (*outs, *args))
    return pl.pallas_call(
        kernel,
        out_shape=outs,
        in_specs=[SMEM] + [VMEM] * len(args),
        out_specs=[VMEM] * len(outs),
        compiler_params=pltpu.CompilerParams(vmem_limit_bytes=6 * 1024 * 1024),
        cost_estimate=pl.CostEstimate(flops=flops, bytes_accessed=size, transcendentals=0),
    )(me, *args)


def strips(width, step=STRIP):
    return [(c, min(c + step, width)) for c in range(0, width, step)]


def slot_tables(me, metas, top, side, capacity):
    count = len(metas)
    span = count * capacity
    tok = metas[0].shape[1]
    slot = lax.broadcasted_iota(jnp.int32, (side * span, tok), 0)
    expert = ((me - lax.rem(me, side)) + slot // span).astype(F32)
    block_of = lax.rem(slot, span) // capacity
    place = lax.rem(slot, capacity).astype(F32)
    row = lax.broadcasted_iota(jnp.int32, (tok, tok), 0)
    column = lax.broadcasted_iota(jnp.int32, (tok, tok), 1)
    earlier = jnp.where(row < column, 1.0, 0.0).astype(BF16)
    tables = []
    for b in range(count):
        named = [jnp.where(metas[b][k : k + 1, :] == expert, 1.0, 0.0) for k in range(top)]
        member = functools.reduce(lambda p, q: p + q, named)
        rank = jnp.dot(member.astype(BF16), earlier, preferred_element_type=F32)
        here = rank == place
        if count > 1:
            here = here & (block_of == b)
        tables.append([jnp.where(here, part, 0.0) for part in named])
    return tables


def pick_kernel(top, side, capacity, scaled, me_ref, *refs):
    count = len(scaled)
    metas, blocks, out = refs[:count], refs[count:-1], refs[-1]
    tables = slot_tables(me_ref[0], metas, top, side, capacity)
    held = jnp.concatenate([functools.reduce(lambda p, q: p + q, ks) for ks in tables], 1)
    held = held.astype(BF16)
    gate = 0.0
    for meta, ks, has in zip(metas, tables, scaled):
        for k, part in enumerate(ks):
            if has:
                part = part * meta[top + k : top + k + 1, :]
            gate += jnp.sum(part, 1, keepdims=True)
    for c, e in strips(out.shape[1]):
        block = jnp.concatenate([ref[:, c:e] for ref in blocks], 0)
        got = jnp.dot(held, block, preferred_element_type=F32)
        out[:, c:e] = ((gate * got) if any(scaled) else got).astype(BF16)


TRANSPOSED = (((0,), (0,)), ((), ()))


def picked_sum(table, back, c, e):
    return lax.dot_general(
        table.astype(BF16), back[:, c:e], TRANSPOSED, preferred_element_type=F32
    )


def sum_kernel(top, side, capacity, me_ref, meta, back, out):
    (table,) = slot_tables(me_ref[0], [meta], top, side, capacity)
    held = functools.reduce(lambda p, q: p + q, table)
    for c, e in strips(out.shape[1]):
        out[:, c:e] = picked_sum(held, back, c, e).astype(BF16)


def mix(top, table, meta, blocks, back, outs, grads, fars=(), far_grads=None):
    tok = meta.shape[1]
    gates = [meta[top + k : top + k + 1, :] for k in range(top)]
    gates = [jnp.transpose(jnp.broadcast_to(g, (8, tok)))[:, :1] for g in gates]
    sums = [jnp.zeros((tok, 1), F32) for _ in range(top)]
    for c, e in strips(back.shape[1]):
        cotangent = jnp.concatenate([ref[:, c:e] for ref in blocks], 0).astype(F32)
        mixed = 0.0
        if fars:
            mixed = jnp.concatenate([ref[:, c:e] for ref in fars], 0).astype(F32)
        for k in range(top):
            got = picked_sum(table[k], back, c, e)
            mixed += gates[k] * got
            sums[k] += jnp.sum(cotangent * got, 1, keepdims=True)
        for n, out in enumerate(outs):
            rows = out.shape[0]
            out[:, c:e] = mixed[n * rows : (n + 1) * rows].astype(BF16)
    lane = lax.broadcasted_iota(jnp.int32, (tok, LANES), 1)
    grad = jnp.zeros((tok, LANES), F32) if far_grads is None else far_grads[...]
    for k in range(top):
        grad += jnp.where(lane == k, sums[k], 0.0)
    grads[...] = grad


def mix_kernel(
    top, side, capacity, me_ref, meta, meta_far, one, two, back, out, grads
):
    tables = slot_tables(me_ref[0], [meta, meta_far], top, side, capacity)
    mix(top, tables[1], meta_far, (one, two), back, (out,), grads)


def mix_last_kernel(
    top, side, capacity, me_ref, meta, meta_far, block, back, far, far_grads, out, grads
):
    tables = slot_tables(me_ref[0], [meta, meta_far], top, side, capacity)
    mix(top, tables[0], meta, (block,), back, (out,), grads, (far,), far_grads)


def sum_last_kernel(top, side, capacity, me_ref, meta, back, far, out):
    (table,) = slot_tables(me_ref[0], [meta], top, side, capacity)
    held = functools.reduce(lambda p, q: p + q, table)
    for c, e in strips(out.shape[1]):
        out[:, c:e] = (picked_sum(held, back, c, e) + far[:, c:e].astype(F32)).astype(BF16)


def fetch(sources, targets, sems):
    copies = []
    for n, (source, target) in enumerate(zip(sources, targets)):
        copies.append(pltpu.make_async_copy(source, target, sems.at[n]))
        copies[n].start()
    return copies


ACROSS_LAST = (((1,), (1,)), ((), ()))


def forward_kernel(side, *refs):
    sources, outs = refs[:5], refs[5:9]
    wg, wu, wd, x, gate, up, hidden, y, sems, out_sems = refs[9:]
    rows, feature = x.shape
    units, half = gate.shape[1], rows // 2
    targets = [wg, x.at[pl.ds(0, half)], x.at[pl.ds(half, half)], wu, wd]
    loads = fetch(sources, targets, sems)
    for load in loads[:3]:
        load.wait()
    for c, e in strips(units, 256):
        gate[:, c:e] = lax.dot_general(
            x[...], wg[c:e, :], ACROSS_LAST, preferred_element_type=F32
        )
    loads[3].wait()
    for c, e in strips(units, 256):
        got = lax.dot_general(x[...], wu[c:e, :], ACROSS_LAST, preferred_element_type=F32)
        up[:, c:e] = got
        pre = gate[:, c:e]
        hidden[:, c:e] = (pre * (1.0 / (1.0 + jnp.exp(-pre))) * got).astype(BF16)
    copies = [
        pltpu.make_async_copy(source, out, out_sems.at[n])
        for n, (source, out) in enumerate(zip((gate, up, hidden, y), outs))
    ]
    for copy in copies[:3]:
        copy.start()
    loads[4].wait()
    for c, e in strips(feature):
        got = jnp.dot(hidden[...], wd[:, c:e], preferred_element_type=F32)
        pair = [
            part.reshape(side, 1, half // side, e - c) for part in (got[:half], got[half:])
        ]
        y[:, c:e] = jnp.concatenate(pair, 1).reshape(rows, e - c).astype(BF16)
    copies[3].start()
    for copy in copies:
        copy.wait()


def backward_kernel(*refs):
    sources, (own_out, far_out, terms_out) = refs[:10], refs[10:13]
    wd, gate, up, wg, wu, hidden, d, x, gg, gu, dx, tiles, sems, out_sems = refs[13:]
    rows, feature = d.shape
    units, half = gate.shape[1], rows // 2
    first, second = pl.ds(0, half), pl.ds(half, half)
    targets = [wd, d.at[first], d.at[second], gate, up, wg, wu, x.at[first], x.at[second], hidden]
    loads = fetch(sources, targets, sems)
    for load in loads[:5]:
        load.wait()
    for c, e in strips(units, 256):
        back = lax.dot_general(d[...], wd[c:e, :], ACROSS_LAST, preferred_element_type=F32)
        pre = gate[:, c:e]
        sig = 1.0 / (1.0 + jnp.exp(-pre))
        gg[:, c:e] = (back * up[:, c:e] * (sig * (1.0 + pre * (1.0 - sig)))).astype(BF16)
        gu[:, c:e] = (back * (pre * sig)).astype(BF16)
    loads[5].wait()
    loads[6].wait()
    for c, e in strips(feature):
        got = jnp.dot(gg[...], wg[:, c:e], preferred_element_type=F32)
        got += jnp.dot(gu[...], wu[:, c:e], preferred_element_type=F32)
        dx[:, c:e] = got.astype(BF16)
    dx_copies = [
        pltpu.make_async_copy(dx.at[second], far_out, out_sems.at[2]),
        pltpu.make_async_copy(dx.at[first], own_out, out_sems.at[3]),
    ]
    for copy in dx_copies:
        copy.start()
    for load in loads[7:]:
        load.wait()
    copies = []
    for n, (left, right) in enumerate(((gg, x), (gu, x), (hidden, d))):
        for r, t in strips(units, tiles.shape[1]):
            slot = len(copies) % 2
            if len(copies) > 1:
                copies[-2].wait()
            for c, e in strips(feature, 1024):
                tiles[slot, : t - r, c:e] = lax.dot_general(
                    left[:, r:t], right[:, c:e], TRANSPOSED, preferred_element_type=F32
                ).astype(BF16)
            copy = pltpu.make_async_copy(
                tiles.at[slot, pl.ds(0, t - r)],
                terms_out.at[pl.ds(n * units + r, t - r)],
                out_sems.at[slot],
            )
            copy.start()
            copies.append(copy)
    for copy in (*copies[-2:], *dx_copies):
        copy.wait()


def streamed_call(kernel, outs, args, scratch):
    anywhere = pl.BlockSpec(memory_space=pltpu.HBM)
    return pl.pallas_call(
        kernel,
        out_shape=outs,
        in_specs=[anywhere] * len(args),
        out_specs=[anywhere] * len(outs),
        scratch_shapes=scratch,
        compiler_params=pltpu.CompilerParams(vmem_limit_bytes=60 * 1024 * 1024),
        cost_estimate=pl.CostEstimate(flops=1, bytes_accessed=1, transcendentals=0),
    )(*args)


def on_device(tokens, expert_ids, gate_prob, w_gate, w_up, w_down, d_mixed):
    tok, feature = tokens.shape
    top = expert_ids.shape[1]
    experts = lax.axis_size("expert")
    capacity = max(2, 2 * tok * top // experts)
    side = experts // 2
    half = side * capacity
    me = lax.axis_index("expert")
    me_arr = me[None]
    sets = [[h * side + p for p in range(side)] for h in range(2)]
    shape = jax.ShapeDtypeStruct

    def across(value):
        return lax.ppermute(value, "expert", [(e, (e + side) % experts) for e in range(experts)])

    def exchange(value):
        shaped = value.reshape(side, value.shape[0] // side, value.shape[1])
        got = lax.all_to_all(shaped, "expert", 0, 0, axis_index_groups=sets, tiled=True)
        return got.reshape(value.shape)

    def after(value, *earlier):
        return lax.optimization_barrier((value, *earlier))

    def call(kernel, outs, args, flops):
        return local_call(
            functools.partial(kernel, top, side, capacity),
            [shape(*out) for out in outs],
            me_arr,
            args,
            flops,
        )

    def pick(metas, blocks, scaled):
        count = len(metas)
        return local_call(
            functools.partial(pick_kernel, top, side, capacity, scaled),
            [shape((count * half, feature), BF16)],
            me_arr,
            [*metas, *blocks],
            2 * count * count * half * tok * feature,
        )[0]

    meta = jnp.concatenate([expert_ids.T.astype(F32), gate_prob.T], 0)
    own = exchange(pick([meta, meta], [tokens, d_mixed], (False, True)))
    own = own.reshape(side, 2, capacity, feature)
    x_far, meta_far = after(across(tokens), across(meta))
    d_far = [across(d_mixed[n * (tok // 2) : (n + 1) * (tok // 2)]) for n in range(2)]
    x_far, d_far[0], own = after(x_far, d_far[0], own)
    x_far_rows = exchange(pick([meta_far], [x_far], (False,)))
    d_picked, _ = after(pick([meta_far], d_far, (True,)), x_far_rows)
    d_far_rows = exchange(d_picked)
    x_own, d_own = (own[:, n].reshape(half, feature) for n in range(2))

    gate_matrix, up_matrix, down_matrix = w_gate[0].T, w_up[0].T, w_down[0]
    units, n_rows = gate_matrix.shape[0], 2 * half
    weight = pltpu.VMEM((units, feature), BF16)
    inner, wide = (n_rows, units), pltpu.VMEM((n_rows, feature), BF16)
    gate_pre, up_pre, hidden, y = streamed_call(
        functools.partial(forward_kernel, side),
        [shape(inner, F32), shape(inner, F32), shape(inner, BF16), shape((n_rows, feature), BF16)],
        [gate_matrix, x_own, x_far_rows, up_matrix, down_matrix],
        [
            *[weight] * 3,
            wide,
            pltpu.VMEM(inner, F32),
            pltpu.VMEM(inner, F32),
            pltpu.VMEM(inner, BF16),
            wide,
            pltpu.SemaphoreType.DMA((5,)),
            pltpu.SemaphoreType.DMA((4,)),
        ],
    )
    y, d_far_rows = after(y, d_far_rows)
    y_back = exchange(y)

    dx_own, dx_far, terms = streamed_call(
        backward_kernel,
        [shape((half, feature), BF16)] * 2 + [shape((3 * units, feature), BF16)],
        [
            down_matrix,
            d_own,
            d_far_rows,
            gate_pre,
            up_pre,
            gate_matrix,
            up_matrix,
            x_own,
            x_far_rows,
            hidden,
        ],
        [
            weight,
            pltpu.VMEM(inner, F32),
            pltpu.VMEM(inner, F32),
            weight,
            weight,
            pltpu.VMEM(inner, BF16),
            wide,
            wide,
            pltpu.VMEM(inner, BF16),
            pltpu.VMEM(inner, BF16),
            wide,
            pltpu.VMEM((2, 256, feature), BF16),
            pltpu.SemaphoreType.DMA((10,)),
            pltpu.SemaphoreType.DMA((4,)),
        ],
    )
    dx_own, dx_far, terms, y_back = after(dx_own, dx_far, terms, y_back)
    summed = lax.psum_scatter(terms, "dp", scatter_dimension=1, tiled=True)

    token_rows, grad_rows = ((tok, feature), BF16), ((tok, LANES), F32)
    work = 2 * half * tok * feature
    mixed_far, grads_far = call(
        mix_kernel, [token_rows, grad_rows], [meta, meta_far, *d_far, y_back], 2 * top * work
    )
    dx_far, mixed_far, grads_far = after(dx_far, mixed_far, grads_far)
    dx_far_back = exchange(dx_far)
    (tokens_far,) = call(sum_kernel, [token_rows], [meta_far, dx_far_back], work)
    tokens_far, dx_own, mixed_far, grads_far = after(
        tokens_far, dx_own, across(mixed_far), across(grads_far)
    )
    dx_own_back = exchange(dx_own)
    mixed, grads = call(
        mix_last_kernel,
        [token_rows, grad_rows],
        [meta, meta_far, d_mixed, y_back, mixed_far, grads_far],
        2 * top * work,
    )
    weight_grads = (
        summed[:units].astype(F32).T[None],
        summed[units : 2 * units].astype(F32).T[None],
        summed[2 * units :].astype(F32)[None],
    )
    dx_own_back, mixed, grads, *weight_grads = after(dx_own_back, mixed, grads, *weight_grads)
    (d_tokens,) = call(
        sum_last_kernel, [token_rows], [meta, dx_own_back, across(tokens_far)], work
    )
    return (mixed, d_tokens, grads[:, :top], *weight_grads)


def solution(mesh):
    in_specs = (
        P(("dp", "expert"), None),
        P(("dp", "expert"), None),
        P(("dp", "expert"), None),
        P("expert", None, None),
        P("expert", None, None),
        P("expert", None, None),
        P(("dp", "expert"), None),
    )
    out_specs = (
        P(("dp", "expert"), None),
        P(("dp", "expert"), None),
        P(("dp", "expert"), None),
        P("expert", "dp", None),
        P("expert", "dp", None),
        P("expert", None, "dp"),
    )
    return jax.shard_map(
        on_device, mesh=mesh, in_specs=in_specs, out_specs=out_specs, check_vma=False
    )
```

```python
import functools

import jax
import jax.numpy as jnp
from jax import lax
from jax.experimental import pallas as pl
from jax.experimental.pallas import tpu as pltpu
from jax.sharding import PartitionSpec as P

BF16 = jnp.bfloat16
F32 = jnp.float32
LANES = 128
STRIP = 512
VMEM = pl.BlockSpec(memory_space=pltpu.VMEM)
SMEM = pl.BlockSpec(memory_space=pltpu.SMEM)


def local_call(kernel, outs, me, args, flops):
    size = sum(x.size * x.dtype.itemsize for x in (*outs, *args))
    return pl.pallas_call(
        kernel,
        out_shape=outs,
        in_specs=[SMEM] + [VMEM] * len(args),
        out_specs=[VMEM] * len(outs),
        compiler_params=pltpu.CompilerParams(vmem_limit_bytes=6 * 1024 * 1024),
        cost_estimate=pl.CostEstimate(flops=flops, bytes_accessed=size, transcendentals=0),
    )(me, *args)


def strips(width, step=STRIP):
    return [(c, min(c + step, width)) for c in range(0, width, step)]


def slot_tables(me, metas, top, side, capacity):
    count = len(metas)
    span = count * capacity
    tok = metas[0].shape[1]
    slot = lax.broadcasted_iota(jnp.int32, (side * span, tok), 0)
    expert = ((me - lax.rem(me, side)) + slot // span).astype(F32)
    block_of = lax.rem(slot, span) // capacity
    place = lax.rem(slot, capacity).astype(F32)
    row = lax.broadcasted_iota(jnp.int32, (tok, tok), 0)
    column = lax.broadcasted_iota(jnp.int32, (tok, tok), 1)
    earlier = jnp.where(row < column, 1.0, 0.0).astype(BF16)
    tables = []
    for b in range(count):
        named = [jnp.where(metas[b][k : k + 1, :] == expert, 1.0, 0.0) for k in range(top)]
        member = functools.reduce(lambda p, q: p + q, named)
        rank = jnp.dot(member.astype(BF16), earlier, preferred_element_type=F32)
        here = rank == place
        if count > 1:
            here = here & (block_of == b)
        tables.append([jnp.where(here, part, 0.0) for part in named])
    return tables


def pick_kernel(top, side, capacity, scaled, me_ref, *refs):
    count = len(scaled)
    metas, blocks, out = refs[:count], refs[count:-1], refs[-1]
    tables = slot_tables(me_ref[0], metas, top, side, capacity)
    held = jnp.concatenate([functools.reduce(lambda p, q: p + q, ks) for ks in tables], 1)
    held = held.astype(BF16)
    gate = 0.0
    for meta, ks, has in zip(metas, tables, scaled):
        for k, part in enumerate(ks):
            if has:
                part = part * meta[top + k : top + k + 1, :]
            gate += jnp.sum(part, 1, keepdims=True)
    for c, e in strips(out.shape[1]):
        block = jnp.concatenate([ref[:, c:e] for ref in blocks], 0)
        got = jnp.dot(held, block, preferred_element_type=F32)
        out[:, c:e] = ((gate * got) if any(scaled) else got).astype(BF16)


def own_pick_kernel(top, side, capacity, me_ref, meta, x_hbm, d_hbm, out, x, d, sems):
    for load in fetch((x_hbm, d_hbm), (x, d), sems):
        load.wait()
    pick_kernel(top, side, capacity, (False, True), me_ref, meta, meta, x, d, out)


TRANSPOSED = (((0,), (0,)), ((), ()))


def picked_sum(table, back, c, e):
    return lax.dot_general(
        table.astype(BF16), back[:, c:e], TRANSPOSED, preferred_element_type=F32
    )


def sum_kernel(top, side, capacity, me_ref, meta, back, out):
    (table,) = slot_tables(me_ref[0], [meta], top, side, capacity)
    held = functools.reduce(lambda p, q: p + q, table)
    for c, e in strips(out.shape[1]):
        out[:, c:e] = picked_sum(held, back, c, e).astype(BF16)


def mix(top, table, meta, blocks, back, outs, grads, fars=(), far_grads=None):
    tok = meta.shape[1]
    gates = [meta[top + k : top + k + 1, :] for k in range(top)]
    gates = [jnp.transpose(jnp.broadcast_to(g, (8, tok)))[:, :1] for g in gates]
    sums = [jnp.zeros((tok, 1), F32) for _ in range(top)]
    for c, e in strips(back.shape[1]):
        cotangent = jnp.concatenate([ref[:, c:e] for ref in blocks], 0).astype(F32)
        mixed = 0.0
        if fars:
            mixed = jnp.concatenate([ref[:, c:e] for ref in fars], 0).astype(F32)
        for k in range(top):
            got = picked_sum(table[k], back, c, e)
            mixed += gates[k] * got
            sums[k] += jnp.sum(cotangent * got, 1, keepdims=True)
        for n, out in enumerate(outs):
            rows = out.shape[0]
            out[:, c:e] = mixed[n * rows : (n + 1) * rows].astype(BF16)
    lane = lax.broadcasted_iota(jnp.int32, (tok, LANES), 1)
    grad = jnp.zeros((tok, LANES), F32) if far_grads is None else far_grads[...]
    for k in range(top):
        grad += jnp.where(lane == k, sums[k], 0.0)
    grads[...] = grad


def mix_kernel(
    top, side, capacity, me_ref, meta, meta_far, one, two, back, out, grads
):
    tables = slot_tables(me_ref[0], [meta, meta_far], top, side, capacity)
    mix(top, tables[1], meta_far, (one, two), back, (out,), grads)


def mix_last_kernel(
    top, side, capacity, me_ref, meta, meta_far, block, back, far, far_grads, out, grads
):
    tables = slot_tables(me_ref[0], [meta, meta_far], top, side, capacity)
    mix(top, tables[0], meta, (block,), back, (out,), grads, (far,), far_grads)


def sum_last_kernel(top, side, capacity, me_ref, meta, back, far, out):
    (table,) = slot_tables(me_ref[0], [meta], top, side, capacity)
    held = functools.reduce(lambda p, q: p + q, table)
    for c, e in strips(out.shape[1]):
        out[:, c:e] = (picked_sum(held, back, c, e) + far[:, c:e].astype(F32)).astype(BF16)


def fetch(sources, targets, sems):
    copies = []
    for n, (source, target) in enumerate(zip(sources, targets)):
        copies.append(pltpu.make_async_copy(source, target, sems.at[n]))
        copies[n].start()
    return copies


ACROSS_LAST = (((1,), (1,)), ((), ()))


def forward_kernel(side, *refs):
    sources, outs = refs[:5], refs[5:9]
    wg, wu, wd, x, gate, up, hidden, y, sems, out_sems = refs[9:]
    rows, feature = x.shape
    units, half = gate.shape[1], rows // 2
    targets = [wg, x.at[pl.ds(0, half)], x.at[pl.ds(half, half)], wu, wd]
    loads = fetch(sources, targets, sems)
    for load in loads[:3]:
        load.wait()
    for c, e in strips(units, 256):
        gate[:, c:e] = lax.dot_general(
            x[...], wg[c:e, :], ACROSS_LAST, preferred_element_type=F32
        )
    loads[3].wait()
    for c, e in strips(units, 256):
        got = lax.dot_general(x[...], wu[c:e, :], ACROSS_LAST, preferred_element_type=F32)
        up[:, c:e] = got
        pre = gate[:, c:e]
        hidden[:, c:e] = (pre * (1.0 / (1.0 + jnp.exp(-pre))) * got).astype(BF16)
    copies = [
        pltpu.make_async_copy(source, out, out_sems.at[n])
        for n, (source, out) in enumerate(zip((gate, up, hidden, y), outs))
    ]
    for copy in copies[:3]:
        copy.start()
    loads[4].wait()
    for c, e in strips(feature):
        got = jnp.dot(hidden[...], wd[:, c:e], preferred_element_type=F32)
        pair = [
            part.reshape(side, 1, half // side, e - c) for part in (got[:half], got[half:])
        ]
        y[:, c:e] = jnp.concatenate(pair, 1).reshape(rows, e - c).astype(BF16)
    copies[3].start()
    for copy in copies:
        copy.wait()


def backward_kernel(*refs):
    sources, (own_out, far_out, terms_out) = refs[:10], refs[10:13]
    wd, gate, up, wg, wu, hidden, d, x, gg, gu, dx, tiles, sems, out_sems = refs[13:]
    rows, feature = d.shape
    units, half = gate.shape[1], rows // 2
    first, second = pl.ds(0, half), pl.ds(half, half)
    targets = [wd, d.at[first], d.at[second], gate, up, wg, wu, x.at[first], x.at[second], hidden]
    loads = fetch(sources, targets, sems)
    for load in loads[:5]:
        load.wait()
    for c, e in strips(units, 256):
        back = lax.dot_general(d[...], wd[c:e, :], ACROSS_LAST, preferred_element_type=F32)
        pre = gate[:, c:e]
        sig = 1.0 / (1.0 + jnp.exp(-pre))
        gg[:, c:e] = (back * up[:, c:e] * (sig * (1.0 + pre * (1.0 - sig)))).astype(BF16)
        gu[:, c:e] = (back * (pre * sig)).astype(BF16)
    loads[5].wait()
    loads[6].wait()
    for c, e in strips(feature):
        got = jnp.dot(gg[...], wg[:, c:e], preferred_element_type=F32)
        got += jnp.dot(gu[...], wu[:, c:e], preferred_element_type=F32)
        dx[:, c:e] = got.astype(BF16)
    dx_copies = [
        pltpu.make_async_copy(dx.at[second], far_out, out_sems.at[2]),
        pltpu.make_async_copy(dx.at[first], own_out, out_sems.at[3]),
    ]
    for copy in dx_copies:
        copy.start()
    for load in loads[7:]:
        load.wait()
    copies = []
    for n, (left, right) in enumerate(((gg, x), (gu, x), (hidden, d))):
        for r, t in strips(units, tiles.shape[1]):
            slot = len(copies) % 2
            if len(copies) > 1:
                copies[-2].wait()
            for c, e in strips(feature, 1024):
                tiles[slot, : t - r, c:e] = lax.dot_general(
                    left[:, r:t], right[:, c:e], TRANSPOSED, preferred_element_type=F32
                ).astype(BF16)
            copy = pltpu.make_async_copy(
                tiles.at[slot, pl.ds(0, t - r)],
                terms_out.at[pl.ds(n * units + r, t - r)],
                out_sems.at[slot],
            )
            copy.start()
            copies.append(copy)
    for copy in (*copies[-2:], *dx_copies):
        copy.wait()


def streamed_call(kernel, outs, args, scratch):
    anywhere = pl.BlockSpec(memory_space=pltpu.HBM)
    return pl.pallas_call(
        kernel,
        out_shape=outs,
        in_specs=[anywhere] * len(args),
        out_specs=[anywhere] * len(outs),
        scratch_shapes=scratch,
        compiler_params=pltpu.CompilerParams(vmem_limit_bytes=60 * 1024 * 1024),
        cost_estimate=pl.CostEstimate(flops=1, bytes_accessed=1, transcendentals=0),
    )(*args)


def on_device(tokens, expert_ids, gate_prob, w_gate, w_up, w_down, d_mixed):
    tok, feature = tokens.shape
    top = expert_ids.shape[1]
    experts = lax.axis_size("expert")
    capacity = max(2, 2 * tok * top // experts)
    side = experts // 2
    half = side * capacity
    me = lax.axis_index("expert")
    me_arr = me[None]
    sets = [[h * side + p for p in range(side)] for h in range(2)]
    shape = jax.ShapeDtypeStruct

    def across(value):
        return lax.ppermute(value, "expert", [(e, (e + side) % experts) for e in range(experts)])

    def exchange(value):
        shaped = value.reshape(side, value.shape[0] // side, value.shape[1])
        got = lax.all_to_all(shaped, "expert", 0, 0, axis_index_groups=sets, tiled=True)
        return got.reshape(value.shape)

    def after(value, *earlier):
        return lax.optimization_barrier((value, *earlier))

    def call(kernel, outs, args, flops):
        return local_call(
            functools.partial(kernel, top, side, capacity),
            [shape(*out) for out in outs],
            me_arr,
            args,
            flops,
        )

    def pick(metas, blocks, scaled, work=None):
        count = len(metas)
        return local_call(
            functools.partial(pick_kernel, top, side, capacity, scaled),
            [shape((count * half, feature), BF16)],
            me_arr,
            [*metas, *blocks],
            work or 2 * count * count * half * tok * feature,
        )[0]

    meta = jnp.concatenate([expert_ids.T.astype(F32), gate_prob.T], 0)
    anywhere = pl.BlockSpec(memory_space=pltpu.HBM)
    picked = pl.pallas_call(
        functools.partial(own_pick_kernel, top, side, capacity),
        out_shape=shape((2 * half, feature), BF16),
        in_specs=[SMEM, VMEM, anywhere, anywhere],
        out_specs=VMEM,
        scratch_shapes=[
            pltpu.VMEM((tok, feature), BF16),
            pltpu.VMEM((tok, feature), BF16),
            pltpu.SemaphoreType.DMA((2,)),
        ],
        compiler_params=pltpu.CompilerParams(vmem_limit_bytes=60 * 1024 * 1024),
        cost_estimate=pl.CostEstimate(
            flops=8 * half * tok * feature, bytes_accessed=1, transcendentals=0
        ),
    )(me_arr, meta, tokens, d_mixed)
    own = exchange(picked)
    own = own.reshape(side, 2, capacity, feature)
    x_far, meta_far = after(across(tokens), across(meta))
    d_far = [across(d_mixed[n * (tok // 2) : (n + 1) * (tok // 2)]) for n in range(2)]
    x_far, d_far[0] = after(x_far, d_far[0])
    x_picked, own = after(pick([meta_far], [x_far], (False,), 10**11), own)
    x_far_rows = exchange(x_picked)
    d_picked, _ = after(pick([meta_far], d_far, (True,)), x_far_rows)
    d_far_rows = exchange(d_picked)
    x_own, d_own = (own[:, n].reshape(half, feature) for n in range(2))

    gate_matrix, up_matrix, down_matrix = w_gate[0].T, w_up[0].T, w_down[0]
    units, n_rows = gate_matrix.shape[0], 2 * half
    weight = pltpu.VMEM((units, feature), BF16)
    inner, wide = (n_rows, units), pltpu.VMEM((n_rows, feature), BF16)
    gate_pre, up_pre, hidden, y = streamed_call(
        functools.partial(forward_kernel, side),
        [shape(inner, F32), shape(inner, F32), shape(inner, BF16), shape((n_rows, feature), BF16)],
        [gate_matrix, x_own, x_far_rows, up_matrix, down_matrix],
        [
            *[weight] * 3,
            wide,
            pltpu.VMEM(inner, F32),
            pltpu.VMEM(inner, F32),
            pltpu.VMEM(inner, BF16),
            wide,
            pltpu.SemaphoreType.DMA((5,)),
            pltpu.SemaphoreType.DMA((4,)),
        ],
    )
    y, d_far_rows = after(y, d_far_rows)
    y_back = exchange(y)

    dx_own, dx_far, terms = streamed_call(
        backward_kernel,
        [shape((half, feature), BF16)] * 2 + [shape((3 * units, feature), BF16)],
        [
            down_matrix,
            d_own,
            d_far_rows,
            gate_pre,
            up_pre,
            gate_matrix,
            up_matrix,
            x_own,
            x_far_rows,
            hidden,
        ],
        [
            weight,
            pltpu.VMEM(inner, F32),
            pltpu.VMEM(inner, F32),
            weight,
            weight,
            pltpu.VMEM(inner, BF16),
            wide,
            wide,
            pltpu.VMEM(inner, BF16),
            pltpu.VMEM(inner, BF16),
            wide,
            pltpu.VMEM((2, 256, feature), BF16),
            pltpu.SemaphoreType.DMA((10,)),
            pltpu.SemaphoreType.DMA((4,)),
        ],
    )
    dx_own, dx_far, terms, y_back = after(dx_own, dx_far, terms, y_back)
    summed = lax.psum_scatter(terms, "dp", scatter_dimension=1, tiled=True)

    token_rows, grad_rows = ((tok, feature), BF16), ((tok, LANES), F32)
    work = 2 * half * tok * feature
    mixed_far, grads_far = call(
        mix_kernel, [token_rows, grad_rows], [meta, meta_far, *d_far, y_back], 2 * top * work
    )
    dx_far, mixed_far, grads_far = after(dx_far, mixed_far, grads_far)
    dx_far_back = exchange(dx_far)
    mixed_far, grads_far = after(across(mixed_far), across(grads_far))
    mixed, grads = call(
        mix_last_kernel,
        [token_rows, grad_rows],
        [meta, meta_far, d_mixed, y_back, mixed_far, grads_far],
        10**11,
    )
    dx_far_back, mixed, grads = after(dx_far_back, mixed, grads)
    (tokens_far,) = call(sum_kernel, [token_rows], [meta_far, dx_far_back], work)
    tokens_far, dx_own = after(tokens_far, dx_own)
    dx_own_back = exchange(dx_own)
    weight_grads = (
        summed[:units].astype(F32).T[None],
        summed[units : 2 * units].astype(F32).T[None],
        summed[2 * units :].astype(F32)[None],
    )
    dx_own_back, mixed, grads, *weight_grads = after(dx_own_back, mixed, grads, *weight_grads)
    (d_tokens,) = call(
        sum_last_kernel, [token_rows], [meta, dx_own_back, across(tokens_far)], work
    )
    return (mixed, d_tokens, grads[:, :top], *weight_grads)


def solution(mesh):
    in_specs = (
        P(("dp", "expert"), None),
        P(("dp", "expert"), None),
        P(("dp", "expert"), None),
        P("expert", None, None),
        P("expert", None, None),
        P("expert", None, None),
        P(("dp", "expert"), None),
    )
    out_specs = (
        P(("dp", "expert"), None),
        P(("dp", "expert"), None),
        P(("dp", "expert"), None),
        P("expert", "dp", None),
        P("expert", "dp", None),
        P("expert", None, "dp"),
    )
    return jax.shard_map(
        on_device, mesh=mesh, in_specs=in_specs, out_specs=out_specs, check_vma=False
    )
```

```python
import functools

import jax
import jax.numpy as jnp
from jax import lax
from jax.experimental import pallas as pl
from jax.experimental.pallas import tpu as pltpu
from jax.sharding import PartitionSpec as P

BF16 = jnp.bfloat16
F32 = jnp.float32
LANES = 128
STRIP = 512
LONG = 10**11
VMEM = pl.BlockSpec(memory_space=pltpu.VMEM)
SMEM = pl.BlockSpec(memory_space=pltpu.SMEM)


def local_call(kernel, outs, me, args, flops):
    size = sum(x.size * x.dtype.itemsize for x in (*outs, *args))
    return pl.pallas_call(
        kernel,
        out_shape=outs,
        in_specs=[SMEM] + [VMEM] * len(args),
        out_specs=[VMEM] * len(outs),
        compiler_params=pltpu.CompilerParams(vmem_limit_bytes=6 * 1024 * 1024),
        cost_estimate=pl.CostEstimate(flops=flops, bytes_accessed=size, transcendentals=0),
    )(me, *args)


def local_call_plain(kernel, outs, args, flops):
    return local_call(lambda me_ref, *refs: kernel(*refs), outs, jnp.zeros((1,), jnp.int32), args, flops)


def strips(width, step=STRIP):
    return [(c, min(c + step, width)) for c in range(0, width, step)]


def slot_tables(me, metas, top, side, capacity):
    count = len(metas)
    span = count * capacity
    tok = metas[0].shape[1]
    slot = lax.broadcasted_iota(jnp.int32, (side * span, tok), 0)
    expert = ((me - lax.rem(me, side)) + slot // span).astype(F32)
    block_of = lax.rem(slot, span) // capacity
    place = lax.rem(slot, capacity).astype(F32)
    row = lax.broadcasted_iota(jnp.int32, (tok, tok), 0)
    column = lax.broadcasted_iota(jnp.int32, (tok, tok), 1)
    earlier = jnp.where(row < column, 1.0, 0.0).astype(BF16)
    tables = []
    for b in range(count):
        named = [jnp.where(metas[b][k : k + 1, :] == expert, 1.0, 0.0) for k in range(top)]
        member = functools.reduce(lambda p, q: p + q, named)
        rank = jnp.dot(member.astype(BF16), earlier, preferred_element_type=F32)
        here = rank == place
        if count > 1:
            here = here & (block_of == b)
        tables.append([jnp.where(here, part, 0.0) for part in named])
    return tables


def pick_kernel(top, side, capacity, scaled, me_ref, *refs):
    count = len(scaled)
    metas, blocks, out = refs[:count], refs[count:-1], refs[-1]
    tables = slot_tables(me_ref[0], metas, top, side, capacity)
    held = jnp.concatenate([functools.reduce(lambda p, q: p + q, ks) for ks in tables], 1)
    held = held.astype(BF16)
    gate = 0.0
    for meta, ks, has in zip(metas, tables, scaled):
        for k, part in enumerate(ks):
            if has:
                part = part * meta[top + k : top + k + 1, :]
            gate += jnp.sum(part, 1, keepdims=True)
    for c, e in strips(out.shape[1]):
        block = jnp.concatenate([ref[:, c:e] for ref in blocks], 0)
        got = jnp.dot(held, block, preferred_element_type=F32)
        out[:, c:e] = ((gate * got) if any(scaled) else got).astype(BF16)


def own_pick_kernel(top, side, capacity, me_ref, meta, x_hbm, d_hbm, out, x, d, sems):
    for load in fetch((x_hbm, d_hbm), (x, d), sems):
        load.wait()
    pick_kernel(top, side, capacity, (False, True), me_ref, meta, meta, x, d, out)


TRANSPOSED = (((0,), (0,)), ((), ()))


def picked_sum(table, back, c, e):
    return lax.dot_general(
        table.astype(BF16), back[:, c:e], TRANSPOSED, preferred_element_type=F32
    )


def table_kernel(top, side, capacity, me_ref, meta, came, out):
    (table,) = slot_tables(me_ref[0], [meta], top, side, capacity)
    out[...] = functools.reduce(lambda p, q: p + q, table).astype(BF16)


def sum_kernel(table, back, *refs):
    out = refs[-1]
    for c, e in strips(out.shape[1]):
        got = picked_sum(table[...], back, c, e)
        for far in refs[:-1]:
            got += far[:, c:e].astype(F32)
        out[:, c:e] = got.astype(BF16)


def mix(top, table, meta, blocks, back, outs, grads, fars=(), far_grads=None):
    tok = meta.shape[1]
    gates = [meta[top + k : top + k + 1, :] for k in range(top)]
    gates = [jnp.transpose(jnp.broadcast_to(g, (8, tok)))[:, :1] for g in gates]
    sums = [jnp.zeros((tok, 1), F32) for _ in range(top)]
    for c, e in strips(back.shape[1]):
        cotangent = jnp.concatenate([ref[:, c:e] for ref in blocks], 0).astype(F32)
        mixed = 0.0
        if fars:
            mixed = jnp.concatenate([ref[:, c:e] for ref in fars], 0).astype(F32)
        for k in range(top):
            got = picked_sum(table[k], back, c, e)
            mixed += gates[k] * got
            sums[k] += jnp.sum(cotangent * got, 1, keepdims=True)
        for n, out in enumerate(outs):
            rows = out.shape[0]
            out[:, c:e] = mixed[n * rows : (n + 1) * rows].astype(BF16)
    lane = lax.broadcasted_iota(jnp.int32, (tok, LANES), 1)
    grad = jnp.zeros((tok, LANES), F32) if far_grads is None else far_grads[...]
    for k in range(top):
        grad += jnp.where(lane == k, sums[k], 0.0)
    grads[...] = grad


def mix_kernel(
    top, side, capacity, me_ref, meta, meta_far, block, back, out, grads
):
    tables = slot_tables(me_ref[0], [meta, meta_far], top, side, capacity)
    mix(top, tables[1], meta_far, (block,), back, (out,), grads)


def mix_last_kernel(
    top, side, capacity, me_ref, meta, meta_far, block, back, far, far_grads, out, grads
):
    tables = slot_tables(me_ref[0], [meta, meta_far], top, side, capacity)
    mix(top, tables[0], meta, (block,), back, (out,), grads, (far,), far_grads)


def fetch(sources, targets, sems):
    copies = []
    for n, (source, target) in enumerate(zip(sources, targets)):
        copies.append(pltpu.make_async_copy(source, target, sems.at[n]))
        copies[n].start()
    return copies


ACROSS_LAST = (((1,), (1,)), ((), ()))


def forward_kernel(side, *refs):
    sources, outs = refs[:5], refs[5:9]
    wg, wu, wd, x, gate, up, hidden, y, sems, out_sems = refs[9:]
    rows, feature = x.shape
    units, half = gate.shape[1], rows // 2
    targets = [wg, x.at[pl.ds(0, half)], x.at[pl.ds(half, half)], wu, wd]
    loads = fetch(sources, targets, sems)
    for load in loads[:3]:
        load.wait()
    for c, e in strips(units, 256):
        gate[:, c:e] = lax.dot_general(
            x[...], wg[c:e, :], ACROSS_LAST, preferred_element_type=F32
        )
    loads[3].wait()
    for c, e in strips(units, 256):
        got = lax.dot_general(x[...], wu[c:e, :], ACROSS_LAST, preferred_element_type=F32)
        up[:, c:e] = got
        pre = gate[:, c:e]
        hidden[:, c:e] = (pre * (1.0 / (1.0 + jnp.exp(-pre))) * got).astype(BF16)
    copies = [
        pltpu.make_async_copy(source, out, out_sems.at[n])
        for n, (source, out) in enumerate(zip((gate, up, hidden, y), outs))
    ]
    for copy in copies[:3]:
        copy.start()
    loads[4].wait()
    for c, e in strips(feature):
        got = jnp.dot(hidden[...], wd[:, c:e], preferred_element_type=F32)
        pair = [
            part.reshape(side, 1, half // side, e - c) for part in (got[:half], got[half:])
        ]
        y[:, c:e] = jnp.concatenate(pair, 1).reshape(rows, e - c).astype(BF16)
    copies[3].start()
    for copy in copies:
        copy.wait()


def backward_kernel(*refs):
    sources, (own_out, far_out, terms_out) = refs[:10], refs[10:13]
    wd, gate, up, wg, wu, hidden, d, x, gg, gu, dx, tiles, sems, out_sems = refs[13:]
    rows, feature = d.shape
    units, half = gate.shape[1], rows // 2
    first, second = pl.ds(0, half), pl.ds(half, half)
    targets = [wd, d.at[first], d.at[second], gate, up, wg, wu, x.at[first], x.at[second], hidden]
    loads = fetch(sources, targets, sems)
    for load in loads[:5]:
        load.wait()
    for c, e in strips(units, 256):
        back = lax.dot_general(d[...], wd[c:e, :], ACROSS_LAST, preferred_element_type=F32)
        pre = gate[:, c:e]
        sig = 1.0 / (1.0 + jnp.exp(-pre))
        gg[:, c:e] = (back * up[:, c:e] * (sig * (1.0 + pre * (1.0 - sig)))).astype(BF16)
        gu[:, c:e] = (back * (pre * sig)).astype(BF16)
    loads[5].wait()
    loads[6].wait()
    for c, e in strips(feature):
        got = jnp.dot(gg[...], wg[:, c:e], preferred_element_type=F32)
        got += jnp.dot(gu[...], wu[:, c:e], preferred_element_type=F32)
        dx[:, c:e] = got.astype(BF16)
    dx_copies = [
        pltpu.make_async_copy(dx.at[second], far_out, out_sems.at[2]),
        pltpu.make_async_copy(dx.at[first], own_out, out_sems.at[3]),
    ]
    for copy in dx_copies:
        copy.start()
    for load in loads[7:]:
        load.wait()
    copies = []
    for n, (left, right) in enumerate(((gg, x), (gu, x), (hidden, d))):
        for r, t in strips(units, tiles.shape[1]):
            slot = len(copies) % 2
            if len(copies) > 1:
                copies[-2].wait()
            for c, e in strips(feature, 1024):
                tiles[slot, : t - r, c:e] = lax.dot_general(
                    left[:, r:t], right[:, c:e], TRANSPOSED, preferred_element_type=F32
                ).astype(BF16)
            copy = pltpu.make_async_copy(
                tiles.at[slot, pl.ds(0, t - r)],
                terms_out.at[pl.ds(n * units + r, t - r)],
                out_sems.at[slot],
            )
            copy.start()
            copies.append(copy)
    for copy in (*copies[-2:], *dx_copies):
        copy.wait()


def streamed_call(kernel, outs, args, scratch):
    anywhere = pl.BlockSpec(memory_space=pltpu.HBM)
    return pl.pallas_call(
        kernel,
        out_shape=outs,
        in_specs=[anywhere] * len(args),
        out_specs=[anywhere] * len(outs),
        scratch_shapes=scratch,
        compiler_params=pltpu.CompilerParams(vmem_limit_bytes=60 * 1024 * 1024),
        cost_estimate=pl.CostEstimate(flops=1, bytes_accessed=1, transcendentals=0),
    )(*args)


def on_device(tokens, expert_ids, gate_prob, w_gate, w_up, w_down, d_mixed):
    tok, feature = tokens.shape
    top = expert_ids.shape[1]
    experts = lax.axis_size("expert")
    capacity = max(2, 2 * tok * top // experts)
    side = experts // 2
    half = side * capacity
    me = lax.axis_index("expert")
    me_arr = me[None]
    sets = [[h * side + p for p in range(side)] for h in range(2)]
    shape = jax.ShapeDtypeStruct

    def across(value):
        return lax.ppermute(value, "expert", [(e, (e + side) % experts) for e in range(experts)])

    def exchange(value):
        shaped = value.reshape(side, value.shape[0] // side, value.shape[1])
        got = lax.all_to_all(shaped, "expert", 0, 0, axis_index_groups=sets, tiled=True)
        return got.reshape(value.shape)

    def after(value, *earlier):
        return lax.optimization_barrier((value, *earlier))

    def call(kernel, outs, args, flops):
        return local_call(
            functools.partial(kernel, top, side, capacity),
            [shape(*out) for out in outs],
            me_arr,
            args,
            flops,
        )

    def pick(metas, blocks, scaled):
        count = len(metas)
        return local_call(
            functools.partial(pick_kernel, top, side, capacity, scaled),
            [shape((count * half, feature), BF16)],
            me_arr,
            [*metas, *blocks],
            LONG,
        )[0]

    meta = jnp.concatenate([expert_ids.T.astype(F32), gate_prob.T], 0)
    anywhere = pl.BlockSpec(memory_space=pltpu.HBM)
    picked = pl.pallas_call(
        functools.partial(own_pick_kernel, top, side, capacity),
        out_shape=shape((2 * half, feature), BF16),
        in_specs=[SMEM, VMEM, anywhere, anywhere],
        out_specs=VMEM,
        scratch_shapes=[
            pltpu.VMEM((tok, feature), BF16),
            pltpu.VMEM((tok, feature), BF16),
            pltpu.SemaphoreType.DMA((2,)),
        ],
        compiler_params=pltpu.CompilerParams(vmem_limit_bytes=60 * 1024 * 1024),
        cost_estimate=pl.CostEstimate(
            flops=8 * half * tok * feature, bytes_accessed=1, transcendentals=0
        ),
    )(me_arr, meta, tokens, d_mixed)
    own = exchange(picked)
    own = own.reshape(side, 2, capacity, feature)
    x_far, meta_far = after(across(tokens), across(meta))
    d_late, x_far = after(d_mixed, x_far)
    d_far = across(d_late)
    x_picked, own = after(pick([meta_far], [x_far], (False,)), own)
    x_far_rows = exchange(x_picked)
    d_picked, x_far_rows = after(pick([meta_far], [d_far], (True,)), x_far_rows)
    d_far_rows = exchange(d_picked)
    x_own, d_own = (own[:, n].reshape(half, feature) for n in range(2))

    gate_matrix, up_matrix, down_matrix = w_gate[0].T, w_up[0].T, w_down[0]
    units, n_rows = gate_matrix.shape[0], 2 * half
    weight = pltpu.VMEM((units, feature), BF16)
    inner, wide = (n_rows, units), pltpu.VMEM((n_rows, feature), BF16)
    gate_pre, up_pre, hidden, y = streamed_call(
        functools.partial(forward_kernel, side),
        [shape(inner, F32), shape(inner, F32), shape(inner, BF16), shape((n_rows, feature), BF16)],
        [gate_matrix, x_own, x_far_rows, up_matrix, down_matrix],
        [
            *[weight] * 3,
            wide,
            pltpu.VMEM(inner, F32),
            pltpu.VMEM(inner, F32),
            pltpu.VMEM(inner, BF16),
            wide,
            pltpu.SemaphoreType.DMA((5,)),
            pltpu.SemaphoreType.DMA((4,)),
        ],
    )
    y, d_far_rows = after(y, d_far_rows)
    y_back = exchange(y)

    dx_own, dx_far, terms = streamed_call(
        backward_kernel,
        [shape((half, feature), BF16)] * 2 + [shape((3 * units, feature), BF16)],
        [
            down_matrix,
            d_own,
            d_far_rows,
            gate_pre,
            up_pre,
            gate_matrix,
            up_matrix,
            x_own,
            x_far_rows,
            hidden,
        ],
        [
            weight,
            pltpu.VMEM(inner, F32),
            pltpu.VMEM(inner, F32),
            weight,
            weight,
            pltpu.VMEM(inner, BF16),
            wide,
            wide,
            pltpu.VMEM(inner, BF16),
            pltpu.VMEM(inner, BF16),
            wide,
            pltpu.VMEM((2, 256, feature), BF16),
            pltpu.SemaphoreType.DMA((10,)),
            pltpu.SemaphoreType.DMA((4,)),
        ],
    )
    dx_own, dx_far, terms, y_back = after(dx_own, dx_far, terms, y_back)
    summed = lax.psum_scatter(terms, "dp", scatter_dimension=1, tiled=True)

    token_rows, grad_rows = ((tok, feature), BF16), ((tok, LANES), F32)
    work = 2 * half * tok * feature
    mixed_far, grads_far = call(
        mix_kernel, [token_rows, grad_rows], [meta, meta_far, d_far, y_back], 2 * top * work
    )
    dx_far, mixed_far, grads_far = after(dx_far, mixed_far, grads_far)
    dx_far_back = exchange(dx_far)
    mixed_far, grads_far = after(across(mixed_far), across(grads_far))

    def table(meta, came):
        return pl.pallas_call(
            functools.partial(table_kernel, top, side, capacity),
            out_shape=shape((half, tok), BF16),
            in_specs=[SMEM, VMEM, anywhere],
            out_specs=VMEM,
            compiler_params=pltpu.CompilerParams(vmem_limit_bytes=60 * 1024 * 1024),
            cost_estimate=pl.CostEstimate(flops=LONG, bytes_accessed=1, transcendentals=0),
        )(me_arr, meta, came)

    def total(table, back, *far):
        return local_call_plain(
            sum_kernel, [shape((tok, feature), BF16)], [table, back, *far], work
        )[0]

    far_table, mixed_far, grads_far, dx_far_back = after(
        table(meta_far, mixed_far), mixed_far, grads_far, dx_far_back
    )
    tokens_far, dx_own = after(total(far_table, dx_far_back), dx_own)
    dx_own_back = exchange(dx_own)
    mixed, grads = call(
        mix_last_kernel,
        [token_rows, grad_rows],
        [meta, meta_far, d_mixed, y_back, mixed_far, grads_far],
        2 * top * work,
    )
    tokens_far = across(tokens_far)
    weight_grads = (
        summed[:units].astype(F32).T[None],
        summed[units : 2 * units].astype(F32).T[None],
        summed[2 * units :].astype(F32)[None],
    )
    tokens_far, mixed, grads, *weight_grads = after(tokens_far, mixed, grads, *weight_grads)
    own_table, tokens_far, dx_own_back = after(table(meta, tokens_far), tokens_far, dx_own_back)
    d_tokens = total(own_table, dx_own_back, tokens_far)
    return (mixed, d_tokens, grads[:, :top], *weight_grads)


def solution(mesh):
    in_specs = (
        P(("dp", "expert"), None),
        P(("dp", "expert"), None),
        P(("dp", "expert"), None),
        P("expert", None, None),
        P("expert", None, None),
        P("expert", None, None),
        P(("dp", "expert"), None),
    )
    out_specs = (
        P(("dp", "expert"), None),
        P(("dp", "expert"), None),
        P(("dp", "expert"), None),
        P("expert", "dp", None),
        P("expert", "dp", None),
        P("expert", None, "dp"),
    )
    return jax.shard_map(
        on_device, mesh=mesh, in_specs=in_specs, out_specs=out_specs, check_vma=False
    )
```

```python
import functools

import jax
import jax.numpy as jnp
from jax import lax
from jax.experimental import pallas as pl
from jax.experimental.pallas import tpu as pltpu
from jax.sharding import PartitionSpec as P

BF16 = jnp.bfloat16
F32 = jnp.float32
LANES = 128
STRIP = 512
LONG = 10**11
VMEM = pl.BlockSpec(memory_space=pltpu.VMEM)
SMEM = pl.BlockSpec(memory_space=pltpu.SMEM)


def local_call(kernel, outs, me, args, flops):
    size = sum(x.size * x.dtype.itemsize for x in (*outs, *args))
    return pl.pallas_call(
        kernel,
        out_shape=outs,
        in_specs=[SMEM] + [VMEM] * len(args),
        out_specs=[VMEM] * len(outs),
        compiler_params=pltpu.CompilerParams(vmem_limit_bytes=6 * 1024 * 1024),
        cost_estimate=pl.CostEstimate(flops=flops, bytes_accessed=size, transcendentals=0),
    )(me, *args)


def local_call_plain(kernel, outs, args, flops):
    return local_call(lambda me_ref, *refs: kernel(*refs), outs, jnp.zeros((1,), jnp.int32), args, flops)


def strips(width, step=STRIP):
    return [(c, min(c + step, width)) for c in range(0, width, step)]


def slot_tables(me, metas, top, side, capacity):
    count = len(metas)
    span = count * capacity
    tok = metas[0].shape[1]
    slot = lax.broadcasted_iota(jnp.int32, (side * span, tok), 0)
    expert = ((me - lax.rem(me, side)) + slot // span).astype(F32)
    block_of = lax.rem(slot, span) // capacity
    place = lax.rem(slot, capacity).astype(F32)
    row = lax.broadcasted_iota(jnp.int32, (tok, tok), 0)
    column = lax.broadcasted_iota(jnp.int32, (tok, tok), 1)
    earlier = jnp.where(row < column, 1.0, 0.0).astype(BF16)
    tables = []
    for b in range(count):
        named = [jnp.where(metas[b][k : k + 1, :] == expert, 1.0, 0.0) for k in range(top)]
        member = functools.reduce(lambda p, q: p + q, named)
        rank = jnp.dot(member.astype(BF16), earlier, preferred_element_type=F32)
        here = rank == place
        if count > 1:
            here = here & (block_of == b)
        tables.append([jnp.where(here, part, 0.0) for part in named])
    return tables


def pick_kernel(top, side, capacity, scaled, me_ref, *refs):
    count = len(scaled)
    metas, blocks, out = refs[:count], refs[count:-1], refs[-1]
    tables = slot_tables(me_ref[0], metas, top, side, capacity)
    held = jnp.concatenate([functools.reduce(lambda p, q: p + q, ks) for ks in tables], 1)
    held = held.astype(BF16)
    gate = 0.0
    for meta, ks, has in zip(metas, tables, scaled):
        for k, part in enumerate(ks):
            if has:
                part = part * meta[top + k : top + k + 1, :]
            gate += jnp.sum(part, 1, keepdims=True)
    for c, e in strips(out.shape[1]):
        block = jnp.concatenate([ref[:, c:e] for ref in blocks], 0)
        got = jnp.dot(held, block, preferred_element_type=F32)
        out[:, c:e] = ((gate * got) if any(scaled) else got).astype(BF16)


def own_pick_kernel(top, side, capacity, me_ref, meta, x_hbm, d_hbm, out, x, d, sems):
    for load in fetch((x_hbm, d_hbm), (x, d), sems):
        load.wait()
    pick_kernel(top, side, capacity, (False, True), me_ref, meta, meta, x, d, out)


TRANSPOSED = (((0,), (0,)), ((), ()))


def picked_sum(table, back, c, e):
    return lax.dot_general(
        table.astype(BF16), back[:, c:e], TRANSPOSED, preferred_element_type=F32
    )


def table_kernel(top, side, capacity, me_ref, meta, came, out):
    (table,) = slot_tables(me_ref[0], [meta], top, side, capacity)
    out[...] = functools.reduce(lambda p, q: p + q, table).astype(BF16)


def sum_kernel(table, back, *refs):
    out = refs[-1]
    for c, e in strips(out.shape[1]):
        got = picked_sum(table[...], back, c, e)
        for far in refs[:-1]:
            got += far[:, c:e].astype(F32)
        out[:, c:e] = got.astype(BF16)


def mix(top, table, meta, blocks, back, outs, grads, fars=(), far_grads=None):
    tok = meta.shape[1]
    gates = [meta[top + k : top + k + 1, :] for k in range(top)]
    gates = [jnp.transpose(jnp.broadcast_to(g, (8, tok)))[:, :1] for g in gates]
    sums = [jnp.zeros((tok, 1), F32) for _ in range(top)]
    for c, e in strips(back.shape[1]):
        cotangent = jnp.concatenate([ref[:, c:e] for ref in blocks], 0).astype(F32)
        mixed = 0.0
        if fars:
            mixed = jnp.concatenate([ref[:, c:e] for ref in fars], 0).astype(F32)
        for k in range(top):
            got = picked_sum(table[k], back, c, e)
            mixed += gates[k] * got
            sums[k] += jnp.sum(cotangent * got, 1, keepdims=True)
        for n, out in enumerate(outs):
            rows = out.shape[0]
            out[:, c:e] = mixed[n * rows : (n + 1) * rows].astype(BF16)
    lane = lax.broadcasted_iota(jnp.int32, (tok, LANES), 1)
    grad = jnp.zeros((tok, LANES), F32)
    for k in range(top):
        grad += jnp.where(lane == k, sums[k], 0.0)
    grad = jnp.transpose(grad)[: grads.shape[0]]
    grads[...] = grad if far_grads is None else grad + far_grads[...]


def mix_kernel(
    top, side, capacity, me_ref, meta, meta_far, block, back, out, grads
):
    tables = slot_tables(me_ref[0], [meta, meta_far], top, side, capacity)
    mix(top, tables[1], meta_far, (block,), back, (out,), grads)


def mix_last_kernel(
    top, side, capacity, me_ref, meta, meta_far, block, back, far, far_grads, out, grads
):
    tables = slot_tables(me_ref[0], [meta, meta_far], top, side, capacity)
    mix(top, tables[0], meta, (block,), back, (out,), grads, (far,), far_grads)


def fetch(sources, targets, sems):
    copies = []
    for n, (source, target) in enumerate(zip(sources, targets)):
        copies.append(pltpu.make_async_copy(source, target, sems.at[n]))
        copies[n].start()
    return copies


ACROSS_LAST = (((1,), (1,)), ((), ()))


def forward_kernel(side, *refs):
    sources, outs = refs[:5], refs[5:9]
    wg, wu, wd, x, gate, up, hidden, y, sems, out_sems = refs[9:]
    rows, feature = x.shape
    units, half = gate.shape[1], rows // 2
    targets = [wg, x.at[pl.ds(0, half)], x.at[pl.ds(half, half)], wu, wd]
    loads = fetch(sources, targets, sems)
    for load in loads[:3]:
        load.wait()
    for c, e in strips(units, 256):
        gate[:, c:e] = lax.dot_general(
            x[...], wg[c:e, :], ACROSS_LAST, preferred_element_type=F32
        )
    loads[3].wait()
    for c, e in strips(units, 256):
        got = lax.dot_general(x[...], wu[c:e, :], ACROSS_LAST, preferred_element_type=F32)
        up[:, c:e] = got
        pre = gate[:, c:e]
        hidden[:, c:e] = (pre * (1.0 / (1.0 + jnp.exp(-pre))) * got).astype(BF16)
    copies = [
        pltpu.make_async_copy(source, out, out_sems.at[n])
        for n, (source, out) in enumerate(zip((gate, up, hidden, y), outs))
    ]
    for copy in copies[:3]:
        copy.start()
    loads[4].wait()
    for c, e in strips(feature):
        got = jnp.dot(hidden[...], wd[:, c:e], preferred_element_type=F32)
        pair = [
            part.reshape(side, 1, half // side, e - c) for part in (got[:half], got[half:])
        ]
        y[:, c:e] = jnp.concatenate(pair, 1).reshape(rows, e - c).astype(BF16)
    copies[3].start()
    for copy in copies:
        copy.wait()


def backward_kernel(*refs):
    sources, (own_out, far_out, terms_out) = refs[:10], refs[10:13]
    wd, gate, up, wg, wu, hidden, d, x, gg, gu, dx, tiles, sems, out_sems = refs[13:]
    rows, feature = d.shape
    units, half = gate.shape[1], rows // 2
    first, second = pl.ds(0, half), pl.ds(half, half)
    targets = [wd, d.at[first], d.at[second], gate, up, wg, wu, x.at[first], x.at[second], hidden]
    loads = fetch(sources, targets, sems)
    for load in loads[:5]:
        load.wait()
    for c, e in strips(units, 256):
        back = lax.dot_general(d[...], wd[c:e, :], ACROSS_LAST, preferred_element_type=F32)
        pre = gate[:, c:e]
        sig = 1.0 / (1.0 + jnp.exp(-pre))
        gg[:, c:e] = (back * up[:, c:e] * (sig * (1.0 + pre * (1.0 - sig)))).astype(BF16)
        gu[:, c:e] = (back * (pre * sig)).astype(BF16)
    loads[5].wait()
    loads[6].wait()
    for c, e in strips(feature):
        got = jnp.dot(gg[...], wg[:, c:e], preferred_element_type=F32)
        got += jnp.dot(gu[...], wu[:, c:e], preferred_element_type=F32)
        dx[:, c:e] = got.astype(BF16)
    dx_copies = [
        pltpu.make_async_copy(dx.at[second], far_out, out_sems.at[2]),
        pltpu.make_async_copy(dx.at[first], own_out, out_sems.at[3]),
    ]
    for copy in dx_copies:
        copy.start()
    for load in loads[7:]:
        load.wait()
    copies = []
    for n, (left, right) in enumerate(((gg, x), (gu, x), (hidden, d))):
        for r, t in strips(units, tiles.shape[1]):
            slot = len(copies) % 2
            if len(copies) > 1:
                copies[-2].wait()
            for c, e in strips(feature, 1024):
                tiles[slot, : t - r, c:e] = lax.dot_general(
                    left[:, r:t], right[:, c:e], TRANSPOSED, preferred_element_type=F32
                ).astype(BF16)
            copy = pltpu.make_async_copy(
                tiles.at[slot, pl.ds(0, t - r)],
                terms_out.at[pl.ds(n * units + r, t - r)],
                out_sems.at[slot],
            )
            copy.start()
            copies.append(copy)
    for copy in (*copies[-2:], *dx_copies):
        copy.wait()


def streamed_call(kernel, outs, args, scratch):
    anywhere = pl.BlockSpec(memory_space=pltpu.HBM)
    return pl.pallas_call(
        kernel,
        out_shape=outs,
        in_specs=[pl.BlockSpec(memory_space=pl.ANY)] * len(args),
        out_specs=[anywhere] * len(outs),
        scratch_shapes=scratch,
        compiler_params=pltpu.CompilerParams(vmem_limit_bytes=60 * 1024 * 1024),
        cost_estimate=pl.CostEstimate(flops=1, bytes_accessed=1, transcendentals=0),
    )(*args)


def on_device(tokens, expert_ids, gate_prob, w_gate, w_up, w_down, d_mixed):
    tok, feature = tokens.shape
    top = expert_ids.shape[1]
    experts = lax.axis_size("expert")
    capacity = max(2, 2 * tok * top // experts)
    side = experts // 2
    half = side * capacity
    me = lax.axis_index("expert")
    me_arr = me[None]
    sets = [[h * side + p for p in range(side)] for h in range(2)]
    shape = jax.ShapeDtypeStruct

    def across(value):
        return lax.ppermute(value, "expert", [(e, (e + side) % experts) for e in range(experts)])

    def exchange(value):
        shaped = value.reshape(side, value.shape[0] // side, value.shape[1])
        got = lax.all_to_all(shaped, "expert", 0, 0, axis_index_groups=sets, tiled=True)
        return got.reshape(value.shape)

    def after(value, *earlier):
        return lax.optimization_barrier((value, *earlier))

    def call(kernel, outs, args, flops):
        return local_call(
            functools.partial(kernel, top, side, capacity),
            [shape(*out) for out in outs],
            me_arr,
            args,
            flops,
        )

    def pick(metas, blocks, scaled):
        count = len(metas)
        return local_call(
            functools.partial(pick_kernel, top, side, capacity, scaled),
            [shape((count * half, feature), BF16)],
            me_arr,
            [*metas, *blocks],
            LONG,
        )[0]

    meta = jnp.concatenate([expert_ids.T.astype(F32), gate_prob.T], 0)
    anywhere = pl.BlockSpec(memory_space=pltpu.HBM)
    picked = pl.pallas_call(
        functools.partial(own_pick_kernel, top, side, capacity),
        out_shape=shape((2 * half, feature), BF16),
        in_specs=[SMEM, VMEM, anywhere, anywhere],
        out_specs=VMEM,
        scratch_shapes=[
            pltpu.VMEM((tok, feature), BF16),
            pltpu.VMEM((tok, feature), BF16),
            pltpu.SemaphoreType.DMA((2,)),
        ],
        compiler_params=pltpu.CompilerParams(vmem_limit_bytes=60 * 1024 * 1024),
        cost_estimate=pl.CostEstimate(
            flops=8 * half * tok * feature, bytes_accessed=1, transcendentals=0
        ),
    )(me_arr, meta, tokens, d_mixed)
    own = exchange(picked)
    own = own.reshape(side, 2, capacity, feature)
    x_far, meta_far = after(across(tokens), across(meta))
    d_late, x_far = after(d_mixed, x_far)
    d_far = across(d_late)
    x_picked, own = after(pick([meta_far], [x_far], (False,)), own)
    x_far_rows = exchange(x_picked)
    d_picked, x_far_rows = after(pick([meta_far], [d_far], (True,)), x_far_rows)
    d_far_rows = exchange(d_picked)
    x_own, d_own = (own[:, n].reshape(half, feature) for n in range(2))

    gate_matrix, up_matrix, down_matrix = w_gate[0].T, w_up[0].T, w_down[0]
    units, n_rows = gate_matrix.shape[0], 2 * half
    weight = pltpu.VMEM((units, feature), BF16)
    inner, wide = (n_rows, units), pltpu.VMEM((n_rows, feature), BF16)
    gate_pre, up_pre, hidden, y = streamed_call(
        functools.partial(forward_kernel, side),
        [shape(inner, F32), shape(inner, F32), shape(inner, BF16), shape((n_rows, feature), BF16)],
        [gate_matrix, x_own, x_far_rows, up_matrix, down_matrix],
        [
            *[weight] * 3,
            wide,
            pltpu.VMEM(inner, F32),
            pltpu.VMEM(inner, F32),
            pltpu.VMEM(inner, BF16),
            wide,
            pltpu.SemaphoreType.DMA((5,)),
            pltpu.SemaphoreType.DMA((4,)),
        ],
    )
    y, d_far_rows = after(y, d_far_rows)
    y_back = exchange(y)

    dx_own, dx_far, terms = streamed_call(
        backward_kernel,
        [shape((half, feature), BF16)] * 2 + [shape((3 * units, feature), BF16)],
        [
            down_matrix,
            d_own,
            d_far_rows,
            gate_pre,
            up_pre,
            gate_matrix,
            up_matrix,
            x_own,
            x_far_rows,
            hidden,
        ],
        [
            weight,
            pltpu.VMEM(inner, F32),
            pltpu.VMEM(inner, F32),
            weight,
            weight,
            pltpu.VMEM(inner, BF16),
            wide,
            wide,
            pltpu.VMEM(inner, BF16),
            pltpu.VMEM(inner, BF16),
            wide,
            pltpu.VMEM((2, 256, feature), BF16),
            pltpu.SemaphoreType.DMA((10,)),
            pltpu.SemaphoreType.DMA((4,)),
        ],
    )
    dx_own, dx_far, terms, y_back = after(dx_own, dx_far, terms, y_back)
    summed = lax.psum_scatter(terms, "dp", scatter_dimension=1, tiled=True)

    token_rows, grad_rows = ((tok, feature), BF16), ((8, tok), F32)
    work = 2 * half * tok * feature
    mixed_far, grads_far = call(
        mix_kernel, [token_rows, grad_rows], [meta, meta_far, d_far, y_back], 2 * top * work
    )
    dx_far, mixed_far, grads_far = after(dx_far, mixed_far, grads_far)
    dx_far_back = exchange(dx_far)
    mixed_far, grads_far = after(across(mixed_far), across(grads_far))

    def table(meta, came):
        return pl.pallas_call(
            functools.partial(table_kernel, top, side, capacity),
            out_shape=shape((half, tok), BF16),
            in_specs=[SMEM, VMEM, anywhere],
            out_specs=VMEM,
            compiler_params=pltpu.CompilerParams(vmem_limit_bytes=60 * 1024 * 1024),
            cost_estimate=pl.CostEstimate(flops=LONG, bytes_accessed=1, transcendentals=0),
        )(me_arr, meta, came)

    def total(table, back, *far):
        return local_call_plain(
            sum_kernel, [shape((tok, feature), BF16)], [table, back, *far], work
        )[0]

    far_table, mixed_far, grads_far, dx_far_back = after(
        table(meta_far, mixed_far), mixed_far, grads_far, dx_far_back
    )
    tokens_far, dx_own = after(total(far_table, dx_far_back), dx_own)
    dx_own_back = exchange(dx_own)
    mixed, grads = call(
        mix_last_kernel,
        [token_rows, grad_rows],
        [meta, meta_far, d_mixed, y_back, mixed_far, grads_far],
        2 * top * work,
    )
    tokens_far = across(tokens_far)
    weight_grads = (
        summed[:units].astype(F32).T[None],
        summed[units : 2 * units].astype(F32).T[None],
        summed[2 * units :].astype(F32)[None],
    )
    tokens_far, mixed, grads, *weight_grads = after(tokens_far, mixed, grads, *weight_grads)
    own_table, tokens_far, dx_own_back = after(table(meta, tokens_far), tokens_far, dx_own_back)
    d_tokens = total(own_table, dx_own_back, tokens_far)
    return (mixed, d_tokens, grads[:top].T, *weight_grads)


def solution(mesh):
    in_specs = (
        P(("dp", "expert"), None),
        P(("dp", "expert"), None),
        P(("dp", "expert"), None),
        P("expert", None, None),
        P("expert", None, None),
        P("expert", None, None),
        P(("dp", "expert"), None),
    )
    out_specs = (
        P(("dp", "expert"), None),
        P(("dp", "expert"), None),
        P(("dp", "expert"), None),
        P("expert", "dp", None),
        P("expert", "dp", None),
        P("expert", None, "dp"),
    )
    return jax.shard_map(
        on_device, mesh=mesh, in_specs=in_specs, out_specs=out_specs, check_vma=False
    )
```

```python
import functools

import jax
import jax.numpy as jnp
from jax import lax
from jax.experimental import pallas as pl
from jax.experimental.pallas import tpu as pltpu
from jax.sharding import PartitionSpec as P

BF16 = jnp.bfloat16
F32 = jnp.float32
LANES = 128
STRIP = 512
LONG = 10**11
VMEM = pl.BlockSpec(memory_space=pltpu.VMEM)
SMEM = pl.BlockSpec(memory_space=pltpu.SMEM)


def local_call(kernel, outs, me, args, flops):
    size = sum(x.size * x.dtype.itemsize for x in (*outs, *args))
    return pl.pallas_call(
        kernel,
        out_shape=outs,
        in_specs=[SMEM] + [VMEM] * len(args),
        out_specs=[VMEM] * len(outs),
        compiler_params=pltpu.CompilerParams(vmem_limit_bytes=6 * 1024 * 1024),
        cost_estimate=pl.CostEstimate(flops=flops, bytes_accessed=size, transcendentals=0),
    )(me, *args)


def local_call_plain(kernel, outs, args, flops):
    return local_call(lambda me_ref, *refs: kernel(*refs), outs, jnp.zeros((1,), jnp.int32), args, flops)


def strips(width, step=STRIP):
    return [(c, min(c + step, width)) for c in range(0, width, step)]


def slot_tables(me, metas, top, side, capacity):
    count = len(metas)
    span = count * capacity
    tok = metas[0].shape[1]
    slot = lax.broadcasted_iota(jnp.int32, (side * span, tok), 0)
    expert = ((me - lax.rem(me, side)) + slot // span).astype(F32)
    block_of = lax.rem(slot, span) // capacity
    place = lax.rem(slot, capacity).astype(F32)
    row = lax.broadcasted_iota(jnp.int32, (tok, tok), 0)
    column = lax.broadcasted_iota(jnp.int32, (tok, tok), 1)
    earlier = jnp.where(row < column, 1.0, 0.0).astype(BF16)
    tables = []
    for b in range(count):
        named = [jnp.where(metas[b][k : k + 1, :] == expert, 1.0, 0.0) for k in range(top)]
        member = functools.reduce(lambda p, q: p + q, named)
        rank = jnp.dot(member.astype(BF16), earlier, preferred_element_type=F32)
        here = rank == place
        if count > 1:
            here = here & (block_of == b)
        tables.append([jnp.where(here, part, 0.0) for part in named])
    return tables


def pick_kernel(top, side, capacity, scaled, me_ref, *refs, loads=()):
    count = len(scaled)
    metas, blocks, out = refs[:count], refs[count:-1], refs[-1]
    tables = slot_tables(me_ref[0], metas, top, side, capacity)
    held = jnp.concatenate([functools.reduce(lambda p, q: p + q, ks) for ks in tables], 1)
    held = held.astype(BF16)
    gate = 0.0
    for meta, ks, has in zip(metas, tables, scaled):
        for k, part in enumerate(ks):
            if has:
                part = part * meta[top + k : top + k + 1, :]
            gate += jnp.sum(part, 1, keepdims=True)
    for load in loads:
        load.wait()
    for c, e in strips(out.shape[1]):
        block = jnp.concatenate([ref[:, c:e] for ref in blocks], 0)
        got = jnp.dot(held, block, preferred_element_type=F32)
        out[:, c:e] = ((gate * got) if any(scaled) else got).astype(BF16)


def own_pick_kernel(top, side, capacity, me_ref, meta, x_hbm, d_hbm, out, x, d, sems):
    loads = fetch((x_hbm, d_hbm), (x, d), sems)
    pick_kernel(
        top, side, capacity, (False, True), me_ref, meta, meta, x, d, out, loads=loads
    )


TRANSPOSED = (((0,), (0,)), ((), ()))


def picked_sum(table, back, c, e):
    return lax.dot_general(
        table.astype(BF16), back[:, c:e], TRANSPOSED, preferred_element_type=F32
    )


def table_kernel(top, side, capacity, me_ref, meta, came, out):
    (table,) = slot_tables(me_ref[0], [meta], top, side, capacity)
    out[...] = functools.reduce(lambda p, q: p + q, table).astype(BF16)


def sum_kernel(table, back, *refs):
    out = refs[-1]
    for c, e in strips(out.shape[1]):
        got = picked_sum(table[...], back, c, e)
        for far in refs[:-1]:
            got += far[:, c:e].astype(F32)
        out[:, c:e] = got.astype(BF16)


def mix(top, table, meta, blocks, back, outs, grads, fars=(), far_grads=None):
    tok = meta.shape[1]
    gates = [meta[top + k : top + k + 1, :] for k in range(top)]
    gates = [jnp.transpose(jnp.broadcast_to(g, (8, tok)))[:, :1] for g in gates]
    sums = [jnp.zeros((tok, 1), F32) for _ in range(top)]
    for c, e in strips(back.shape[1]):
        cotangent = jnp.concatenate([ref[:, c:e] for ref in blocks], 0).astype(F32)
        mixed = 0.0
        if fars:
            mixed = jnp.concatenate([ref[:, c:e] for ref in fars], 0).astype(F32)
        for k in range(top):
            got = picked_sum(table[k], back, c, e)
            mixed += gates[k] * got
            sums[k] += jnp.sum(cotangent * got, 1, keepdims=True)
        for n, out in enumerate(outs):
            rows = out.shape[0]
            out[:, c:e] = mixed[n * rows : (n + 1) * rows].astype(BF16)
    lane = lax.broadcasted_iota(jnp.int32, (tok, LANES), 1)
    grad = jnp.zeros((tok, LANES), F32)
    for k in range(top):
        grad += jnp.where(lane == k, sums[k], 0.0)
    grad = jnp.transpose(grad)[: grads.shape[0]]
    grads[...] = grad if far_grads is None else grad + far_grads[...]


def mix_kernel(
    top, side, capacity, me_ref, meta, meta_far, block, back, out, grads
):
    tables = slot_tables(me_ref[0], [meta, meta_far], top, side, capacity)
    mix(top, tables[1], meta_far, (block,), back, (out,), grads)


def mix_last_kernel(
    top, side, capacity, me_ref, meta, meta_far, block, back, far, far_grads, out, grads
):
    tables = slot_tables(me_ref[0], [meta, meta_far], top, side, capacity)
    mix(top, tables[0], meta, (block,), back, (out,), grads, (far,), far_grads)


def fetch(sources, targets, sems):
    copies = []
    for n, (source, target) in enumerate(zip(sources, targets)):
        copies.append(pltpu.make_async_copy(source, target, sems.at[n]))
        copies[n].start()
    return copies


ACROSS_LAST = (((1,), (1,)), ((), ()))


def forward_kernel(side, *refs):
    sources, outs = refs[:5], refs[5:9]
    wg, wu, wd, x, gate, up, hidden, y, sems, out_sems = refs[9:]
    rows, feature = x.shape
    units, half = gate.shape[1], rows // 2
    targets = [wg, x.at[pl.ds(0, half)], x.at[pl.ds(half, half)], wu, wd]
    loads = fetch(sources, targets, sems)
    for load in loads[:3]:
        load.wait()
    for c, e in strips(units, 256):
        gate[:, c:e] = lax.dot_general(
            x[...], wg[c:e, :], ACROSS_LAST, preferred_element_type=F32
        )
    loads[3].wait()
    for c, e in strips(units, 256):
        got = lax.dot_general(x[...], wu[c:e, :], ACROSS_LAST, preferred_element_type=F32)
        up[:, c:e] = got
        pre = gate[:, c:e]
        hidden[:, c:e] = (pre * (1.0 / (1.0 + jnp.exp(-pre))) * got).astype(BF16)
    copies = [
        pltpu.make_async_copy(source, out, out_sems.at[n])
        for n, (source, out) in enumerate(zip((gate, up, hidden, y), outs))
    ]
    for copy in copies[:3]:
        copy.start()
    loads[4].wait()
    for c, e in strips(feature):
        got = jnp.dot(hidden[...], wd[:, c:e], preferred_element_type=F32)
        pair = [
            part.reshape(side, 1, half // side, e - c) for part in (got[:half], got[half:])
        ]
        y[:, c:e] = jnp.concatenate(pair, 1).reshape(rows, e - c).astype(BF16)
    copies[3].start()
    for copy in copies:
        copy.wait()


def backward_kernel(*refs):
    sources, (own_out, far_out, terms_out) = refs[:10], refs[10:13]
    wd, gate, up, wg, wu, hidden, d, x, gg, gu, dx, tiles, sems, out_sems = refs[13:]
    rows, feature = d.shape
    units, half = gate.shape[1], rows // 2
    first, second = pl.ds(0, half), pl.ds(half, half)
    targets = [wd, d.at[first], d.at[second], gate, up, wg, wu, x.at[first], x.at[second], hidden]
    loads = fetch(sources, targets, sems)
    for load in loads[:5]:
        load.wait()
    for c, e in strips(units, 256):
        back = lax.dot_general(d[...], wd[c:e, :], ACROSS_LAST, preferred_element_type=F32)
        pre = gate[:, c:e]
        sig = 1.0 / (1.0 + jnp.exp(-pre))
        gg[:, c:e] = (back * up[:, c:e] * (sig * (1.0 + pre * (1.0 - sig)))).astype(BF16)
        gu[:, c:e] = (back * (pre * sig)).astype(BF16)
    loads[5].wait()
    loads[6].wait()
    for c, e in strips(feature):
        got = jnp.dot(gg[...], wg[:, c:e], preferred_element_type=F32)
        got += jnp.dot(gu[...], wu[:, c:e], preferred_element_type=F32)
        dx[:, c:e] = got.astype(BF16)
    dx_copies = [
        pltpu.make_async_copy(dx.at[second], far_out, out_sems.at[2]),
        pltpu.make_async_copy(dx.at[first], own_out, out_sems.at[3]),
    ]
    for copy in dx_copies:
        copy.start()
    for load in loads[7:]:
        load.wait()
    copies = []
    for n, (left, right) in enumerate(((gg, x), (gu, x), (hidden, d))):
        for r, t in strips(units, tiles.shape[1]):
            slot = len(copies) % 2
            if len(copies) > 1:
                copies[-2].wait()
            for c, e in strips(feature, 1024):
                tiles[slot, : t - r, c:e] = lax.dot_general(
                    left[:, r:t], right[:, c:e], TRANSPOSED, preferred_element_type=F32
                ).astype(BF16)
            copy = pltpu.make_async_copy(
                tiles.at[slot, pl.ds(0, t - r)],
                terms_out.at[pl.ds(n * units + r, t - r)],
                out_sems.at[slot],
            )
            copy.start()
            copies.append(copy)
    for copy in (*copies[-2:], *dx_copies):
        copy.wait()


def streamed_call(kernel, outs, args, scratch):
    anywhere = pl.BlockSpec(memory_space=pltpu.HBM)
    return pl.pallas_call(
        kernel,
        out_shape=outs,
        in_specs=[pl.BlockSpec(memory_space=pl.ANY)] * len(args),
        out_specs=[anywhere] * len(outs),
        scratch_shapes=scratch,
        compiler_params=pltpu.CompilerParams(vmem_limit_bytes=60 * 1024 * 1024),
        cost_estimate=pl.CostEstimate(flops=1, bytes_accessed=1, transcendentals=0),
    )(*args)


def on_device(tokens, expert_ids, gate_prob, w_gate, w_up, w_down, d_mixed):
    tok, feature = tokens.shape
    top = expert_ids.shape[1]
    experts = lax.axis_size("expert")
    capacity = max(2, 2 * tok * top // experts)
    side = experts // 2
    half = side * capacity
    me = lax.axis_index("expert")
    me_arr = me[None]
    sets = [[h * side + p for p in range(side)] for h in range(2)]
    shape = jax.ShapeDtypeStruct

    def across(value):
        return lax.ppermute(value, "expert", [(e, (e + side) % experts) for e in range(experts)])

    def exchange(value):
        shaped = value.reshape(side, value.shape[0] // side, value.shape[1])
        got = lax.all_to_all(shaped, "expert", 0, 0, axis_index_groups=sets, tiled=True)
        return got.reshape(value.shape)

    def after(value, *earlier):
        return lax.optimization_barrier((value, *earlier))

    def call(kernel, outs, args, flops):
        return local_call(
            functools.partial(kernel, top, side, capacity),
            [shape(*out) for out in outs],
            me_arr,
            args,
            flops,
        )

    def pick(metas, blocks, scaled):
        count = len(metas)
        return local_call(
            functools.partial(pick_kernel, top, side, capacity, scaled),
            [shape((count * half, feature), BF16)],
            me_arr,
            [*metas, *blocks],
            LONG,
        )[0]

    meta = jnp.concatenate([expert_ids.T.astype(F32), gate_prob.T], 0)
    anywhere = pl.BlockSpec(memory_space=pltpu.HBM)
    picked = pl.pallas_call(
        functools.partial(own_pick_kernel, top, side, capacity),
        out_shape=shape((2 * half, feature), BF16),
        in_specs=[SMEM, VMEM, anywhere, anywhere],
        out_specs=VMEM,
        scratch_shapes=[
            pltpu.VMEM((tok, feature), BF16),
            pltpu.VMEM((tok, feature), BF16),
            pltpu.SemaphoreType.DMA((2,)),
        ],
        compiler_params=pltpu.CompilerParams(vmem_limit_bytes=60 * 1024 * 1024),
        cost_estimate=pl.CostEstimate(
            flops=8 * half * tok * feature, bytes_accessed=1, transcendentals=0
        ),
    )(me_arr, meta, tokens, d_mixed)
    own = exchange(picked)
    own = own.reshape(side, 2, capacity, feature)
    x_far, meta_far = after(across(tokens), across(meta))
    x_picked, own = after(pick([meta_far], [x_far], (False,)), own)
    d_late, own = after(d_mixed, own)
    d_far = across(d_late)
    x_far_rows = exchange(x_picked)
    x_own, d_own = (own[:, n].reshape(half, feature) for n in range(2))
    d_picked, x_own, d_own, x_far_rows = after(
        pick([meta_far], [d_far], (True,)), x_own, d_own, x_far_rows
    )
    d_far_rows = exchange(d_picked)

    gate_matrix, up_matrix, down_matrix = w_gate[0].T, w_up[0].T, w_down[0]
    units, n_rows = gate_matrix.shape[0], 2 * half
    weight = pltpu.VMEM((units, feature), BF16)
    inner, wide = (n_rows, units), pltpu.VMEM((n_rows, feature), BF16)
    gate_pre, up_pre, hidden, y = streamed_call(
        functools.partial(forward_kernel, side),
        [shape(inner, F32), shape(inner, F32), shape(inner, BF16), shape((n_rows, feature), BF16)],
        [gate_matrix, x_own, x_far_rows, up_matrix, down_matrix],
        [
            *[weight] * 3,
            wide,
            pltpu.VMEM(inner, F32),
            pltpu.VMEM(inner, F32),
            pltpu.VMEM(inner, BF16),
            wide,
            pltpu.SemaphoreType.DMA((5,)),
            pltpu.SemaphoreType.DMA((4,)),
        ],
    )
    y, d_far_rows = after(y, d_far_rows)
    y_back = exchange(y)

    dx_own, dx_far, terms = streamed_call(
        backward_kernel,
        [shape((half, feature), BF16)] * 2 + [shape((3 * units, feature), BF16)],
        [
            down_matrix,
            d_own,
            d_far_rows,
            gate_pre,
            up_pre,
            gate_matrix,
            up_matrix,
            x_own,
            x_far_rows,
            hidden,
        ],
        [
            weight,
            pltpu.VMEM(inner, F32),
            pltpu.VMEM(inner, F32),
            weight,
            weight,
            pltpu.VMEM(inner, BF16),
            wide,
            wide,
            pltpu.VMEM(inner, BF16),
            pltpu.VMEM(inner, BF16),
            wide,
            pltpu.VMEM((2, 256, feature), BF16),
            pltpu.SemaphoreType.DMA((10,)),
            pltpu.SemaphoreType.DMA((4,)),
        ],
    )
    dx_own, dx_far, terms, y_back = after(dx_own, dx_far, terms, y_back)
    summed = lax.psum_scatter(terms, "dp", scatter_dimension=1, tiled=True)

    token_rows, grad_rows = ((tok, feature), BF16), ((8, tok), F32)
    work = 2 * half * tok * feature
    mixed_far, grads_far = call(
        mix_kernel, [token_rows, grad_rows], [meta, meta_far, d_far, y_back], 2 * top * work
    )
    dx_far, mixed_far, grads_far = after(dx_far, mixed_far, grads_far)
    dx_far_back = exchange(dx_far)
    mixed_far, grads_far = after(across(mixed_far), across(grads_far))

    def table(meta, came):
        return pl.pallas_call(
            functools.partial(table_kernel, top, side, capacity),
            out_shape=shape((half, tok), BF16),
            in_specs=[SMEM, VMEM, anywhere],
            out_specs=VMEM,
            compiler_params=pltpu.CompilerParams(vmem_limit_bytes=60 * 1024 * 1024),
            cost_estimate=pl.CostEstimate(flops=LONG, bytes_accessed=1, transcendentals=0),
        )(me_arr, meta, came)

    def total(table, back, *far):
        return local_call_plain(
            sum_kernel, [shape((tok, feature), BF16)], [table, back, *far], work
        )[0]

    far_table, mixed_far, grads_far, dx_far_back = after(
        table(meta_far, mixed_far), mixed_far, grads_far, dx_far_back
    )
    tokens_far, dx_own = after(total(far_table, dx_far_back), dx_own)
    dx_own_back = exchange(dx_own)
    mixed, grads = call(
        mix_last_kernel,
        [token_rows, grad_rows],
        [meta, meta_far, d_mixed, y_back, mixed_far, grads_far],
        2 * top * work,
    )
    tokens_far = across(tokens_far)
    weight_grads = (
        summed[:units].astype(F32).T[None],
        summed[units : 2 * units].astype(F32).T[None],
        summed[2 * units :].astype(F32)[None],
    )
    tokens_far, mixed, grads, *weight_grads = after(tokens_far, mixed, grads, *weight_grads)
    own_table, tokens_far, dx_own_back = after(table(meta, tokens_far), tokens_far, dx_own_back)
    d_tokens = total(own_table, dx_own_back, tokens_far)
    return (mixed, d_tokens, grads[:top].T, *weight_grads)


def solution(mesh):
    in_specs = (
        P(("dp", "expert"), None),
        P(("dp", "expert"), None),
        P(("dp", "expert"), None),
        P("expert", None, None),
        P("expert", None, None),
        P("expert", None, None),
        P(("dp", "expert"), None),
    )
    out_specs = (
        P(("dp", "expert"), None),
        P(("dp", "expert"), None),
        P(("dp", "expert"), None),
        P("expert", "dp", None),
        P("expert", "dp", None),
        P("expert", None, "dp"),
    )
    return jax.shard_map(
        on_device, mesh=mesh, in_specs=in_specs, out_specs=out_specs, check_vma=False
    )
```

```python
import functools

import jax
import jax.numpy as jnp
from jax import lax
from jax.experimental import pallas as pl
from jax.experimental.pallas import tpu as pltpu
from jax.sharding import PartitionSpec as P

BF16 = jnp.bfloat16
F32 = jnp.float32
LANES = 128
STRIP = 512
LONG = 10**11
VMEM = pl.BlockSpec(memory_space=pltpu.VMEM)
SMEM = pl.BlockSpec(memory_space=pltpu.SMEM)


def local_call(kernel, outs, me, args, flops):
    size = sum(x.size * x.dtype.itemsize for x in (*outs, *args))
    return pl.pallas_call(
        kernel,
        out_shape=outs,
        in_specs=[SMEM] + [VMEM] * len(args),
        out_specs=[VMEM] * len(outs),
        compiler_params=pltpu.CompilerParams(vmem_limit_bytes=6 * 1024 * 1024),
        cost_estimate=pl.CostEstimate(flops=flops, bytes_accessed=size, transcendentals=0),
    )(me, *args)


def local_call_plain(kernel, outs, args, flops):
    return local_call(lambda me_ref, *refs: kernel(*refs), outs, jnp.zeros((1,), jnp.int32), args, flops)


def strips(width, step=STRIP):
    return [(c, min(c + step, width)) for c in range(0, width, step)]


def slot_tables(me, metas, top, side, capacity):
    count = len(metas)
    span = count * capacity
    tok = metas[0].shape[1]
    slot = lax.broadcasted_iota(jnp.int32, (side * span, tok), 0)
    expert = ((me - lax.rem(me, side)) + slot // span).astype(F32)
    block_of = lax.rem(slot, span) // capacity
    place = lax.rem(slot, capacity).astype(F32)
    row = lax.broadcasted_iota(jnp.int32, (tok, tok), 0)
    column = lax.broadcasted_iota(jnp.int32, (tok, tok), 1)
    earlier = jnp.where(row < column, 1.0, 0.0).astype(BF16)
    tables = []
    for b in range(count):
        named = [jnp.where(metas[b][k : k + 1, :] == expert, 1.0, 0.0) for k in range(top)]
        member = functools.reduce(lambda p, q: p + q, named)
        rank = jnp.dot(member.astype(BF16), earlier, preferred_element_type=F32)
        here = rank == place
        if count > 1:
            here = here & (block_of == b)
        tables.append([jnp.where(here, part, 0.0) for part in named])
    return tables


def pick_kernel(top, side, capacity, scaled, me_ref, *refs, loads=()):
    count = len(scaled)
    metas, blocks, out = refs[:count], refs[count:-1], refs[-1]
    tables = slot_tables(me_ref[0], metas, top, side, capacity)
    held = jnp.concatenate([functools.reduce(lambda p, q: p + q, ks) for ks in tables], 1)
    held = held.astype(BF16)
    gate = 0.0
    for meta, ks, has in zip(metas, tables, scaled):
        for k, part in enumerate(ks):
            if has:
                part = part * meta[top + k : top + k + 1, :]
            gate += jnp.sum(part, 1, keepdims=True)
    for load in loads:
        load.wait()
    for c, e in strips(out.shape[1]):
        block = jnp.concatenate([ref[:, c:e] for ref in blocks], 0)
        got = jnp.dot(held, block, preferred_element_type=F32)
        out[:, c:e] = ((gate * got) if any(scaled) else got).astype(BF16)


def own_pick_kernel(top, side, capacity, me_ref, meta, x_hbm, d_hbm, out, x, d, sems):
    loads = fetch((x_hbm, d_hbm), (x, d), sems)
    pick_kernel(
        top, side, capacity, (False, True), me_ref, meta, meta, x, d, out, loads=loads
    )


TRANSPOSED = (((0,), (0,)), ((), ()))


def picked_sum(table, back, c, e):
    return lax.dot_general(
        table.astype(BF16), back[:, c:e], TRANSPOSED, preferred_element_type=F32
    )


def table_kernel(top, side, capacity, me_ref, meta, came, out):
    (table,) = slot_tables(me_ref[0], [meta], top, side, capacity)
    out[...] = functools.reduce(lambda p, q: p + q, table).astype(BF16)


def sum_kernel(table, back, *refs):
    out = refs[-1]
    for c, e in strips(out.shape[1]):
        got = picked_sum(table[...], back, c, e)
        for far in refs[:-1]:
            got += far[:, c:e].astype(F32)
        out[:, c:e] = got.astype(BF16)


def mix(top, table, meta, blocks, back, outs, grads, fars=(), far_grads=None):
    tok = meta.shape[1]
    gates = [meta[top + k : top + k + 1, :] for k in range(top)]
    gates = [jnp.transpose(jnp.broadcast_to(g, (8, tok)))[:, :1] for g in gates]
    sums = [jnp.zeros((tok, 1), F32) for _ in range(top)]
    for c, e in strips(back.shape[1]):
        cotangent = jnp.concatenate([ref[:, c:e] for ref in blocks], 0).astype(F32)
        mixed = 0.0
        if fars:
            mixed = jnp.concatenate([ref[:, c:e] for ref in fars], 0).astype(F32)
        for k in range(top):
            got = picked_sum(table[k], back, c, e)
            mixed += gates[k] * got
            sums[k] += jnp.sum(cotangent * got, 1, keepdims=True)
        for n, out in enumerate(outs):
            rows = out.shape[0]
            out[:, c:e] = mixed[n * rows : (n + 1) * rows].astype(BF16)
    lane = lax.broadcasted_iota(jnp.int32, (tok, LANES), 1)
    grad = jnp.zeros((tok, LANES), F32)
    for k in range(top):
        grad += jnp.where(lane == k, sums[k], 0.0)
    grad = jnp.transpose(grad)[: grads.shape[0]]
    grads[...] = grad if far_grads is None else grad + far_grads[...]


def mix_kernel(
    top, side, capacity, me_ref, meta, meta_far, block, back, out, grads
):
    tables = slot_tables(me_ref[0], [meta, meta_far], top, side, capacity)
    mix(top, tables[1], meta_far, (block,), back, (out,), grads)


def mix_last_kernel(
    top, side, capacity, me_ref, meta, meta_far, block, back, far, far_grads, out, grads
):
    tables = slot_tables(me_ref[0], [meta, meta_far], top, side, capacity)
    mix(top, tables[0], meta, (block,), back, (out,), grads, (far,), far_grads)


def fetch(sources, targets, sems):
    copies = []
    for n, (source, target) in enumerate(zip(sources, targets)):
        copies.append(pltpu.make_async_copy(source, target, sems.at[n]))
        copies[n].start()
    return copies


ACROSS_LAST = (((1,), (1,)), ((), ()))


def own_rows(own, stream, target):
    side, _, capacity, _ = own.shape
    return (
        [own.at[q, stream] for q in range(side)],
        [target.at[pl.ds(q * capacity, capacity)] for q in range(side)],
    )


def forward_kernel(side, *refs):
    (wg_in, own, far, wu_in, wd_in), outs = refs[:5], refs[5:9]
    wg, wu, wd, x, gate, up, hidden, y, sems, out_sems = refs[9:]
    rows, feature = x.shape
    units, half = gate.shape[1], rows // 2
    x_from, x_to = own_rows(own, 0, x)
    loads = fetch(
        [wg_in, far, *x_from, wu_in, wd_in], [wg, x.at[pl.ds(half, half)], *x_to, wu, wd], sems
    )
    for load in loads[:-2]:
        load.wait()
    for c, e in strips(units, 256):
        gate[:, c:e] = lax.dot_general(
            x[...], wg[c:e, :], ACROSS_LAST, preferred_element_type=F32
        )
    loads[-2].wait()
    for c, e in strips(units, 256):
        got = lax.dot_general(x[...], wu[c:e, :], ACROSS_LAST, preferred_element_type=F32)
        up[:, c:e] = got
        pre = gate[:, c:e]
        hidden[:, c:e] = (pre * (1.0 / (1.0 + jnp.exp(-pre))) * got).astype(BF16)
    copies = [
        pltpu.make_async_copy(source, out, out_sems.at[n])
        for n, (source, out) in enumerate(zip((gate, up, hidden, y), outs))
    ]
    for copy in copies[:3]:
        copy.start()
    loads[-1].wait()
    for c, e in strips(feature):
        got = jnp.dot(hidden[...], wd[:, c:e], preferred_element_type=F32)
        pair = [
            part.reshape(side, 1, half // side, e - c) for part in (got[:half], got[half:])
        ]
        y[:, c:e] = jnp.concatenate(pair, 1).reshape(rows, e - c).astype(BF16)
    copies[3].start()
    for copy in copies:
        copy.wait()


def backward_kernel(*refs):
    (wd_in, own, d_far, gate_in, up_in, wg_in, wu_in, x_far, hidden_in) = refs[:9]
    own_out, far_out, terms_out = refs[9:12]
    wd, gate, up, wg, wu, hidden, d, x, gg, gu, dx, tiles, sems, out_sems = refs[12:]
    rows, feature = d.shape
    units, half = gate.shape[1], rows // 2
    first, second = pl.ds(0, half), pl.ds(half, half)
    d_from, d_to = own_rows(own, 1, d)
    x_from, x_to = own_rows(own, 0, x)
    loads = fetch(
        [wd_in, *d_from, d_far, gate_in, up_in, wg_in, wu_in, *x_from, x_far, hidden_in],
        [wd, *d_to, d.at[second], gate, up, wg, wu, *x_to, x.at[second], hidden],
        sems,
    )
    side = len(d_to)
    for load in loads[: side + 4]:
        load.wait()
    for c, e in strips(units, 256):
        back = lax.dot_general(d[...], wd[c:e, :], ACROSS_LAST, preferred_element_type=F32)
        pre = gate[:, c:e]
        sig = 1.0 / (1.0 + jnp.exp(-pre))
        gg[:, c:e] = (back * up[:, c:e] * (sig * (1.0 + pre * (1.0 - sig)))).astype(BF16)
        gu[:, c:e] = (back * (pre * sig)).astype(BF16)
    for load in loads[side + 4 : side + 6]:
        load.wait()
    for c, e in strips(feature):
        got = jnp.dot(gg[...], wg[:, c:e], preferred_element_type=F32)
        got += jnp.dot(gu[...], wu[:, c:e], preferred_element_type=F32)
        dx[:, c:e] = got.astype(BF16)
    dx_copies = [
        pltpu.make_async_copy(dx.at[second], far_out, out_sems.at[2]),
        pltpu.make_async_copy(dx.at[first], own_out, out_sems.at[3]),
    ]
    for copy in dx_copies:
        copy.start()
    for load in loads[side + 6 :]:
        load.wait()
    copies = []
    for n, (left, right) in enumerate(((gg, x), (gu, x), (hidden, d))):
        for r, t in strips(units, tiles.shape[1]):
            slot = len(copies) % 2
            if len(copies) > 1:
                copies[-2].wait()
            for c, e in strips(feature, 1024):
                tiles[slot, : t - r, c:e] = lax.dot_general(
                    left[:, r:t], right[:, c:e], TRANSPOSED, preferred_element_type=F32
                ).astype(BF16)
            copy = pltpu.make_async_copy(
                tiles.at[slot, pl.ds(0, t - r)],
                terms_out.at[pl.ds(n * units + r, t - r)],
                out_sems.at[slot],
            )
            copy.start()
            copies.append(copy)
    for copy in (*copies[-2:], *dx_copies):
        copy.wait()


def streamed_call(kernel, outs, args, scratch):
    anywhere = pl.BlockSpec(memory_space=pltpu.HBM)
    return pl.pallas_call(
        kernel,
        out_shape=outs,
        in_specs=[pl.BlockSpec(memory_space=pl.ANY)] * len(args),
        out_specs=[anywhere] * len(outs),
        scratch_shapes=scratch,
        compiler_params=pltpu.CompilerParams(vmem_limit_bytes=60 * 1024 * 1024),
        cost_estimate=pl.CostEstimate(flops=1, bytes_accessed=1, transcendentals=0),
    )(*args)


def on_device(tokens, expert_ids, gate_prob, w_gate, w_up, w_down, d_mixed):
    tok, feature = tokens.shape
    top = expert_ids.shape[1]
    experts = lax.axis_size("expert")
    capacity = max(2, 2 * tok * top // experts)
    side = experts // 2
    half = side * capacity
    me = lax.axis_index("expert")
    me_arr = me[None]
    sets = [[h * side + p for p in range(side)] for h in range(2)]
    shape = jax.ShapeDtypeStruct

    def across(value):
        return lax.ppermute(value, "expert", [(e, (e + side) % experts) for e in range(experts)])

    def exchange(value):
        shaped = value.reshape(side, value.shape[0] // side, value.shape[1])
        got = lax.all_to_all(shaped, "expert", 0, 0, axis_index_groups=sets, tiled=True)
        return got.reshape(value.shape)

    def after(value, *earlier):
        return lax.optimization_barrier((value, *earlier))

    def call(kernel, outs, args, flops):
        return local_call(
            functools.partial(kernel, top, side, capacity),
            [shape(*out) for out in outs],
            me_arr,
            args,
            flops,
        )

    def pick(metas, blocks, scaled):
        count = len(metas)
        return local_call(
            functools.partial(pick_kernel, top, side, capacity, scaled),
            [shape((count * half, feature), BF16)],
            me_arr,
            [*metas, *blocks],
            LONG,
        )[0]

    meta = jnp.concatenate([expert_ids.T.astype(F32), gate_prob.T], 0)
    anywhere = pl.BlockSpec(memory_space=pltpu.HBM)
    picked = pl.pallas_call(
        functools.partial(own_pick_kernel, top, side, capacity),
        out_shape=shape((2 * half, feature), BF16),
        in_specs=[SMEM, VMEM, anywhere, anywhere],
        out_specs=VMEM,
        scratch_shapes=[
            pltpu.VMEM((tok, feature), BF16),
            pltpu.VMEM((tok, feature), BF16),
            pltpu.SemaphoreType.DMA((2,)),
        ],
        compiler_params=pltpu.CompilerParams(vmem_limit_bytes=60 * 1024 * 1024),
        cost_estimate=pl.CostEstimate(
            flops=8 * half * tok * feature, bytes_accessed=1, transcendentals=0
        ),
    )(me_arr, meta, tokens, d_mixed)
    own = exchange(picked)
    own = own.reshape(side, 2, capacity, feature)
    x_far, meta_far = after(across(tokens), across(meta))
    x_picked, own = after(pick([meta_far], [x_far], (False,)), own)
    d_late, own = after(d_mixed, own)
    d_far = across(d_late)
    x_far_rows = exchange(x_picked)
    d_picked, x_far_rows = after(pick([meta_far], [d_far], (True,)), x_far_rows)
    d_far_rows = exchange(d_picked)

    gate_matrix, up_matrix, down_matrix = w_gate[0].T, w_up[0].T, w_down[0]
    units, n_rows = gate_matrix.shape[0], 2 * half
    weight = pltpu.VMEM((units, feature), BF16)
    inner, wide = (n_rows, units), pltpu.VMEM((n_rows, feature), BF16)
    gate_pre, up_pre, hidden, y = streamed_call(
        functools.partial(forward_kernel, side),
        [shape(inner, F32), shape(inner, F32), shape(inner, BF16), shape((n_rows, feature), BF16)],
        [gate_matrix, own, x_far_rows, up_matrix, down_matrix],
        [
            *[weight] * 3,
            wide,
            pltpu.VMEM(inner, F32),
            pltpu.VMEM(inner, F32),
            pltpu.VMEM(inner, BF16),
            wide,
            pltpu.SemaphoreType.DMA((side + 4,)),
            pltpu.SemaphoreType.DMA((4,)),
        ],
    )
    y, d_far_rows = after(y, d_far_rows)
    y_back = exchange(y)

    dx_own, dx_far, terms = streamed_call(
        backward_kernel,
        [shape((half, feature), BF16)] * 2 + [shape((3 * units, feature), BF16)],
        [
            down_matrix,
            own,
            d_far_rows,
            gate_pre,
            up_pre,
            gate_matrix,
            up_matrix,
            x_far_rows,
            hidden,
        ],
        [
            weight,
            pltpu.VMEM(inner, F32),
            pltpu.VMEM(inner, F32),
            weight,
            weight,
            pltpu.VMEM(inner, BF16),
            wide,
            wide,
            pltpu.VMEM(inner, BF16),
            pltpu.VMEM(inner, BF16),
            wide,
            pltpu.VMEM((2, 256, feature), BF16),
            pltpu.SemaphoreType.DMA((2 * side + 8,)),
            pltpu.SemaphoreType.DMA((4,)),
        ],
    )
    dx_own, dx_far, terms, y_back = after(dx_own, dx_far, terms, y_back)
    summed = lax.psum_scatter(terms, "dp", scatter_dimension=1, tiled=True)

    token_rows, grad_rows = ((tok, feature), BF16), ((8, tok), F32)
    work = 2 * half * tok * feature
    mixed_far, grads_far = call(
        mix_kernel, [token_rows, grad_rows], [meta, meta_far, d_far, y_back], 2 * top * work
    )
    dx_far, mixed_far, grads_far = after(dx_far, mixed_far, grads_far)
    dx_far_back = exchange(dx_far)
    mixed_far, grads_far = after(across(mixed_far), across(grads_far))

    def table(meta, came):
        return pl.pallas_call(
            functools.partial(table_kernel, top, side, capacity),
            out_shape=shape((half, tok), BF16),
            in_specs=[SMEM, VMEM, anywhere],
            out_specs=VMEM,
            compiler_params=pltpu.CompilerParams(vmem_limit_bytes=60 * 1024 * 1024),
            cost_estimate=pl.CostEstimate(flops=LONG, bytes_accessed=1, transcendentals=0),
        )(me_arr, meta, came)

    def total(table, back, *far):
        return local_call_plain(
            sum_kernel, [shape((tok, feature), BF16)], [table, back, *far], work
        )[0]

    far_table, mixed_far, grads_far, dx_far_back = after(
        table(meta_far, mixed_far), mixed_far, grads_far, dx_far_back
    )
    tokens_far, dx_own = after(total(far_table, dx_far_back), dx_own)
    dx_own_back = exchange(dx_own)
    mixed, grads = call(
        mix_last_kernel,
        [token_rows, grad_rows],
        [meta, meta_far, d_mixed, y_back, mixed_far, grads_far],
        2 * top * work,
    )
    tokens_far = across(tokens_far)
    weight_grads = (
        summed[:units].astype(F32).T[None],
        summed[units : 2 * units].astype(F32).T[None],
        summed[2 * units :].astype(F32)[None],
    )
    tokens_far, mixed, grads, *weight_grads = after(tokens_far, mixed, grads, *weight_grads)
    own_table, tokens_far, dx_own_back = after(table(meta, tokens_far), tokens_far, dx_own_back)
    d_tokens = total(own_table, dx_own_back, tokens_far)
    return (mixed, d_tokens, grads[:top].T, *weight_grads)


def solution(mesh):
    in_specs = (
        P(("dp", "expert"), None),
        P(("dp", "expert"), None),
        P(("dp", "expert"), None),
        P("expert", None, None),
        P("expert", None, None),
        P("expert", None, None),
        P(("dp", "expert"), None),
    )
    out_specs = (
        P(("dp", "expert"), None),
        P(("dp", "expert"), None),
        P(("dp", "expert"), None),
        P("expert", "dp", None),
        P("expert", "dp", None),
        P("expert", None, "dp"),
    )
    return jax.shard_map(
        on_device, mesh=mesh, in_specs=in_specs, out_specs=out_specs, check_vma=False
    )
```

```python
import functools

import jax
import jax.numpy as jnp
from jax import lax
from jax.experimental import pallas as pl
from jax.experimental.pallas import tpu as pltpu
from jax.sharding import PartitionSpec as P

BF16 = jnp.bfloat16
F32 = jnp.float32
LANES = 128
STRIP = 512
LONG = 10**11
VMEM = pl.BlockSpec(memory_space=pltpu.VMEM)
SMEM = pl.BlockSpec(memory_space=pltpu.SMEM)


def local_call(kernel, outs, me, args, flops):
    size = sum(x.size * x.dtype.itemsize for x in (*outs, *args))
    return pl.pallas_call(
        kernel,
        out_shape=outs,
        in_specs=[SMEM] + [VMEM] * len(args),
        out_specs=[VMEM] * len(outs),
        compiler_params=pltpu.CompilerParams(vmem_limit_bytes=6 * 1024 * 1024),
        cost_estimate=pl.CostEstimate(flops=flops, bytes_accessed=size, transcendentals=0),
    )(me, *args)


def local_call_plain(kernel, outs, args, flops):
    return local_call(lambda me_ref, *refs: kernel(*refs), outs, jnp.zeros((1,), jnp.int32), args, flops)


def strips(width, step=STRIP):
    return [(c, min(c + step, width)) for c in range(0, width, step)]


def slot_tables(me, metas, top, side, capacity, wanted=None):
    count = len(metas)
    span = count * capacity
    tok = metas[0].shape[1]
    slot = lax.broadcasted_iota(jnp.int32, (side * span, tok), 0)
    expert = ((me - lax.rem(me, side)) + slot // span).astype(F32)
    block_of = lax.rem(slot, span) // capacity
    place = lax.rem(slot, capacity).astype(F32)
    row = lax.broadcasted_iota(jnp.int32, (tok, tok), 0)
    column = lax.broadcasted_iota(jnp.int32, (tok, tok), 1)
    earlier = jnp.where(row < column, 1.0, 0.0).astype(BF16)
    tables = []
    for b in range(count) if wanted is None else (wanted,):
        named = [jnp.where(metas[b][k : k + 1, :] == expert, 1.0, 0.0) for k in range(top)]
        member = functools.reduce(lambda p, q: p + q, named)
        rank = jnp.dot(member.astype(BF16), earlier, preferred_element_type=F32)
        here = rank == place
        if count > 1:
            here = here & (block_of == b)
        tables.append([jnp.where(here, part, 0.0) for part in named])
    return tables


def pick_kernel(top, side, capacity, scaled, me_ref, *refs, loads=()):
    count = len(scaled)
    metas, blocks, out = refs[:count], refs[count:-1], refs[-1]
    tables = slot_tables(me_ref[0], metas, top, side, capacity)
    held = jnp.concatenate([functools.reduce(lambda p, q: p + q, ks) for ks in tables], 1)
    held = held.astype(BF16)
    gate = 0.0
    for meta, ks, has in zip(metas, tables, scaled):
        for k, part in enumerate(ks):
            if has:
                part = part * meta[top + k : top + k + 1, :]
            gate += jnp.sum(part, 1, keepdims=True)
    for load in loads:
        load.wait()
    for c, e in strips(out.shape[1]):
        block = jnp.concatenate([ref[:, c:e] for ref in blocks], 0)
        got = jnp.dot(held, block, preferred_element_type=F32)
        out[:, c:e] = ((gate * got) if any(scaled) else got).astype(BF16)


def own_pick_kernel(top, side, capacity, me_ref, meta, x_hbm, d_hbm, out, x, d, sems):
    loads = fetch((x_hbm, d_hbm), (x, d), sems)
    pick_kernel(
        top, side, capacity, (False, True), me_ref, meta, meta, x, d, out, loads=loads
    )


TRANSPOSED = (((0,), (0,)), ((), ()))


def picked_sum(table, back, c, e):
    return lax.dot_general(
        table.astype(BF16), back[:, c:e], TRANSPOSED, preferred_element_type=F32
    )


def table_kernel(top, side, capacity, me_ref, meta, came, out):
    (table,) = slot_tables(me_ref[0], [meta], top, side, capacity)
    out[...] = functools.reduce(lambda p, q: p + q, table).astype(BF16)


def sum_kernel(table, back, *refs):
    out = refs[-1]
    for c, e in strips(out.shape[1]):
        got = picked_sum(table, back, c, e)
        for far in refs[:-1]:
            got += far[:, c:e].astype(F32)
        out[:, c:e] = got.astype(BF16)


def mix(top, table, meta, blocks, back, outs, grads, fars=()):
    tok = meta.shape[1]
    gates = [meta[top + k : top + k + 1, :] for k in range(top)]
    gates = [jnp.transpose(jnp.broadcast_to(g, (8, tok)))[:, :1] for g in gates]
    sums = [jnp.zeros((tok, 1), F32) for _ in range(top)]
    for c, e in strips(back.shape[1]):
        cotangent = jnp.concatenate([ref[:, c:e] for ref in blocks], 0).astype(F32)
        mixed = 0.0
        if fars:
            mixed = jnp.concatenate([ref[:, c:e] for ref in fars], 0).astype(F32)
        for k in range(top):
            got = picked_sum(table[k], back, c, e)
            mixed += gates[k] * got
            sums[k] += jnp.sum(cotangent * got, 1, keepdims=True)
        for n, out in enumerate(outs):
            rows = out.shape[0]
            out[:, c:e] = mixed[n * rows : (n + 1) * rows].astype(BF16)
    lane = lax.broadcasted_iota(jnp.int32, (tok, LANES), 1)
    grad = jnp.zeros((tok, LANES), F32)
    for k in range(top):
        grad += jnp.where(lane == k, sums[k], 0.0)
    grads[...] = jnp.transpose(grad)[: grads.shape[0]]


def mix_kernel(
    top, side, capacity, me_ref, meta, meta_far, block, back, out, grads
):
    (table,) = slot_tables(me_ref[0], [meta, meta_far], top, side, capacity, 1)
    mix(top, table, meta_far, (block,), back, (out,), grads)


def mix_last_kernel(top, side, capacity, me_ref, meta, meta_far, block, back, far, out, grads):
    (table,) = slot_tables(me_ref[0], [meta, meta_far], top, side, capacity, 0)
    mix(top, table, meta, (block,), back, (out,), grads, (far,))


def fetch(sources, targets, sems):
    copies = []
    for n, (source, target) in enumerate(zip(sources, targets)):
        copies.append(pltpu.make_async_copy(source, target, sems.at[n]))
        copies[n].start()
    return copies


ACROSS_LAST = (((1,), (1,)), ((), ()))


def own_rows(own, stream, target):
    side, _, capacity, _ = own.shape
    return (
        [own.at[q, stream] for q in range(side)],
        [target.at[pl.ds(q * capacity, capacity)] for q in range(side)],
    )


def forward_kernel(side, *refs):
    (wg_in, own, far, wu_in, wd_in), outs = refs[:5], refs[5:9]
    wg, wu, wd, x, gate, up, hidden, y, sems, out_sems = refs[9:]
    rows, feature = x.shape
    units, half = gate.shape[1], rows // 2
    x_from, x_to = own_rows(own, 0, x)
    loads = fetch(
        [wg_in, far, *x_from, wu_in, wd_in], [wg, x.at[pl.ds(half, half)], *x_to, wu, wd], sems
    )
    for load in loads[:-2]:
        load.wait()
    for c, e in strips(units, 256):
        gate[:, c:e] = lax.dot_general(
            x[...], wg[c:e, :], ACROSS_LAST, preferred_element_type=F32
        )
    loads[-2].wait()
    for c, e in strips(units, 256):
        got = lax.dot_general(x[...], wu[c:e, :], ACROSS_LAST, preferred_element_type=F32)
        up[:, c:e] = got
        pre = gate[:, c:e]
        hidden[:, c:e] = (pre * (1.0 / (1.0 + jnp.exp(-pre))) * got).astype(BF16)
    copies = [
        pltpu.make_async_copy(source, out, out_sems.at[n])
        for n, (source, out) in enumerate(zip((gate, up, hidden, y), outs))
    ]
    for copy in copies[:3]:
        copy.start()
    loads[-1].wait()
    for c, e in strips(feature):
        got = jnp.dot(hidden[...], wd[:, c:e], preferred_element_type=F32)
        pair = [
            part.reshape(side, 1, half // side, e - c) for part in (got[:half], got[half:])
        ]
        y[:, c:e] = jnp.concatenate(pair, 1).reshape(rows, e - c).astype(BF16)
    copies[3].start()
    for copy in copies:
        copy.wait()


def backward_kernel(*refs):
    (wd_in, own, d_far, gate_in, up_in, wg_in, wu_in, x_far, hidden_in) = refs[:9]
    own_out, far_out, terms_out = refs[9:12]
    wd, gate, up, wg, wu, hidden, d, x, gg, gu, dx, tiles, sems, out_sems = refs[12:]
    rows, feature = d.shape
    units, half = gate.shape[1], rows // 2
    first, second = pl.ds(0, half), pl.ds(half, half)
    d_from, d_to = own_rows(own, 1, d)
    x_from, x_to = own_rows(own, 0, x)
    loads = fetch(
        [wd_in, *d_from, d_far, gate_in, up_in, wg_in, wu_in, *x_from, x_far, hidden_in],
        [wd, *d_to, d.at[second], gate, up, wg, wu, *x_to, x.at[second], hidden],
        sems,
    )
    side = len(d_to)
    for load in loads[: side + 4]:
        load.wait()
    for c, e in strips(units, 256):
        back = lax.dot_general(d[...], wd[c:e, :], ACROSS_LAST, preferred_element_type=F32)
        pre = gate[:, c:e]
        sig = 1.0 / (1.0 + jnp.exp(-pre))
        gg[:, c:e] = (back * up[:, c:e] * (sig * (1.0 + pre * (1.0 - sig)))).astype(BF16)
        gu[:, c:e] = (back * (pre * sig)).astype(BF16)
    for load in loads[side + 4 : side + 6]:
        load.wait()
    for c, e in strips(feature):
        got = jnp.dot(gg[...], wg[:, c:e], preferred_element_type=F32)
        got += jnp.dot(gu[...], wu[:, c:e], preferred_element_type=F32)
        dx[:, c:e] = got.astype(BF16)
    dx_copies = [
        pltpu.make_async_copy(dx.at[second], far_out, out_sems.at[2]),
        pltpu.make_async_copy(dx.at[first], own_out, out_sems.at[3]),
    ]
    for copy in dx_copies:
        copy.start()
    for load in loads[side + 6 :]:
        load.wait()
    copies = []
    for n, (left, right) in enumerate(((gg, x), (gu, x), (hidden, d))):
        for r, t in strips(units, tiles.shape[1]):
            slot = len(copies) % 2
            if len(copies) > 1:
                copies[-2].wait()
            for c, e in strips(feature, 1024):
                tiles[slot, : t - r, c:e] = lax.dot_general(
                    left[:, r:t], right[:, c:e], TRANSPOSED, preferred_element_type=F32
                ).astype(BF16)
            copy = pltpu.make_async_copy(
                tiles.at[slot, pl.ds(0, t - r)],
                terms_out.at[pl.ds(n * units + r, t - r)],
                out_sems.at[slot],
            )
            copy.start()
            copies.append(copy)
    for copy in (*copies[-2:], *dx_copies):
        copy.wait()


def streamed_call(kernel, outs, args, scratch):
    anywhere = pl.BlockSpec(memory_space=pltpu.HBM)
    return pl.pallas_call(
        kernel,
        out_shape=outs,
        in_specs=[pl.BlockSpec(memory_space=pl.ANY)] * len(args),
        out_specs=[anywhere] * len(outs),
        scratch_shapes=scratch,
        compiler_params=pltpu.CompilerParams(vmem_limit_bytes=60 * 1024 * 1024),
        cost_estimate=pl.CostEstimate(flops=1, bytes_accessed=1, transcendentals=0),
    )(*args)


def on_device(tokens, expert_ids, gate_prob, w_gate, w_up, w_down, d_mixed):
    tok, feature = tokens.shape
    top = expert_ids.shape[1]
    experts = lax.axis_size("expert")
    capacity = max(2, 2 * tok * top // experts)
    side = experts // 2
    half = side * capacity
    me = lax.axis_index("expert")
    me_arr = me[None]
    sets = [[h * side + p for p in range(side)] for h in range(2)]
    shape = jax.ShapeDtypeStruct

    def across(value):
        return lax.ppermute(value, "expert", [(e, (e + side) % experts) for e in range(experts)])

    def exchange(value):
        shaped = value.reshape(side, value.shape[0] // side, value.shape[1])
        got = lax.all_to_all(shaped, "expert", 0, 0, axis_index_groups=sets, tiled=True)
        return got.reshape(value.shape)

    def after(value, *earlier):
        return lax.optimization_barrier((value, *earlier))

    def call(kernel, outs, args, flops):
        return local_call(
            functools.partial(kernel, top, side, capacity),
            [shape(*out) for out in outs],
            me_arr,
            args,
            flops,
        )

    def pick(metas, blocks, scaled):
        count = len(metas)
        return local_call(
            functools.partial(pick_kernel, top, side, capacity, scaled),
            [shape((count * half, feature), BF16)],
            me_arr,
            [*metas, *blocks],
            LONG,
        )[0]

    meta = jnp.concatenate([expert_ids.T.astype(F32), gate_prob.T], 0)
    anywhere = pl.BlockSpec(memory_space=pltpu.HBM)
    picked = pl.pallas_call(
        functools.partial(own_pick_kernel, top, side, capacity),
        out_shape=shape((2 * half, feature), BF16),
        in_specs=[SMEM, VMEM, anywhere, anywhere],
        out_specs=VMEM,
        scratch_shapes=[
            pltpu.VMEM((tok, feature), BF16),
            pltpu.VMEM((tok, feature), BF16),
            pltpu.SemaphoreType.DMA((2,)),
        ],
        compiler_params=pltpu.CompilerParams(vmem_limit_bytes=60 * 1024 * 1024),
        cost_estimate=pl.CostEstimate(
            flops=8 * half * tok * feature, bytes_accessed=1, transcendentals=0
        ),
    )(me_arr, meta, tokens, d_mixed)
    own = exchange(picked)
    own = own.reshape(side, 2, capacity, feature)
    x_far, meta_far = after(across(tokens), across(meta))
    x_picked, own = after(pick([meta_far], [x_far], (False,)), own)
    d_late, own = after(d_mixed, own)
    d_far = across(d_late)
    x_far_rows = exchange(x_picked)
    d_picked, x_far_rows = after(pick([meta_far], [d_far], (True,)), x_far_rows)
    d_far_rows = exchange(d_picked)

    gate_matrix, up_matrix, down_matrix = w_gate[0].T, w_up[0].T, w_down[0]
    units, n_rows = gate_matrix.shape[0], 2 * half
    weight = pltpu.VMEM((units, feature), BF16)
    inner, wide = (n_rows, units), pltpu.VMEM((n_rows, feature), BF16)
    gate_pre, up_pre, hidden, y = streamed_call(
        functools.partial(forward_kernel, side),
        [shape(inner, F32), shape(inner, F32), shape(inner, BF16), shape((n_rows, feature), BF16)],
        [gate_matrix, own, x_far_rows, up_matrix, down_matrix],
        [
            *[weight] * 3,
            wide,
            pltpu.VMEM(inner, F32),
            pltpu.VMEM(inner, F32),
            pltpu.VMEM(inner, BF16),
            wide,
            pltpu.SemaphoreType.DMA((side + 4,)),
            pltpu.SemaphoreType.DMA((4,)),
        ],
    )
    y, d_far_rows = after(y, d_far_rows)
    y_back = exchange(y)

    dx_own, dx_far, terms = streamed_call(
        backward_kernel,
        [shape((half, feature), BF16)] * 2 + [shape((3 * units, feature), BF16)],
        [
            down_matrix,
            own,
            d_far_rows,
            gate_pre,
            up_pre,
            gate_matrix,
            up_matrix,
            x_far_rows,
            hidden,
        ],
        [
            weight,
            pltpu.VMEM(inner, F32),
            pltpu.VMEM(inner, F32),
            weight,
            weight,
            pltpu.VMEM(inner, BF16),
            wide,
            wide,
            pltpu.VMEM(inner, BF16),
            pltpu.VMEM(inner, BF16),
            wide,
            pltpu.VMEM((2, 256, feature), BF16),
            pltpu.SemaphoreType.DMA((2 * side + 8,)),
            pltpu.SemaphoreType.DMA((4,)),
        ],
    )
    dx_own, dx_far, terms, y_back = after(dx_own, dx_far, terms, y_back)
    summed = lax.psum_scatter(terms, "dp", scatter_dimension=1, tiled=True)

    token_rows, grad_rows = ((tok, feature), BF16), ((8, tok), F32)
    work = 2 * half * tok * feature
    mixed_far, grads_far = call(
        mix_kernel, [token_rows, grad_rows], [meta, meta_far, d_far, y_back], 2 * top * work
    )
    dx_far, mixed_far, grads_far = after(dx_far, mixed_far, grads_far)
    dx_far_back = exchange(dx_far)
    mixed_far = across(mixed_far)

    def table(meta, came):
        return pl.pallas_call(
            functools.partial(table_kernel, top, side, capacity),
            out_shape=shape((half, tok), BF16),
            in_specs=[SMEM, VMEM, anywhere],
            out_specs=VMEM,
            compiler_params=pltpu.CompilerParams(vmem_limit_bytes=60 * 1024 * 1024),
            cost_estimate=pl.CostEstimate(flops=LONG, bytes_accessed=1, transcendentals=0),
        )(me_arr, meta, came)

    def total(table, back, *far):
        return local_call_plain(
            lambda table, *refs: sum_kernel(table[...], *refs),
            [shape((tok, feature), BF16)],
            [table, back, *far],
            work,
        )[0]

    far_table, mixed_far, dx_far_back = after(
        table(meta_far, mixed_far), mixed_far, dx_far_back
    )
    tokens_far, dx_own, grads_far = after(total(far_table, dx_far_back), dx_own, grads_far)
    dx_own_back = exchange(dx_own)
    mixed, grads = call(
        mix_last_kernel,
        [token_rows, grad_rows],
        [meta, meta_far, d_mixed, y_back, mixed_far],
        2 * top * work,
    )
    tokens_far = across(tokens_far)
    weight_grads = (
        summed[:units].astype(F32).T[None],
        summed[units : 2 * units].astype(F32).T[None],
        summed[2 * units :].astype(F32)[None],
    )
    mixed, grads, grads_far, *weight_grads = after(mixed, grads, grads_far, *weight_grads)
    grads = grads + across(grads_far)
    tokens_far, mixed, *weight_grads = after(tokens_far, mixed, *weight_grads)
    own_table, tokens_far, dx_own_back = after(table(meta, tokens_far), tokens_far, dx_own_back)
    d_tokens = total(own_table, dx_own_back, tokens_far)
    return (mixed, d_tokens, grads[:top].T, *weight_grads)


def solution(mesh):
    in_specs = (
        P(("dp", "expert"), None),
        P(("dp", "expert"), None),
        P(("dp", "expert"), None),
        P("expert", None, None),
        P("expert", None, None),
        P("expert", None, None),
        P(("dp", "expert"), None),
    )
    out_specs = (
        P(("dp", "expert"), None),
        P(("dp", "expert"), None),
        P(("dp", "expert"), None),
        P("expert", "dp", None),
        P("expert", "dp", None),
        P("expert", None, "dp"),
    )
    return jax.shard_map(
        on_device, mesh=mesh, in_specs=in_specs, out_specs=out_specs, check_vma=False
    )
```

```python
import functools

import jax
import jax.numpy as jnp
from jax import lax
from jax.experimental import pallas as pl
from jax.experimental.pallas import tpu as pltpu
from jax.sharding import PartitionSpec as P

BF16 = jnp.bfloat16
F32 = jnp.float32
LANES = 128
STRIP = 512
LONG = 10**11
VMEM = pl.BlockSpec(memory_space=pltpu.VMEM)
SMEM = pl.BlockSpec(memory_space=pltpu.SMEM)


def local_call(kernel, outs, me, args, flops):
    size = sum(x.size * x.dtype.itemsize for x in (*outs, *args))
    return pl.pallas_call(
        kernel,
        out_shape=outs,
        in_specs=[SMEM] + [VMEM] * len(args),
        out_specs=[VMEM] * len(outs),
        compiler_params=pltpu.CompilerParams(vmem_limit_bytes=6 * 1024 * 1024),
        cost_estimate=pl.CostEstimate(flops=flops, bytes_accessed=size, transcendentals=0),
    )(me, *args)


def local_call_plain(kernel, outs, args, flops):
    return local_call(lambda me_ref, *refs: kernel(*refs), outs, jnp.zeros((1,), jnp.int32), args, flops)


def strips(width, step=STRIP):
    return [(c, min(c + step, width)) for c in range(0, width, step)]


def slot_tables(me, metas, top, side, capacity, wanted=None):
    count = len(metas)
    span = count * capacity
    tok = metas[0].shape[1]
    slot = lax.broadcasted_iota(jnp.int32, (side * span, tok), 0)
    expert = ((me - lax.rem(me, side)) + slot // span).astype(F32)
    block_of = lax.rem(slot, span) // capacity
    place = lax.rem(slot, capacity).astype(F32)
    row = lax.broadcasted_iota(jnp.int32, (tok, tok), 0)
    column = lax.broadcasted_iota(jnp.int32, (tok, tok), 1)
    earlier = jnp.where(row < column, 1.0, 0.0).astype(BF16)
    tables = []
    for b in range(count) if wanted is None else (wanted,):
        named = [jnp.where(metas[b][k : k + 1, :] == expert, 1.0, 0.0) for k in range(top)]
        member = functools.reduce(lambda p, q: p + q, named)
        rank = jnp.dot(member.astype(BF16), earlier, preferred_element_type=F32)
        here = rank == place
        if count > 1:
            here = here & (block_of == b)
        tables.append([jnp.where(here, part, 0.0) for part in named])
    return tables


def pick_kernel(top, side, capacity, scaled, me_ref, *refs, loads=()):
    count = len(scaled)
    metas, blocks, out = refs[:count], refs[count:-1], refs[-1]
    tables = slot_tables(me_ref[0], metas, top, side, capacity)
    held = jnp.concatenate([functools.reduce(lambda p, q: p + q, ks) for ks in tables], 1)
    held = held.astype(BF16)
    gate = 0.0
    for meta, ks, has in zip(metas, tables, scaled):
        for k, part in enumerate(ks):
            if has:
                part = part * meta[top + k : top + k + 1, :]
            gate += jnp.sum(part, 1, keepdims=True)
    for load in loads:
        load.wait()
    for c, e in strips(out.shape[1]):
        block = jnp.concatenate([ref[:, c:e] for ref in blocks], 0)
        got = jnp.dot(held, block, preferred_element_type=F32)
        out[:, c:e] = ((gate * got) if any(scaled) else got).astype(BF16)


def own_pick_kernel(top, side, capacity, me_ref, meta, x_hbm, d_hbm, out, x, d, sems):
    loads = fetch((x_hbm, d_hbm), (x, d), sems)
    pick_kernel(
        top, side, capacity, (False, True), me_ref, meta, meta, x, d, out, loads=loads
    )


TRANSPOSED = (((0,), (0,)), ((), ()))


def picked_sum(table, back, c, e):
    return lax.dot_general(
        table.astype(BF16), back[:, c:e], TRANSPOSED, preferred_element_type=F32
    )


def table_kernel(top, side, capacity, me_ref, meta, came, out):
    (table,) = slot_tables(me_ref[0], [meta], top, side, capacity)
    out[...] = functools.reduce(lambda p, q: p + q, table).astype(BF16)


def sum_kernel(table, back, *refs):
    out = refs[-1]
    for c, e in strips(out.shape[1]):
        got = picked_sum(table, back, c, e)
        for far in refs[:-1]:
            got += far[:, c:e].astype(F32)
        out[:, c:e] = got.astype(BF16)


def mix(top, table, meta, blocks, back, outs, grads, fars=()):
    tok = meta.shape[1]
    gates = [meta[top + k : top + k + 1, :] for k in range(top)]
    gates = [jnp.transpose(jnp.broadcast_to(g, (8, tok)))[:, :1] for g in gates]
    sums = [jnp.zeros((tok, 1), F32) for _ in range(top)]
    for c, e in strips(back.shape[1]):
        cotangent = jnp.concatenate([ref[:, c:e] for ref in blocks], 0).astype(F32)
        mixed = 0.0
        if fars:
            mixed = jnp.concatenate([ref[:, c:e] for ref in fars], 0).astype(F32)
        for k in range(top):
            got = picked_sum(table[k], back, c, e)
            mixed += gates[k] * got
            sums[k] += jnp.sum(cotangent * got, 1, keepdims=True)
        for n, out in enumerate(outs):
            rows = out.shape[0]
            out[:, c:e] = mixed[n * rows : (n + 1) * rows].astype(BF16)
    lane = lax.broadcasted_iota(jnp.int32, (tok, LANES), 1)
    grad = jnp.zeros((tok, LANES), F32)
    for k in range(top):
        grad += jnp.where(lane == k, sums[k], 0.0)
    grads[...] = jnp.transpose(grad)[: grads.shape[0]]


def mix_kernel(
    top, side, capacity, me_ref, meta, meta_far, block, back, out, grads
):
    (table,) = slot_tables(me_ref[0], [meta, meta_far], top, side, capacity, 1)
    mix(top, table, meta_far, (block,), back, (out,), grads)


def mix_last_kernel(top, side, capacity, me_ref, meta, meta_far, block, back, far, out, grads):
    (table,) = slot_tables(me_ref[0], [meta, meta_far], top, side, capacity, 0)
    mix(top, table, meta, (block,), back, (out,), grads, (far,))


def fetch(sources, targets, sems):
    copies = []
    for n, (source, target) in enumerate(zip(sources, targets)):
        copies.append(pltpu.make_async_copy(source, target, sems.at[n]))
        copies[n].start()
    return copies


ACROSS_LAST = (((1,), (1,)), ((), ()))


def own_rows(own, stream, target):
    side, _, capacity, _ = own.shape
    return (
        [own.at[q, stream] for q in range(side)],
        [target.at[pl.ds(q * capacity, capacity)] for q in range(side)],
    )


def forward_kernel(side, *refs):
    (wg_in, own, far, wu_in, wd_in), outs = refs[:5], refs[5:9]
    wg, wu, wd, x, gate, up, hidden, y, sems, out_sems = refs[9:]
    rows, feature = x.shape
    units, half = gate.shape[1], rows // 2
    x_from, x_to = own_rows(own, 0, x)
    loads = fetch(
        [wg_in, far, *x_from, wu_in, wd_in], [wg, x.at[pl.ds(half, half)], *x_to, wu, wd], sems
    )
    for load in loads[:-2]:
        load.wait()
    for c, e in strips(units, 256):
        gate[:, c:e] = lax.dot_general(
            x[...], wg[c:e, :], ACROSS_LAST, preferred_element_type=F32
        )
    loads[-2].wait()
    for c, e in strips(units, 256):
        got = lax.dot_general(x[...], wu[c:e, :], ACROSS_LAST, preferred_element_type=F32)
        up[:, c:e] = got
        pre = gate[:, c:e]
        hidden[:, c:e] = (pre * (1.0 / (1.0 + jnp.exp(-pre))) * got).astype(BF16)
    copies = [
        pltpu.make_async_copy(source, out, out_sems.at[n])
        for n, (source, out) in enumerate(zip((gate, up, hidden, y), outs))
    ]
    for copy in copies[:3]:
        copy.start()
    loads[-1].wait()
    for c, e in strips(feature):
        got = jnp.dot(hidden[...], wd[:, c:e], preferred_element_type=F32)
        pair = [
            part.reshape(side, 1, half // side, e - c) for part in (got[:half], got[half:])
        ]
        y[:, c:e] = jnp.concatenate(pair, 1).reshape(rows, e - c).astype(BF16)
    copies[3].start()
    for copy in copies:
        copy.wait()


def backward_kernel(*refs):
    (wd_in, own, d_far, gate_in, up_in, wg_in, wu_in, x_far, hidden_in) = refs[:9]
    own_out, far_out, terms_out = refs[9:12]
    wd, gate, up, wg, wu, hidden, d, x, gg, gu, dx, tiles, sems, out_sems = refs[12:]
    rows, feature = d.shape
    units, half = gate.shape[1], rows // 2
    first, second = pl.ds(0, half), pl.ds(half, half)
    d_from, d_to = own_rows(own, 1, d)
    x_from, x_to = own_rows(own, 0, x)
    loads = fetch(
        [wd_in, *d_from, d_far, gate_in, up_in, wg_in, wu_in, *x_from, x_far, hidden_in],
        [wd, *d_to, d.at[second], gate, up, wg, wu, *x_to, x.at[second], hidden],
        sems,
    )
    side = len(d_to)
    for load in loads[: side + 4]:
        load.wait()
    for c, e in strips(units, 256):
        back = lax.dot_general(d[...], wd[c:e, :], ACROSS_LAST, preferred_element_type=F32)
        pre = gate[:, c:e]
        sig = 1.0 / (1.0 + jnp.exp(-pre))
        gg[:, c:e] = (back * up[:, c:e] * (sig * (1.0 + pre * (1.0 - sig)))).astype(BF16)
        gu[:, c:e] = (back * (pre * sig)).astype(BF16)
    for load in loads[side + 4 : side + 6]:
        load.wait()
    for c, e in strips(feature):
        got = jnp.dot(gg[...], wg[:, c:e], preferred_element_type=F32)
        got += jnp.dot(gu[...], wu[:, c:e], preferred_element_type=F32)
        dx[:, c:e] = got.astype(BF16)
    dx_copies = [
        pltpu.make_async_copy(dx.at[second], far_out, out_sems.at[2]),
        pltpu.make_async_copy(dx.at[first], own_out, out_sems.at[3]),
    ]
    for copy in dx_copies:
        copy.start()
    for load in loads[side + 6 :]:
        load.wait()
    copies = []
    for n, (left, right) in enumerate(((gg, x), (gu, x), (hidden, d))):
        for r, t in strips(units, tiles.shape[1]):
            slot = len(copies) % 2
            if len(copies) > 1:
                copies[-2].wait()
            for c, e in strips(feature, 1024):
                tiles[slot, : t - r, c:e] = lax.dot_general(
                    left[:, r:t], right[:, c:e], TRANSPOSED, preferred_element_type=F32
                ).astype(BF16)
            copy = pltpu.make_async_copy(
                tiles.at[slot, pl.ds(0, t - r)],
                terms_out.at[pl.ds(n * units + r, t - r)],
                out_sems.at[slot],
            )
            copy.start()
            copies.append(copy)
    for copy in (*copies[-2:], *dx_copies):
        copy.wait()


def streamed_call(kernel, outs, args, scratch):
    anywhere = pl.BlockSpec(memory_space=pltpu.HBM)
    return pl.pallas_call(
        kernel,
        out_shape=outs,
        in_specs=[pl.BlockSpec(memory_space=pl.ANY)] * len(args),
        out_specs=[anywhere] * len(outs),
        scratch_shapes=scratch,
        compiler_params=pltpu.CompilerParams(vmem_limit_bytes=60 * 1024 * 1024),
        cost_estimate=pl.CostEstimate(flops=1, bytes_accessed=1, transcendentals=0),
    )(*args)


def on_device(tokens, expert_ids, gate_prob, w_gate, w_up, w_down, d_mixed):
    tok, feature = tokens.shape
    top = expert_ids.shape[1]
    experts = lax.axis_size("expert")
    capacity = max(2, 2 * tok * top // experts)
    side = experts // 2
    half = side * capacity
    me = lax.axis_index("expert")
    me_arr = me[None]
    sets = [[h * side + p for p in range(side)] for h in range(2)]
    shape = jax.ShapeDtypeStruct

    def across(value):
        return lax.ppermute(value, "expert", [(e, (e + side) % experts) for e in range(experts)])

    def exchange(value):
        shaped = value.reshape(side, value.shape[0] // side, value.shape[1])
        got = lax.all_to_all(shaped, "expert", 0, 0, axis_index_groups=sets, tiled=True)
        return got.reshape(value.shape)

    def after(value, *earlier):
        return lax.optimization_barrier((value, *earlier))

    def call(kernel, outs, args, flops):
        return local_call(
            functools.partial(kernel, top, side, capacity),
            [shape(*out) for out in outs],
            me_arr,
            args,
            flops,
        )

    def pick(metas, blocks, scaled):
        count = len(metas)
        return local_call(
            functools.partial(pick_kernel, top, side, capacity, scaled),
            [shape((count * half, feature), BF16)],
            me_arr,
            [*metas, *blocks],
            LONG,
        )[0]

    meta = jnp.concatenate([expert_ids.T.astype(F32), gate_prob.T], 0)
    anywhere = pl.BlockSpec(memory_space=pltpu.HBM)
    picked = pl.pallas_call(
        functools.partial(own_pick_kernel, top, side, capacity),
        out_shape=shape((2 * half, feature), BF16),
        in_specs=[SMEM, VMEM, anywhere, anywhere],
        out_specs=VMEM,
        scratch_shapes=[
            pltpu.VMEM((tok, feature), BF16),
            pltpu.VMEM((tok, feature), BF16),
            pltpu.SemaphoreType.DMA((2,)),
        ],
        compiler_params=pltpu.CompilerParams(vmem_limit_bytes=60 * 1024 * 1024),
        cost_estimate=pl.CostEstimate(
            flops=8 * half * tok * feature, bytes_accessed=1, transcendentals=0
        ),
    )(me_arr, meta, tokens, d_mixed)
    own = exchange(picked)
    own = own.reshape(side, 2, capacity, feature)
    x_far, meta_far = after(across(tokens), across(meta))
    x_picked, own = after(pick([meta_far], [x_far], (False,)), own)
    d_late, own = after(d_mixed, own)
    d_far = across(d_late)
    x_far_rows = exchange(x_picked)
    d_picked, x_far_rows = after(pick([meta_far], [d_far], (True,)), x_far_rows)
    d_far_rows = exchange(d_picked)

    gate_matrix, up_matrix, down_matrix = w_gate[0].T, w_up[0].T, w_down[0]
    units, n_rows = gate_matrix.shape[0], 2 * half
    weight = pltpu.VMEM((units, feature), BF16)
    inner, wide = (n_rows, units), pltpu.VMEM((n_rows, feature), BF16)
    gate_pre, up_pre, hidden, y = streamed_call(
        functools.partial(forward_kernel, side),
        [shape(inner, F32), shape(inner, F32), shape(inner, BF16), shape((n_rows, feature), BF16)],
        [gate_matrix, own, x_far_rows, up_matrix, down_matrix],
        [
            *[weight] * 3,
            wide,
            pltpu.VMEM(inner, F32),
            pltpu.VMEM(inner, F32),
            pltpu.VMEM(inner, BF16),
            wide,
            pltpu.SemaphoreType.DMA((side + 4,)),
            pltpu.SemaphoreType.DMA((4,)),
        ],
    )
    y, d_far_rows = after(y, d_far_rows)
    y_back = exchange(y)

    dx_own, dx_far, terms = streamed_call(
        backward_kernel,
        [shape((half, feature), BF16)] * 2 + [shape((3 * units, feature), BF16)],
        [
            down_matrix,
            own,
            d_far_rows,
            gate_pre,
            up_pre,
            gate_matrix,
            up_matrix,
            x_far_rows,
            hidden,
        ],
        [
            weight,
            pltpu.VMEM(inner, F32),
            pltpu.VMEM(inner, F32),
            weight,
            weight,
            pltpu.VMEM(inner, BF16),
            wide,
            wide,
            pltpu.VMEM(inner, BF16),
            pltpu.VMEM(inner, BF16),
            wide,
            pltpu.VMEM((2, 256, feature), BF16),
            pltpu.SemaphoreType.DMA((2 * side + 8,)),
            pltpu.SemaphoreType.DMA((4,)),
        ],
    )
    dx_own, dx_far, terms, y_back = after(dx_own, dx_far, terms, y_back)
    summed = lax.psum_scatter(terms, "dp", scatter_dimension=1, tiled=True)

    token_rows, grad_rows = ((tok, feature), BF16), ((8, tok), F32)
    work = 2 * half * tok * feature
    mixed_far, grads_far = call(
        mix_kernel, [token_rows, grad_rows], [meta, meta_far, d_far, y_back], 2 * top * work
    )
    dx_far, mixed_far, grads_far = after(dx_far, mixed_far, grads_far)
    dx_far_back = exchange(dx_far)
    mixed_far = across(mixed_far)

    def table(meta, came):
        return pl.pallas_call(
            functools.partial(table_kernel, top, side, capacity),
            out_shape=shape((half, tok), BF16),
            in_specs=[SMEM, VMEM, anywhere],
            out_specs=VMEM,
            compiler_params=pltpu.CompilerParams(vmem_limit_bytes=60 * 1024 * 1024),
            cost_estimate=pl.CostEstimate(flops=LONG, bytes_accessed=1, transcendentals=0),
        )(me_arr, meta, came)

    def total(table, back, *far):
        return local_call_plain(
            lambda table, *refs: sum_kernel(table[...], *refs),
            [shape((tok, feature), BF16)],
            [table, back, *far],
            work,
        )[0]

    far_table, mixed_far, dx_far_back = after(
        table(meta_far, mixed_far), mixed_far, dx_far_back
    )
    tokens_far, dx_own, grads_far = after(
        total(far_table, dx_far_back), dx_own, across(grads_far)
    )
    dx_own_back = exchange(dx_own)
    mixed, grads = call(
        mix_last_kernel,
        [token_rows, grad_rows],
        [meta, meta_far, d_mixed, y_back, mixed_far],
        2 * top * work,
    )
    tokens_far = across(tokens_far)
    weight_grads = (
        summed[:units].astype(F32).T[None],
        summed[units : 2 * units].astype(F32).T[None],
        summed[2 * units :].astype(F32)[None],
    )
    grads = grads + grads_far
    tokens_far, mixed, grads, *weight_grads = after(tokens_far, mixed, grads, *weight_grads)
    own_table, tokens_far, dx_own_back = after(table(meta, tokens_far), tokens_far, dx_own_back)
    d_tokens = total(own_table, dx_own_back, tokens_far)
    return (mixed, d_tokens, grads[:top].T, *weight_grads)


def solution(mesh):
    in_specs = (
        P(("dp", "expert"), None),
        P(("dp", "expert"), None),
        P(("dp", "expert"), None),
        P("expert", None, None),
        P("expert", None, None),
        P("expert", None, None),
        P(("dp", "expert"), None),
    )
    out_specs = (
        P(("dp", "expert"), None),
        P(("dp", "expert"), None),
        P(("dp", "expert"), None),
        P("expert", "dp", None),
        P("expert", "dp", None),
        P("expert", None, "dp"),
    )
    return jax.shard_map(
        on_device, mesh=mesh, in_specs=in_specs, out_specs=out_specs, check_vma=False
    )
```

```python
import functools

import jax
import jax.numpy as jnp
from jax import lax
from jax.experimental import pallas as pl
from jax.experimental.pallas import tpu as pltpu
from jax.sharding import PartitionSpec as P

BF16 = jnp.bfloat16
F32 = jnp.float32
LANES = 128
STRIP = 512
LONG = 10**11
VMEM = pl.BlockSpec(memory_space=pltpu.VMEM)
SMEM = pl.BlockSpec(memory_space=pltpu.SMEM)


def local_call(kernel, outs, me, args, flops):
    size = sum(x.size * x.dtype.itemsize for x in (*outs, *args))
    return pl.pallas_call(
        kernel,
        out_shape=outs,
        in_specs=[SMEM] + [VMEM] * len(args),
        out_specs=[VMEM] * len(outs),
        compiler_params=pltpu.CompilerParams(vmem_limit_bytes=60 * 1024 * 1024),
        cost_estimate=pl.CostEstimate(flops=flops, bytes_accessed=size, transcendentals=0),
    )(me, *args)


def local_call_plain(kernel, outs, args, flops):
    return local_call(lambda me_ref, *refs: kernel(*refs), outs, jnp.zeros((1,), jnp.int32), args, flops)


def strips(width, step=STRIP):
    return [(c, min(c + step, width)) for c in range(0, width, step)]


def slot_tables(me, metas, top, side, capacity, wanted=None):
    count = len(metas)
    span = count * capacity
    tok = metas[0].shape[1]
    slot = lax.broadcasted_iota(jnp.int32, (side * span, tok), 0)
    expert = ((me - lax.rem(me, side)) + slot // span).astype(F32)
    block_of = lax.rem(slot, span) // capacity
    place = lax.rem(slot, capacity).astype(F32)
    row = lax.broadcasted_iota(jnp.int32, (tok, tok), 0)
    column = lax.broadcasted_iota(jnp.int32, (tok, tok), 1)
    earlier = jnp.where(row < column, 1.0, 0.0).astype(BF16)
    tables = []
    for b in range(count) if wanted is None else (wanted,):
        named = [jnp.where(metas[b][k : k + 1, :] == expert, 1.0, 0.0) for k in range(top)]
        member = functools.reduce(lambda p, q: p + q, named)
        rank = jnp.dot(member.astype(BF16), earlier, preferred_element_type=F32)
        here = rank == place
        if count > 1:
            here = here & (block_of == b)
        tables.append([jnp.where(here, part, 0.0) for part in named])
    return tables


def pick_kernel(top, side, capacity, scaled, me_ref, *refs, loads=()):
    count = len(scaled)
    metas, blocks, out = refs[:count], refs[count:-1], refs[-1]
    tables = slot_tables(me_ref[0], metas, top, side, capacity)
    held = jnp.concatenate([functools.reduce(lambda p, q: p + q, ks) for ks in tables], 1)
    held = held.astype(BF16)
    gate = 0.0
    for meta, ks, has in zip(metas, tables, scaled):
        for k, part in enumerate(ks):
            if has:
                part = part * meta[top + k : top + k + 1, :]
            gate += jnp.sum(part, 1, keepdims=True)
    for load in loads:
        load.wait()
    for c, e in strips(out.shape[1]):
        block = jnp.concatenate([ref[:, c:e] for ref in blocks], 0)
        got = jnp.dot(held, block, preferred_element_type=F32)
        out[:, c:e] = ((gate * got) if any(scaled) else got).astype(BF16)


def own_pick_kernel(top, side, capacity, me_ref, meta, x_hbm, d_hbm, out, x, d, sems):
    loads = fetch((x_hbm, d_hbm), (x, d), sems)
    pick_kernel(
        top, side, capacity, (False, True), me_ref, meta, meta, x, d, out, loads=loads
    )


TRANSPOSED = (((0,), (0,)), ((), ()))


def picked_sum(table, back, c, e):
    return lax.dot_general(
        table.astype(BF16), back[:, c:e], TRANSPOSED, preferred_element_type=F32
    )


def table_kernel(top, side, capacity, me_ref, meta, came, out):
    (table,) = slot_tables(me_ref[0], [meta], top, side, capacity)
    out[...] = functools.reduce(lambda p, q: p + q, table).astype(BF16)


def sum_kernel(table, back, *refs):
    out = refs[-1]
    for c, e in strips(out.shape[1]):
        got = picked_sum(table, back, c, e)
        for far in refs[:-1]:
            got += far[:, c:e].astype(F32)
        out[:, c:e] = got.astype(BF16)


def mix(top, table, meta, blocks, back, outs, grads, fars=()):
    tok = meta.shape[1]
    gates = [meta[top + k : top + k + 1, :] for k in range(top)]
    gates = [jnp.transpose(jnp.broadcast_to(g, (8, tok)))[:, :1] for g in gates]
    sums = [jnp.zeros((tok, 1), F32) for _ in range(top)]
    for c, e in strips(back.shape[1]):
        cotangent = jnp.concatenate([ref[:, c:e] for ref in blocks], 0).astype(F32)
        mixed = 0.0
        if fars:
            mixed = jnp.concatenate([ref[:, c:e] for ref in fars], 0).astype(F32)
        for k in range(top):
            got = picked_sum(table[k], back, c, e)
            mixed += gates[k] * got
            sums[k] += jnp.sum(cotangent * got, 1, keepdims=True)
        for n, out in enumerate(outs):
            rows = out.shape[0]
            out[:, c:e] = mixed[n * rows : (n + 1) * rows].astype(BF16)
    lane = lax.broadcasted_iota(jnp.int32, (tok, LANES), 1)
    grad = jnp.zeros((tok, LANES), F32)
    for k in range(top):
        grad += jnp.where(lane == k, sums[k], 0.0)
    grads[...] = jnp.transpose(grad)[: grads.shape[0]]


def mix_kernel(
    top, side, capacity, me_ref, meta, meta_far, block, back, out, grads
):
    (table,) = slot_tables(me_ref[0], [meta, meta_far], top, side, capacity, 1)
    mix(top, table, meta_far, (block,), back, (out,), grads)


def mix_last_kernel(top, side, capacity, me_ref, meta, meta_far, block, back, far, out, grads):
    (table,) = slot_tables(me_ref[0], [meta, meta_far], top, side, capacity, 0)
    mix(top, table, meta, (block,), back, (out,), grads, (far,))


def fetch(sources, targets, sems):
    copies = []
    for n, (source, target) in enumerate(zip(sources, targets)):
        copies.append(pltpu.make_async_copy(source, target, sems.at[n]))
        copies[n].start()
    return copies


ACROSS_LAST = (((1,), (1,)), ((), ()))


def own_rows(own, stream, target):
    side, _, capacity, _ = own.shape
    return (
        [own.at[q, stream] for q in range(side)],
        [target.at[pl.ds(q * capacity, capacity)] for q in range(side)],
    )


def forward_kernel(side, *refs):
    (wg_in, own, far, wu_in, wd_in), outs = refs[:5], refs[5:9]
    wg, wu, wd, x, gate, up, hidden, y, sems, out_sems = refs[9:]
    rows, feature = x.shape
    units, half = gate.shape[1], rows // 2
    x_from, x_to = own_rows(own, 0, x)
    loads = fetch(
        [wg_in, far, *x_from, wu_in, wd_in], [wg, x.at[pl.ds(half, half)], *x_to, wu, wd], sems
    )
    for load in loads[:-2]:
        load.wait()
    for c, e in strips(units, 256):
        gate[:, c:e] = lax.dot_general(
            x[...], wg[c:e, :], ACROSS_LAST, preferred_element_type=F32
        )
    loads[-2].wait()
    for c, e in strips(units, 256):
        got = lax.dot_general(x[...], wu[c:e, :], ACROSS_LAST, preferred_element_type=F32)
        up[:, c:e] = got
        pre = gate[:, c:e]
        hidden[:, c:e] = (pre * (1.0 / (1.0 + jnp.exp(-pre))) * got).astype(BF16)
    copies = [
        pltpu.make_async_copy(source, out, out_sems.at[n])
        for n, (source, out) in enumerate(zip((gate, up, hidden, y), outs))
    ]
    for copy in copies[:3]:
        copy.start()
    loads[-1].wait()
    for c, e in strips(feature):
        got = jnp.dot(hidden[...], wd[:, c:e], preferred_element_type=F32)
        pair = [
            part.reshape(side, 1, half // side, e - c) for part in (got[:half], got[half:])
        ]
        y[:, c:e] = jnp.concatenate(pair, 1).reshape(rows, e - c).astype(BF16)
    copies[3].start()
    for copy in copies:
        copy.wait()


def backward_kernel(*refs):
    (wd_in, own, d_far, gate_in, up_in, wg_in, wu_in, x_far, hidden_in) = refs[:9]
    own_out, far_out, terms_out = refs[9:12]
    wd, gate, up, wg, wu, hidden, d, x, gg, gu, dx, tiles, sems, out_sems = refs[12:]
    rows, feature = d.shape
    units, half = gate.shape[1], rows // 2
    first, second = pl.ds(0, half), pl.ds(half, half)
    d_from, d_to = own_rows(own, 1, d)
    x_from, x_to = own_rows(own, 0, x)
    loads = fetch(
        [wd_in, *d_from, d_far, gate_in, up_in, wg_in, wu_in, *x_from, x_far, hidden_in],
        [wd, *d_to, d.at[second], gate, up, wg, wu, *x_to, x.at[second], hidden],
        sems,
    )
    side = len(d_to)
    for load in loads[: side + 4]:
        load.wait()
    for c, e in strips(units, 256):
        back = lax.dot_general(d[...], wd[c:e, :], ACROSS_LAST, preferred_element_type=F32)
        pre = gate[:, c:e]
        sig = 1.0 / (1.0 + jnp.exp(-pre))
        gg[:, c:e] = (back * up[:, c:e] * (sig * (1.0 + pre * (1.0 - sig)))).astype(BF16)
        gu[:, c:e] = (back * (pre * sig)).astype(BF16)
    for load in loads[side + 4 : side + 6]:
        load.wait()
    for c, e in strips(feature):
        got = jnp.dot(gg[...], wg[:, c:e], preferred_element_type=F32)
        got += jnp.dot(gu[...], wu[:, c:e], preferred_element_type=F32)
        dx[:, c:e] = got.astype(BF16)
    dx_copies = [
        pltpu.make_async_copy(dx.at[second], far_out, out_sems.at[2]),
        pltpu.make_async_copy(dx.at[first], own_out, out_sems.at[3]),
    ]
    for copy in dx_copies:
        copy.start()
    for load in loads[side + 6 :]:
        load.wait()
    copies = []
    for n, (left, right) in enumerate(((gg, x), (gu, x), (hidden, d))):
        for r, t in strips(units, tiles.shape[1]):
            slot = len(copies) % 2
            if len(copies) > 1:
                copies[-2].wait()
            for c, e in strips(feature, 1024):
                tiles[slot, : t - r, c:e] = lax.dot_general(
                    left[:, r:t], right[:, c:e], TRANSPOSED, preferred_element_type=F32
                ).astype(BF16)
            copy = pltpu.make_async_copy(
                tiles.at[slot, pl.ds(0, t - r)],
                terms_out.at[pl.ds(n * units + r, t - r)],
                out_sems.at[slot],
            )
            copy.start()
            copies.append(copy)
    for copy in (*copies[-2:], *dx_copies):
        copy.wait()


def streamed_call(kernel, outs, args, scratch):
    anywhere = pl.BlockSpec(memory_space=pltpu.HBM)
    return pl.pallas_call(
        kernel,
        out_shape=outs,
        in_specs=[pl.BlockSpec(memory_space=pl.ANY)] * len(args),
        out_specs=[anywhere] * len(outs),
        scratch_shapes=scratch,
        compiler_params=pltpu.CompilerParams(vmem_limit_bytes=60 * 1024 * 1024),
        cost_estimate=pl.CostEstimate(flops=1, bytes_accessed=1, transcendentals=0),
    )(*args)


def on_device(tokens, expert_ids, gate_prob, w_gate, w_up, w_down, d_mixed):
    tok, feature = tokens.shape
    top = expert_ids.shape[1]
    experts = lax.axis_size("expert")
    capacity = max(2, 2 * tok * top // experts)
    side = experts // 2
    half = side * capacity
    me = lax.axis_index("expert")
    me_arr = me[None]
    sets = [[h * side + p for p in range(side)] for h in range(2)]
    shape = jax.ShapeDtypeStruct

    def across(value):
        return lax.ppermute(value, "expert", [(e, (e + side) % experts) for e in range(experts)])

    def exchange(value):
        shaped = value.reshape(side, value.shape[0] // side, value.shape[1])
        got = lax.all_to_all(shaped, "expert", 0, 0, axis_index_groups=sets, tiled=True)
        return got.reshape(value.shape)

    def after(value, *earlier):
        return lax.optimization_barrier((value, *earlier))

    def call(kernel, outs, args, flops):
        return local_call(
            functools.partial(kernel, top, side, capacity),
            [shape(*out) for out in outs],
            me_arr,
            args,
            flops,
        )

    def pick(metas, blocks, scaled):
        count = len(metas)
        return local_call(
            functools.partial(pick_kernel, top, side, capacity, scaled),
            [shape((count * half, feature), BF16)],
            me_arr,
            [*metas, *blocks],
            LONG,
        )[0]

    meta = jnp.concatenate([expert_ids.T.astype(F32), gate_prob.T], 0)
    anywhere = pl.BlockSpec(memory_space=pltpu.HBM)
    picked = pl.pallas_call(
        functools.partial(own_pick_kernel, top, side, capacity),
        out_shape=shape((2 * half, feature), BF16),
        in_specs=[SMEM, VMEM, anywhere, anywhere],
        out_specs=VMEM,
        scratch_shapes=[
            pltpu.VMEM((tok, feature), BF16),
            pltpu.VMEM((tok, feature), BF16),
            pltpu.SemaphoreType.DMA((2,)),
        ],
        compiler_params=pltpu.CompilerParams(vmem_limit_bytes=60 * 1024 * 1024),
        cost_estimate=pl.CostEstimate(
            flops=8 * half * tok * feature, bytes_accessed=1, transcendentals=0
        ),
    )(me_arr, meta, tokens, d_mixed)
    own = exchange(picked)
    own = own.reshape(side, 2, capacity, feature)
    x_far, meta_far = after(across(tokens), across(meta))
    x_picked, own = after(pick([meta_far], [x_far], (False,)), own)
    d_late, own = after(d_mixed, own)
    d_far = across(d_late)
    x_far_rows = exchange(x_picked)
    d_picked, x_far_rows = after(pick([meta_far], [d_far], (True,)), x_far_rows)
    d_far_rows = exchange(d_picked)

    gate_matrix, up_matrix, down_matrix = w_gate[0].T, w_up[0].T, w_down[0]
    units, n_rows = gate_matrix.shape[0], 2 * half
    weight = pltpu.VMEM((units, feature), BF16)
    inner, wide = (n_rows, units), pltpu.VMEM((n_rows, feature), BF16)
    gate_pre, up_pre, hidden, y = streamed_call(
        functools.partial(forward_kernel, side),
        [shape(inner, F32), shape(inner, F32), shape(inner, BF16), shape((n_rows, feature), BF16)],
        [gate_matrix, own, x_far_rows, up_matrix, down_matrix],
        [
            *[weight] * 3,
            wide,
            pltpu.VMEM(inner, F32),
            pltpu.VMEM(inner, F32),
            pltpu.VMEM(inner, BF16),
            wide,
            pltpu.SemaphoreType.DMA((side + 4,)),
            pltpu.SemaphoreType.DMA((4,)),
        ],
    )
    y, d_far_rows = after(y, d_far_rows)
    y_back = exchange(y)

    dx_own, dx_far, terms = streamed_call(
        backward_kernel,
        [shape((half, feature), BF16)] * 2 + [shape((3 * units, feature), BF16)],
        [
            down_matrix,
            own,
            d_far_rows,
            gate_pre,
            up_pre,
            gate_matrix,
            up_matrix,
            x_far_rows,
            hidden,
        ],
        [
            weight,
            pltpu.VMEM(inner, F32),
            pltpu.VMEM(inner, F32),
            weight,
            weight,
            pltpu.VMEM(inner, BF16),
            wide,
            wide,
            pltpu.VMEM(inner, BF16),
            pltpu.VMEM(inner, BF16),
            wide,
            pltpu.VMEM((2, 256, feature), BF16),
            pltpu.SemaphoreType.DMA((2 * side + 8,)),
            pltpu.SemaphoreType.DMA((4,)),
        ],
    )
    dx_own, dx_far, terms, y_back = after(dx_own, dx_far, terms, y_back)
    summed = lax.psum_scatter(terms, "dp", scatter_dimension=1, tiled=True)

    token_rows, grad_rows = ((tok, feature), BF16), ((8, tok), F32)
    work = 2 * half * tok * feature
    mixed_far, grads_far = call(
        mix_kernel, [token_rows, grad_rows], [meta, meta_far, d_far, y_back], 2 * top * work
    )
    dx_far, mixed_far, grads_far = after(dx_far, mixed_far, grads_far)
    dx_far_back = exchange(dx_far)
    mixed_far = across(mixed_far)

    def table(meta, came):
        return pl.pallas_call(
            functools.partial(table_kernel, top, side, capacity),
            out_shape=shape((half, tok), BF16),
            in_specs=[SMEM, VMEM, anywhere],
            out_specs=VMEM,
            compiler_params=pltpu.CompilerParams(vmem_limit_bytes=60 * 1024 * 1024),
            cost_estimate=pl.CostEstimate(flops=LONG, bytes_accessed=1, transcendentals=0),
        )(me_arr, meta, came)

    def total(table, back, *far):
        return local_call_plain(
            lambda table, *refs: sum_kernel(table[...], *refs),
            [shape((tok, feature), BF16)],
            [table, back, *far],
            work,
        )[0]

    far_table, mixed_far, dx_far_back = after(
        table(meta_far, mixed_far), mixed_far, dx_far_back
    )
    tokens_far, dx_own, grads_far = after(
        total(far_table, dx_far_back), dx_own, across(grads_far)
    )
    dx_own_back = exchange(dx_own)
    mixed, grads = call(
        mix_last_kernel,
        [token_rows, grad_rows],
        [meta, meta_far, d_mixed, y_back, mixed_far],
        2 * top * work,
    )
    tokens_far = across(tokens_far)
    weight_grads = (
        summed[:units].astype(F32).T[None],
        summed[units : 2 * units].astype(F32).T[None],
        summed[2 * units :].astype(F32)[None],
    )
    grads = grads + grads_far
    tokens_far, mixed, grads, *weight_grads = after(tokens_far, mixed, grads, *weight_grads)
    own_table, tokens_far, dx_own_back = after(table(meta, tokens_far), tokens_far, dx_own_back)
    d_tokens = total(own_table, dx_own_back, tokens_far)
    return (mixed, d_tokens, grads[:top].T, *weight_grads)


def solution(mesh):
    in_specs = (
        P(("dp", "expert"), None),
        P(("dp", "expert"), None),
        P(("dp", "expert"), None),
        P("expert", None, None),
        P("expert", None, None),
        P("expert", None, None),
        P(("dp", "expert"), None),
    )
    out_specs = (
        P(("dp", "expert"), None),
        P(("dp", "expert"), None),
        P(("dp", "expert"), None),
        P("expert", "dp", None),
        P("expert", "dp", None),
        P("expert", None, "dp"),
    )
    return jax.shard_map(
        on_device, mesh=mesh, in_specs=in_specs, out_specs=out_specs, check_vma=False
    )
```
